128 devices in a mesh: dp: 32 (over x, z, core), row: 2 (over y_lo), col: 2 (over y_hi).
Axes of the slice: x: 4, y: 4 (y_hi: 2, y_lo: 2; y = y_hi * 2 + y_lo), z: 4, core: 2. Of those that a mesh axis runs over, the one named last changes fastest.
Arguments:
- tokens: bfloat16 [16384, 1536], P(('dp', 'row'), 'col'), may hold values from -6 to 6
- cotangent: bfloat16 [16384, 1536], P(('dp', 'row'), 'col'), may hold values from -6 to 6
- norm_gains: bfloat16 [2, 2, 1536], P(None, None, 'col'), may hold values from 0.5 to 1.5
- query_weight: bfloat16 [2, 1536, 1536], P(None, 'col', 'row'), may hold values from -0.15625 to 0.15625
- key_weight: bfloat16 [2, 1536, 256], P(None, 'col', 'row'), may hold values from -0.15625 to 0.15625
- value_weight: bfloat16 [2, 1536, 256], P(None, 'col', 'row'), may hold values from -0.15625 to 0.15625
- output_weight: bfloat16 [2, 1536, 1536], P(None, 'row', 'col'), may hold values from -1.75 to 1.75
- router_weight: bfloat16 [2, 1536, 8], P(None, 'col'), may hold values from -0.078125 to 0.078125
- gate_weight: bfloat16 [2, 8, 1536, 768], P(None, None, 'col', 'row'), may hold values from -0.15625 to 0.15625
- up_weight: bfloat16 [2, 8, 1536, 768], P(None, None, 'col', 'row'), may hold values from -0.15625 to 0.15625
- down_weight: bfloat16 [2, 8, 768, 1536], P(None, None, 'row', 'col'), may hold values from -0.875 to 0.875
- expert_ids: int32 [2, 16384, 4], P(None, 'dp'), may hold values from 0 to 7, all different within a row; in each aligned block of 512 rows (0 to 511, 512 to 1023, ..., all dimensions but the last counted through in order) at most 288 rows name the same one
- seq_lengths: int32 [128], replicated, may hold values from 1 to 509, as said below
- seq_owner: int32 [128], replicated, may hold values from 0 to 31, as said below
Outputs:
- block_output: bfloat16 [16384, 1536], P(('dp', 'row'), 'col')
- grad_tokens: bfloat16 [16384, 1536], P(('dp', 'row'), 'col')
- grad_gains: float32 [2, 2, 1536], P(None, None, 'col')
- grad_query: float32 [2, 1536, 1536], P(None, ('col', 'dp'), 'row')
- grad_key: float32 [2, 1536, 256], P(None, ('col', 'dp'), 'row')
- grad_value: float32 [2, 1536, 256], P(None, ('col', 'dp'), 'row')
- grad_output: float32 [2, 1536, 1536], P(None, ('row', 'dp'), 'col')
- grad_router: float32 [2, 1536, 8], P(None, 'col')
- grad_gate: float32 [2, 8, 1536, 768], P(None, None, ('col', 'dp'), 'row')
- grad_up: float32 [2, 8, 1536, 768], P(None, None, ('col', 'dp'), 'row')
- grad_down: float32 [2, 8, 768, 1536], P(None, None, ('row', 'dp'), 'col')
The draws below stay inside these ranges and needn't reach their ends.
Inputs may be any that keep to these rules, and one draw needn't show every extreme that they name: `seq_owner`: each data index holds exactly 4 sequences. `seq_lengths`: the sequences of one data index take at most 512 rows together, and one of them is longer than 256. `expert_ids`: the 4 experts of a token differ; within one layer and the 512 rows of one data index no expert is named more than 288 times.
All inputs are finite; a program needn't handle non-finite values.
Results may differ from the reference program's by a relative error of at most 0.022.
Values may be sent and summed in bfloat16 or wider, within the bound.
No kernel may reach another device: no remote copies, remote signals or barrier semaphores. Data moves between devices by JAX's collectives and lax.ppermute only.
A program may use at most 256 MiB of HBM per device.

```python
import math
import jax
import jax.numpy as jnp
import numpy as np
from jax import lax

D = 1536
HEADS = 12
KV_HEADS = 2
HEAD = 128
FF = 768
TOP = 4
EXPERTS = 8
LAYERS = 2
SEQ_DEV = 4
TOK_DP = 512
CAP = 288
TOKENS = 16384
N_DP = 32


def deal_sequences(key):
    seq_total = N_DP * SEQ_DEV
    shuffled = jax.random.permutation(jax.random.fold_in(key, 21), seq_total).astype(jnp.int32)
    owner_index = (shuffled // SEQ_DEV).astype(jnp.int32)
    slot_in_group = (shuffled % SEQ_DEV).astype(jnp.int32)
    longest = jax.random.randint(jax.random.fold_in(key, 22), (N_DP,), TOK_DP // 2 + 1, TOK_DP - SEQ_DEV + 2)
    forced = jax.random.randint(jax.random.fold_in(key, 23), (), 0, N_DP)
    longest = jnp.where(jnp.arange(N_DP, dtype=jnp.int32) == forced, TOK_DP - SEQ_DEV + 1, longest).astype(jnp.int32)
    headroom = (TOK_DP - longest) // (SEQ_DEV - 1)
    spread = jax.random.randint(jax.random.fold_in(key, 24), (N_DP, SEQ_DEV), 0, 1048576)
    shorter = 1 + spread % headroom[:, None]
    long_slot = jax.random.randint(jax.random.fold_in(key, 25), (N_DP,), 0, SEQ_DEV)
    length_table = jnp.where(jnp.arange(SEQ_DEV, dtype=jnp.int32)[None, :] == long_slot[:, None], longest[:, None], shorter).astype(jnp.int32)
    return (length_table[owner_index, slot_in_group].astype(jnp.int32), owner_index)


def draw_seq_lengths(key, part):
    lengths_drawn, owner_drawn = deal_sequences(key)
    return lengths_drawn


def draw_seq_owner(key, part):
    lengths_drawn, owner_drawn = deal_sequences(key)
    return owner_drawn


def shard_levels(stream_key, extent, split, smallest, top_value):
    level = 1.0
    for dim, blocks in split:
        heights = jax.random.uniform(jax.random.fold_in(jax.random.fold_in(stream_key, 6), dim), (blocks,), jnp.float32, smallest / len(split), top_value / len(split))
        level = level * jnp.repeat(jnp.exp(heights), extent[dim] // blocks).reshape((-1,) + (1,) * (len(extent) - 1 - dim))
    return level


def deal_out(key, own, number, rows, number_of, top, limit, skew):
    sequence = jax.random.permutation(key, number_of)
    heavy_load, common = load_shares(number_of, rows * top, limit, skew, True), load_shares(number_of, rows * top, limit, skew, False)
    places = jnp.arange(number_of)

    def named(sizes, offset_by):
        used = int((sizes > 0).sum())
        fixed = max(1, used // 4)
        passed = fixed + (places - fixed + offset_by * (used - fixed)) % max(1, number_of - fixed)
        return jnp.zeros((number_of,), jnp.int32).at[sequence[jnp.where(places < fixed, places, passed)]].set(jnp.asarray(sizes, jnp.int32))

    sizes = jnp.where(number % 4 == 0, named(heavy_load, number // 4), named(common, number - number // 4 - 1))
    mixed = jax.random.permutation(jax.random.fold_in(own, 3), number_of)
    donor, receiver = mixed[0:number_of // 2 * 2:2], mixed[1:number_of // 2 * 2:2]
    room = jnp.minimum(sizes[donor] - 1, limit - sizes[receiver]) // 2
    room = jnp.where((donor == sequence[0]) | (receiver == sequence[0]) | (sizes[receiver] == 0), 0, jnp.maximum(room, 0))
    passed = jax.random.randint(jax.random.fold_in(own, 4), (number_of // 2,), 0, 1 << 20) % (room + 1)
    sizes = sizes.at[donor].add(-passed).at[receiver].add(passed)
    items = jnp.searchsorted(jnp.cumsum(sizes), jnp.arange(rows * top), side="right").astype(jnp.int32)
    table = items.reshape(top, rows).T
    table = table[jax.random.permutation(jax.random.fold_in(own, 1), rows)]
    offset_by = jax.random.randint(jax.random.fold_in(own, 2), (rows, 1), 0, top)
    return jnp.take_along_axis(table, (jnp.arange(top)[None, :] + offset_by) % top, axis=1)


def load_shares(number_of, total, most, lean, full):
    weights = [(1 << 20) // math.isqrt(standing ** lean) + 1 for standing in range(1, number_of + 1)]
    largest = most if full else min(most, max(-(-total // number_of), total * weights[0] // sum(weights)))
    least = 1 if total - largest >= number_of - 1 else 0
    holding, spare = [largest] + [least] * (number_of - 1), total - largest - least * (number_of - 1)
    while spare > 0:
        free = [i for i in range(1, number_of) if holding[i] < largest] or [i for i in range(1, number_of) if holding[i] < most]
        mass, budget = sum([weights[i] for i in free]), spare
        for i in free:
            more = min(most - holding[i], max(1, budget * weights[i] // mass), spare)
            holding[i] = holding[i] + more
            spare = spare - more
    return np.array(holding)


def bell_draw(key, dims, scale, limit, split=(), kind=jnp.bfloat16):
    values = scale * jax.random.normal(key, dims, jnp.float32)
    if split:
        values = values * shard_levels(key, dims, split, -0.22, 0.18)
    return jnp.clip(values, -limit, limit).astype(kind)


def setup_inputs(seed: int = 0) -> dict:
    key_of = jax.random.split(jax.random.key(seed), 15)
    tokens = bell_draw(key_of[0], (TOKENS, D), 1.0, 6.0, ((0, 64), (1, 2)))
    cotangent = bell_draw(key_of[1], (TOKENS, D), 1.0, 6.0, ((0, 64), (1, 2)))
    norm_gains = jnp.clip(1.0 + 0.1 * jax.random.normal(key_of[2], (LAYERS, 2, D), jnp.float32), 0.5, 1.5).astype(jnp.bfloat16)
    query_weight = bell_draw(key_of[3], (LAYERS, D, HEADS * HEAD), D ** -0.5, 0.15625, ((1, 2), (2, 2)))
    key_weight = bell_draw(key_of[4], (LAYERS, D, KV_HEADS * HEAD), D ** -0.5, 0.15625, ((1, 2), (2, 2)))
    value_weight = bell_draw(key_of[5], (LAYERS, D, KV_HEADS * HEAD), D ** -0.5, 0.15625, ((1, 2), (2, 2)))
    output_weight = bell_draw(key_of[6], (LAYERS, HEADS * HEAD, D), (max(HEADS * HEAD // 128, 1)) ** -0.5, 1.75, ((1, 2), (2, 2)))
    router_weight = bell_draw(key_of[7], (LAYERS, D, EXPERTS), (4 * D) ** -0.5, 0.078125, ((1, 2),))
    gate_weight = bell_draw(key_of[8], (LAYERS, EXPERTS, D, FF), D ** -0.5, 0.15625, ((2, 2), (3, 2)))
    up_weight = bell_draw(key_of[9], (LAYERS, EXPERTS, D, FF), D ** -0.5, 0.15625, ((2, 2), (3, 2)))
    down_weight = bell_draw(key_of[10], (LAYERS, EXPERTS, FF, D), (FF // 16) ** -0.5, 0.875, ((2, 2), (3, 2)))
    expert_ids_keys = jax.random.split(jax.random.fold_in(key_of[11], 1), LAYERS * TOKENS // TOK_DP)
    expert_ids_turns = jax.random.permutation(jax.random.fold_in(key_of[11], 3), LAYERS * TOKENS // TOK_DP)
    expert_ids = jax.vmap(lambda own, number: deal_out(jax.random.fold_in(key_of[11], 2), own, number, TOK_DP, EXPERTS, TOP, CAP, 0))(expert_ids_keys, expert_ids_turns).reshape((LAYERS, TOKENS, TOP))
    seq_lengths = draw_seq_lengths(jax.random.fold_in(key_of[14], 71), 0)
    seq_owner = draw_seq_owner(jax.random.fold_in(key_of[14], 71), 0)
    return {"tokens": tokens, "cotangent": cotangent, "norm_gains": norm_gains, "query_weight": query_weight, "key_weight": key_weight, "value_weight": value_weight, "output_weight": output_weight, "router_weight": router_weight, "gate_weight": gate_weight, "up_weight": up_weight, "down_weight": down_weight, "expert_ids": expert_ids, "seq_lengths": seq_lengths, "seq_owner": seq_owner}


@jax.custom_vjp
def low(v):
    return lax.optimization_barrier(v.astype(jnp.bfloat16)).astype(jnp.float32)

@jax.custom_vjp
def low_back(v):
    return v

def low_keep(v):
    return (low(v), None)

def low_pass(kept, grad):
    return (grad,)

def back_keep(v):
    return (v, None)

def back_low(kept, grad):
    return (low(grad),)
low.defvjp(low_keep, low_pass)
low_back.defvjp(back_keep, back_low)
EPSILON = 1e-06
ROPE_THETA = 1000000.0
MASKED_SCORE = -1e+30
HIGHEST_PRECISION = lax.Precision.HIGHEST

def segments(seq_lengths, seq_owner, data_index, places_count):
    owned_len = jnp.where(seq_owner == data_index, seq_lengths, 0).astype(jnp.int32)
    seq_ends = jnp.cumsum(owned_len).astype(jnp.int32)
    places = jnp.arange(places_count, dtype=jnp.int32)
    finished = (seq_ends[None, :] <= places[:, None]).astype(jnp.int32)
    segment = lax.optimization_barrier(jnp.sum(finished, axis=1)).astype(jnp.int32)
    starts = lax.optimization_barrier(jnp.sum(finished * owned_len[None, :], axis=1)).astype(jnp.int32)
    valid_row = places < jnp.sum(owned_len)
    position = jnp.where(valid_row, places - starts, 0).astype(jnp.int32)
    return (segment, position, valid_row)

def rotate(values, position, direction):
    half_dim = values.shape[-1] // 2
    exponent = jnp.arange(half_dim, dtype=jnp.float32) * (-2.0 / values.shape[-1])
    frequency = jnp.power(ROPE_THETA, exponent)
    angle_grid = position.astype(jnp.float32)[:, None] * frequency[None, :]
    cosine = jnp.cos(angle_grid)
    sine_part = jnp.sin(angle_grid) * direction
    former = values[..., :half_dim]
    latter = values[..., half_dim:]
    return jnp.concatenate([former * cosine - latter * sine_part, latter * cosine + former * sine_part], axis=-1)

def rms_norm(stream, gain):
    scale = lax.rsqrt(lax.optimization_barrier(jnp.mean(stream * stream, axis=-1, keepdims=True)) + EPSILON)
    return stream * scale * gain

def route_slots(expert_ids):
    flat_ids = expert_ids.reshape(-1).astype(jnp.int32)
    pair_count = flat_ids.shape[0]
    one_hot = (flat_ids[:, None] == jnp.arange(EXPERTS, dtype=jnp.int32)[None, :]).astype(jnp.int32)
    earlier = jnp.cumsum(one_hot, axis=0) - one_hot
    slot_index = lax.optimization_barrier(jnp.sum(earlier * one_hot, axis=1)).astype(jnp.int32)
    pair_slot = (flat_ids * CAP + slot_index).astype(jnp.int32)
    slot_pair = jnp.full((EXPERTS * CAP,), pair_count, jnp.int32).at[pair_slot].set(jnp.arange(pair_count, dtype=jnp.int32))
    return (pair_slot, slot_pair)

def attend(stream, gain, query_weight, key_weight, value_weight, output_weight, segment, position, valid_row):
    rows_all = stream.shape[0]
    normed = low(rms_norm(stream, gain))
    query_heads = jnp.dot(normed, query_weight, precision=HIGHEST_PRECISION).reshape(rows_all, HEADS, HEAD).transpose(1, 0, 2)
    key_heads = jnp.dot(normed, key_weight, precision=HIGHEST_PRECISION).reshape(rows_all, KV_HEADS, HEAD).transpose(1, 0, 2)
    value_heads = jnp.dot(normed, value_weight, precision=HIGHEST_PRECISION).reshape(rows_all, KV_HEADS, HEAD).transpose(1, 0, 2)
    query_heads = low(rotate(low_back(query_heads), position, 1.0))
    key_heads = low(rotate(low_back(key_heads), position, 1.0))
    value_heads = low(low_back(value_heads))
    key_heads = jnp.repeat(key_heads, HEADS // KV_HEADS, axis=0)
    value_heads = jnp.repeat(value_heads, HEADS // KV_HEADS, axis=0)
    scores = low_back(jnp.einsum('hqd,hkd->hqk', query_heads, key_heads, precision=HIGHEST_PRECISION) * HEAD ** (-0.5))
    places = jnp.arange(rows_all, dtype=jnp.int32)
    seen_mask = (segment[:, None] == segment[None, :]) & (places[None, :] <= places[:, None]) & valid_row[:, None]
    row_max = lax.optimization_barrier(jnp.max(jnp.where(seen_mask, scores, MASKED_SCORE), axis=-1, keepdims=True))
    row_max = jnp.where(valid_row[:, None], row_max, 0.0)
    exponent = jnp.where(seen_mask, jnp.exp(scores - row_max), 0.0)
    denominator = lax.optimization_barrier(jnp.sum(exponent, axis=-1, keepdims=True)) + jnp.where(valid_row, 0.0, 1.0)[:, None]
    probabilities = low(exponent / denominator)
    attended = jnp.einsum('hqk,hkd->hqd', probabilities, value_heads, precision=HIGHEST_PRECISION)
    attended = low(low_back(attended)).transpose(1, 0, 2).reshape(rows_all, HEADS * HEAD)
    return stream + low_back(jnp.dot(attended, output_weight, precision=HIGHEST_PRECISION))

def experts(stream, gain, router_weight, gate_weight, up_weight, down_weight, expert_ids):
    rows_all = stream.shape[0]
    normed = low(rms_norm(stream, gain))
    logits = jnp.dot(normed, router_weight, precision=HIGHEST_PRECISION)
    chosen = jnp.take_along_axis(logits, expert_ids, axis=1)
    gate_share = jax.nn.softmax(chosen, axis=-1)
    pair_slot, slot_pair = route_slots(expert_ids)
    slot_token = slot_pair // TOP
    expert_rows = jnp.take(normed, slot_token, axis=0, mode='fill', fill_value=0.0).reshape(EXPERTS, CAP, D)
    slot_weight = jnp.take(gate_share.reshape(-1), slot_pair, mode='fill', fill_value=0.0).reshape(EXPERTS, CAP, 1)
    gate_value = low_back(jnp.einsum('esd,edf->esf', expert_rows, gate_weight, precision=HIGHEST_PRECISION))
    up_value = low_back(jnp.einsum('esd,edf->esf', expert_rows, up_weight, precision=HIGHEST_PRECISION))
    hidden = low(slot_weight * jax.nn.silu(gate_value) * up_value)
    result = jnp.einsum('esf,efd->esd', hidden, down_weight, precision=HIGHEST_PRECISION).reshape(EXPERTS * CAP, D)
    combined = jnp.take(result, pair_slot, axis=0).reshape(rows_all, TOP, D).sum(axis=1)
    return stream + low_back(combined)

def reference(tokens, cotangent, norm_gains, query_weight, key_weight, value_weight, output_weight, router_weight, gate_weight, up_weight, down_weight, expert_ids, seq_lengths, seq_owner):
    params = tuple((weight.astype(jnp.float32) for weight in (norm_gains, query_weight, key_weight, value_weight, output_weight, router_weight, gate_weight, up_weight, down_weight)))
    blocks = tokens.astype(jnp.float32).reshape(N_DP, TOK_DP, D)
    group_ids = jnp.transpose(expert_ids.reshape(LAYERS, N_DP, TOK_DP, TOP), (1, 0, 2, 3))
    data_indices = jnp.arange(N_DP, dtype=jnp.int32)

    def one_group(weights, stream, layer_ids, data_index):
        gains_all, query_all, key_all, value_all, output_all, router_all, gate_all, up_all, down_all = weights
        segment, position, valid_row = segments(seq_lengths, seq_owner, data_index, TOK_DP)
        for layer_index in range(LAYERS):
            stream = attend(stream, gains_all[layer_index, 0], query_all[layer_index], key_all[layer_index], value_all[layer_index], output_all[layer_index], segment, position, valid_row)
            stream = experts(stream, gains_all[layer_index, 1], router_all[layer_index], gate_all[layer_index], up_all[layer_index], down_all[layer_index], layer_ids[layer_index])
        return stream
    checkpointed = jax.checkpoint(one_group)

    def run_all(weights, streams):
        return lax.map(lambda group_item: checkpointed(weights, group_item[0], group_item[1], group_item[2]), (streams, group_ids, data_indices))
    outputs, pull = jax.vjp(run_all, params, blocks)
    grad_params, grad_blocks = pull(cotangent.astype(jnp.float32).reshape(N_DP, TOK_DP, D))
    grad_gains, grad_query, grad_key, grad_value, grad_output, grad_router, grad_gate, grad_up, grad_down = grad_params
    return (outputs.reshape(TOKENS, D).astype(jnp.bfloat16), grad_blocks.reshape(TOKENS, D).astype(jnp.bfloat16), grad_gains, grad_query, grad_key, grad_value, grad_output, grad_router, grad_gate, grad_up, grad_down)
```

```python
import jax
import jax.numpy as jnp
from jax import lax
from jax.sharding import PartitionSpec as P

D = 1536
HALF = D // 2
HEAD = 128
Q_HEADS = 6
EXPERTS = 8
MINE = 4
FF = 384
LAYERS = 2
TOK_DP = 512
QUARTER = 128
EPSILON = 1e-06
ROPE_THETA = 1000000.0
MASKED_SCORE = -1e30
ACROSS = (((1,), (1,)), ((), ()))
DOWNWARD = (((0,), (0,)), ((), ()))
SWAP = [(0, 1), (1, 0)]
DIAGONAL = [(0, 3), (1, 2), (2, 1), (3, 0)]
N_DP = 32
BF16 = jnp.bfloat16
F32 = jnp.float32


def dot(a, b):
    return jnp.dot(a, b, preferred_element_type=F32)


def dot_across(a, b):
    return lax.dot_general(a, b, ACROSS, preferred_element_type=F32)


def dot_down(a, b):
    return lax.dot_general(a, b, DOWNWARD, preferred_element_type=F32)


def over_row(x):
    return lax.ppermute(x, "row", SWAP)


def over_col(x):
    return lax.ppermute(x, "col", SWAP)


def over_both(x):
    return lax.ppermute(x, ("row", "col"), DIAGONAL)


def over_dp(x, target):
    return lax.ppermute(x, "dp", [(i, target(i)) for i in range(N_DP)])


def by_col(column, own, other, axis):
    return jnp.where(
        column == 0,
        jnp.concatenate([own, other], axis=axis),
        jnp.concatenate([other, own], axis=axis),
    )


def half_of(x, index, axis):
    size = x.shape[axis] // 2
    return lax.dynamic_slice_in_dim(x, index * size, size, axis=axis)


def halves(x):
    return [x[:, :HALF], x[:, HALF:]]


def pack(parts):
    return jnp.concatenate([x.astype(BF16) for x in parts], axis=1)


def to_quarter(block, column):
    own = half_of(block, column, 0)
    other = over_col(half_of(block, 1 - column, 0))
    return by_col(column, own, other, 1)


def from_quarter(block, column):
    own = half_of(block, column, 1)
    other = over_col(half_of(block, 1 - column, 1))
    return by_col(column, own, other, 0)


def gather_four(x):
    return jnp.concatenate([x, over_row(x), over_col(x), over_both(x)], axis=0)


def scatter_four(x):
    own, row, col, both = [x[i * QUARTER : (i + 1) * QUARTER] for i in range(4)]
    return (
        own
        + over_row(row.astype(BF16)).astype(F32)
        + over_col(col.astype(BF16)).astype(F32)
        + over_both(both.astype(BF16)).astype(F32)
    )


def gather_two(x):
    return jnp.concatenate([x, over_row(x)], axis=0)


def scatter_two(x):
    return x[:QUARTER] + over_row(x[QUARTER:].astype(BF16)).astype(F32)


def segments(seq_lengths, seq_owner, data_index):
    owned_len = jnp.where(seq_owner == data_index, seq_lengths, 0)
    seq_ends = jnp.cumsum(owned_len)
    places = jnp.arange(TOK_DP, dtype=jnp.int32)
    finished = (seq_ends[None, :] <= places[:, None]).astype(jnp.int32)
    segment = jnp.sum(finished, axis=1)
    starts = jnp.sum(finished * owned_len[None, :], axis=1)
    valid_row = places < jnp.sum(owned_len)
    position = jnp.where(valid_row, places - starts, 0)
    return (segment, position, valid_row, places)


def rotate(values, cosine, sine):
    half_dim = values.shape[-1] // 2
    former = values[..., :half_dim]
    latter = values[..., half_dim:]
    return jnp.concatenate(
        [former * cosine - latter * sine, latter * cosine + former * sine], axis=-1
    )


def normalize(stream, gain):
    inv_rms = lax.rsqrt(jnp.mean(stream * stream, axis=1, keepdims=True) + EPSILON)
    return (inv_rms, (stream * inv_rms * gain).astype(BF16))


def norm_back(upstream, grad_normed, stream, inv_rms, gain):
    scaled = gain * grad_normed
    dots = jnp.sum(scaled * stream, axis=1, keepdims=True)
    grad_stream = upstream + inv_rms * scaled - stream * (inv_rms * inv_rms * inv_rms * dots / D)
    grad_gain = jnp.sum(grad_normed * stream * inv_rms, axis=0)
    return (grad_stream, grad_gain)


def attention_weights(own, column, core):
    sent = over_col(half_of(own, core, 0))
    swapped = over_dp(sent, lambda i: i ^ 1)
    return jnp.where(
        core == 0,
        jnp.concatenate([sent, swapped], axis=0),
        jnp.concatenate([swapped, sent], axis=0),
    )


def expert_weights(gate, up, down, column, data_index):
    rows = 48
    start = (data_index % 16) * rows

    def piece(weight, side):
        cut = lax.dynamic_slice(weight, (MINE * side, start, 0), (MINE, rows, FF))
        return cut.transpose(1, 0, 2).reshape(rows, MINE * FF)

    def down_piece(side):
        place = (MINE * side + data_index // 8, (data_index % 8) * rows, 0)
        return lax.dynamic_slice(down, place, (1, rows, HALF))[0]

    def pack(side):
        return jnp.concatenate([piece(gate, side), piece(up, side), down_piece(side)], axis=1)

    other = over_col(pack(1 - column))
    own = pack(column)
    mine = data_index // 16 == column
    gate_up = jnp.where(mine, own[:, : 2 * D], other[:, : 2 * D])
    downs = by_col(column, own[:, 2 * D :], other[:, 2 * D :], 1)
    whole = lax.all_gather(jnp.concatenate([gate_up, downs], axis=1), "dp", axis=0, tiled=True)
    return (whole[:, : 2 * D], whole[:, 2 * D :])


def attention_forward(stream, gain, qkv_weight, out_weight, geometry):
    cosine, sine, seen_mask, row_valid = geometry
    inv_rms, normed = normalize(stream, gain)
    inputs = gather_two(normed)
    qkv = dot(inputs, qkv_weight)
    rows = inputs.shape[0]
    width = Q_HEADS * HEAD
    key_rot = rotate(qkv[:, width : width + HEAD], cosine, sine).astype(BF16)
    value_low = qkv[:, width + HEAD :].astype(BF16)
    pair = jnp.concatenate([key_rot, value_low], axis=1)
    pair = jnp.concatenate([pair, over_col(pair)], axis=0)
    keys, values = pair[:, :HEAD], pair[:, HEAD:]
    query = qkv[:, :width].reshape(rows, Q_HEADS, HEAD).transpose(1, 0, 2)
    query_rot = rotate(query, cosine, sine).astype(BF16).reshape(Q_HEADS * rows, HEAD)
    scores = dot_across(query_rot, keys).reshape(Q_HEADS, rows, TOK_DP) * HEAD ** (-0.5)
    row_max = jnp.max(jnp.where(seen_mask, scores, MASKED_SCORE), axis=-1, keepdims=True)
    row_max = jnp.where(row_valid, row_max, 0.0)
    exponent = jnp.where(seen_mask, jnp.exp(scores - row_max), 0.0)
    denominator = jnp.sum(exponent, axis=-1, keepdims=True) + jnp.where(row_valid, 0.0, 1.0)
    log_total = row_max + jnp.log(denominator)
    probabilities = (exponent / denominator).astype(BF16).reshape(Q_HEADS * rows, TOK_DP)
    attended = dot(probabilities, values).reshape(Q_HEADS, rows, HEAD)
    attended = attended.transpose(1, 0, 2).reshape(rows, width).astype(BF16)
    branch = scatter_two(dot(attended, out_weight))
    cache = (stream, inv_rms, inputs, query_rot, keys, values, log_total, attended)
    return (cache, stream + branch)


def attention_backward(upstream, cache, gain, qkv_weight, out_weight, geometry):
    cosine, sine, seen_mask, row_valid = geometry
    stream, inv_rms, inputs, query_rot, keys, values, log_total, attended = cache
    rows = inputs.shape[0]
    width = Q_HEADS * HEAD
    out_grad = gather_two(upstream.astype(BF16))
    attended_grad = dot_across(out_grad, out_weight).astype(BF16)
    attended_grad = (
        attended_grad.reshape(rows, Q_HEADS, HEAD).transpose(1, 0, 2).reshape(Q_HEADS * rows, HEAD)
    )
    scores = dot_across(query_rot, keys).reshape(Q_HEADS, rows, TOK_DP) * HEAD ** (-0.5)
    probabilities = jnp.where(seen_mask, jnp.exp(scores - log_total), 0.0)
    prob_grad = dot_across(attended_grad, values).reshape(Q_HEADS, rows, TOK_DP)
    low_prob = probabilities.astype(BF16).reshape(Q_HEADS * rows, TOK_DP)
    value_grad = dot_down(low_prob, attended_grad)
    row_delta = jnp.sum(prob_grad * probabilities, axis=-1, keepdims=True)
    score_grad = (probabilities * (prob_grad - row_delta)).astype(BF16)
    score_grad = score_grad.reshape(Q_HEADS * rows, TOK_DP)
    key_grad = dot_down(score_grad, query_rot) * HEAD ** (-0.5)
    pair = jnp.concatenate([key_grad, value_grad], axis=1)
    pair = pair[:rows] + over_col(pair[rows:].astype(BF16)).astype(F32)
    query_grad = dot(score_grad, keys) * HEAD ** (-0.5)
    query_grad = rotate(query_grad.reshape(Q_HEADS, rows, HEAD), cosine, -sine)
    query_grad = query_grad.transpose(1, 0, 2).reshape(rows, width)
    key_grad = rotate(pair[:, :HEAD], cosine, -sine)
    qkv_grad = jnp.concatenate([query_grad, key_grad, pair[:, HEAD:]], axis=1).astype(BF16)
    normed_grad = scatter_two(dot_across(qkv_grad, qkv_weight))
    packed = pack(
        [dot_down(x, qkv_grad) for x in halves(inputs)]
        + [dot_down(attended, x) for x in halves(out_grad)]
    )
    grad_stream, grad_gain = norm_back(upstream, normed_grad, stream, inv_rms, gain)
    return (grad_stream, packed, grad_gain)


def spread(share):
    rows = share.shape[0]
    return jnp.concatenate(
        [jnp.broadcast_to(share[:, e : e + 1], (rows, FF)) for e in range(MINE)], axis=1
    )


def expert_forward(stream, gain, router, gate_up_weight, down_weight, chosen_mask, column):
    inv_rms, normed = normalize(stream, gain)
    inputs = gather_four(normed)
    logits = dot(inputs, router)
    top = jnp.max(jnp.where(chosen_mask, logits, MASKED_SCORE), axis=1, keepdims=True)
    exponent = jnp.where(chosen_mask, jnp.exp(logits - top), 0.0)
    share = exponent / jnp.sum(exponent, axis=1, keepdims=True)
    mine = lax.dynamic_slice_in_dim(share, column * MINE, MINE, axis=1)
    gate_up = dot(inputs, gate_up_weight)
    gate_value, up_value = gate_up[:, :D], gate_up[:, D:]
    hidden = (spread(mine) * jax.nn.silu(gate_value) * up_value).astype(BF16)
    branch = scatter_four(dot(hidden, down_weight))
    cache = (stream, inv_rms, inputs, gate_up, share, mine, hidden)
    return (cache, stream + branch)


def split_low(values):
    high = values.astype(BF16)
    low = (values - high.astype(F32)).astype(BF16)
    return jnp.concatenate([high, low], axis=1)


def expert_backward(upstream, cache, gain, router, gate_up_weight, down_weight, column):
    stream, inv_rms, inputs, gate_up, share, mine, hidden = cache
    gate_value, up_value = gate_up[:, :D], gate_up[:, D:]
    rows = inputs.shape[0]
    out_grad = gather_four(upstream.astype(BF16))
    hidden_grad = dot_across(out_grad, down_weight)
    sigmoid_gate = jax.nn.sigmoid(gate_value)
    silu_gate = gate_value * sigmoid_gate
    share_grad = jnp.sum((hidden_grad * silu_gate * up_value).reshape(rows, MINE, FF), axis=2)
    activation_grad = hidden_grad * spread(mine)
    gate_grad = (
        activation_grad * up_value * sigmoid_gate * (1.0 + gate_value * (1.0 - sigmoid_gate))
    )
    gate_up_grad = jnp.concatenate([gate_grad, activation_grad * silu_gate], axis=1).astype(BF16)
    zeros = jnp.zeros_like(share_grad)
    share_grad = by_col(column, share_grad, zeros, 1)
    logits_grad = share * (share_grad - jnp.sum(share * share_grad, axis=1, keepdims=True))
    logits_low = split_low(logits_grad)
    input_grad = dot_across(gate_up_grad, gate_up_weight)
    input_grad = input_grad + dot_across(logits_low, jnp.concatenate([router, router], axis=1))
    normed_grad = scatter_four(input_grad)
    packed = pack(
        [dot_down(x, gate_up_grad) for x in halves(inputs)]
        + [dot_down(x, out_grad) for x in halves(hidden)]
    )
    router_grad = dot_down(logits_low, inputs)
    router_grad = router_grad[:EXPERTS] + router_grad[EXPERTS:]
    grad_stream, grad_gain = norm_back(upstream, normed_grad, stream, inv_rms, gain)
    return (grad_stream, packed, grad_gain, router_grad)


def sum_over_dp(packed):
    return lax.psum_scatter(packed, "dp", scatter_dimension=0, tiled=True)


def sum_everywhere(values):
    values = values + over_row(values)
    for step in (1, 8, 16, 2, 4):
        values = values + over_dp(values, lambda i, step=step: i ^ step)
    return values


def swap_half(block, column, width):
    own = lax.dynamic_slice_in_dim(block, column * width, width, axis=1)
    other = over_col(lax.dynamic_slice_in_dim(block, (1 - column) * width, width, axis=1))
    return (own, other)


def place_attention(summed, column):
    split = 2 * (Q_HEADS + 2) * HEAD
    parts = (swap_half(summed[:, :split], column, split // 2), swap_half(summed[:, split:], column, HALF))
    return [own.astype(F32) + other.astype(F32) for own, other in parts]


def place_experts(summed, column, data_index):
    own, other = swap_half(summed[:, : 4 * D], column, 2 * D)

    def unfold(block):
        return block.reshape(24, 2, MINE, FF).transpose(1, 2, 0, 3)

    gate_up = by_col(column, unfold(own), unfold(other), 1).astype(F32)
    down = summed[:, 4 * D :]
    upper = (data_index >= 16).astype(jnp.int32)
    former = lax.dynamic_slice_in_dim(down, 12 * upper, 12, axis=0)
    latter = lax.dynamic_slice_in_dim(down, 12 - 12 * upper, 12, axis=0)
    former = over_dp(former, lambda i: 2 * (i % 16) + i // 16)
    latter = over_dp(latter, lambda i: 2 * (i % 16) + 1 - i // 16)
    odd = data_index % 2 == 1
    low, high = jnp.where(odd, latter, former), jnp.where(odd, former, latter)
    down = jnp.stack([low[:, :D], high[:, :D], low[:, D:], high[:, D:]])
    down_other = over_col(half_of(down, 1 - column, 2))
    down = by_col(column, half_of(down, column, 2), down_other, 0).astype(F32)
    return (gate_up[0], gate_up[1], down)


def shards(
    tokens,
    cotangent,
    norm_gains,
    query_weight,
    key_weight,
    value_weight,
    output_weight,
    router_weight,
    gate_weight,
    up_weight,
    down_weight,
    expert_ids,
    seq_lengths,
    seq_owner,
):
    data_index = lax.axis_index("dp")
    row = lax.axis_index("row")
    column = lax.axis_index("col")
    core = data_index % 2
    stream = to_quarter(tokens, column).astype(F32)
    qkv_own = [
        jnp.concatenate([query_weight[i], key_weight[i], value_weight[i]], axis=1)
        for i in range(LAYERS)
    ]
    qkv_weights, out_weights, expert_parts = [None] * LAYERS, [None] * LAYERS, [None] * LAYERS
    for i in range(LAYERS):
        other = attention_weights(qkv_own[i], column, core)
        qkv_weights[i] = by_col(column, qkv_own[i], other, 0)
        other = attention_weights(output_weight[i], column, core)
        out_weights[i] = by_col(column, output_weight[i], other, 1)
        expert_parts[i] = expert_weights(
            gate_weight[i], up_weight[i], down_weight[i], column, data_index
        )
    gains = norm_gains.reshape(2 * LAYERS, HALF)
    router_own = router_weight.transpose(0, 2, 1).reshape(LAYERS * EXPERTS, HALF)
    small = jnp.concatenate([gains, router_own], axis=0)
    small = by_col(column, small, over_col(small), 1)
    gains = small[: 2 * LAYERS].astype(F32).reshape(LAYERS, 2, D)
    routers = small[2 * LAYERS :].reshape(LAYERS, EXPERTS, D).transpose(0, 2, 1)

    segment, position, valid_row, places = segments(seq_lengths, seq_owner, data_index)
    starts = (
        row * 256 + column * QUARTER,
        (1 - row) * 256 + column * QUARTER,
        row * 256 + (1 - column) * QUARTER,
        (1 - row) * 256 + (1 - column) * QUARTER,
    )

    def arranged(x, axis=0):
        return jnp.concatenate(
            [lax.dynamic_slice_in_dim(x, s, QUARTER, axis=axis) for s in starts], axis=axis
        )

    segment, position, places = arranged(segment), arranged(position), arranged(places)
    valid_row = arranged(valid_row.astype(jnp.int32)) > 0
    ids = arranged(expert_ids, 1)
    chosen_masks = jnp.any(
        ids[:, :, :, None] == jnp.arange(EXPERTS, dtype=jnp.int32)[None, None, None, :], axis=2
    )
    rows = 2 * QUARTER
    frequency = jnp.power(
        ROPE_THETA, jnp.arange(HEAD // 2, dtype=F32) * (-2.0 / HEAD)
    )
    angle = position[:rows].astype(F32)[:, None] * frequency[None, :]
    seen_mask = (
        (segment[:rows, None] == segment[None, :])
        & (places[None, :] <= places[:rows, None])
        & valid_row[:rows, None]
    )
    geometry = (jnp.cos(angle), jnp.sin(angle), seen_mask[None], valid_row[:rows][None, :, None])

    caches = []
    for i in range(LAYERS):
        attention_cache, stream = attention_forward(
            stream, gains[i, 0], qkv_weights[i], out_weights[i], geometry
        )
        expert_cache, stream = expert_forward(
            stream, gains[i, 1], routers[i], *expert_parts[i], chosen_masks[i], column
        )
        caches.append((attention_cache, expert_cache))
    block_output = from_quarter(stream.astype(BF16), column)
    upstream = to_quarter(cotangent, column).astype(F32)
    attention_sums, expert_sums, smalls = [None] * LAYERS, [None] * LAYERS, [None] * LAYERS
    for i in reversed(range(LAYERS)):
        attention_cache, expert_cache = caches[i]
        upstream, packed, expert_gain, router_grad = expert_backward(
            upstream, expert_cache, gains[i, 1], routers[i], *expert_parts[i], column
        )
        expert_sums[i] = sum_over_dp(packed)
        upstream, packed, attention_gain = attention_backward(
            upstream, attention_cache, gains[i, 0], qkv_weights[i], out_weights[i], geometry
        )
        attention_sums[i] = sum_over_dp(packed)
        smalls[i] = jnp.concatenate([attention_gain[None], expert_gain[None], router_grad], axis=0)
    grad_tokens = from_quarter(upstream.astype(BF16), column)

    small = jnp.concatenate(smalls, axis=0)
    small = half_of(small, column, 1) + over_col(half_of(small, 1 - column, 1))
    small = sum_everywhere(small).reshape(LAYERS, 2 + EXPERTS, HALF)
    grad_gains = small[:, :2]
    grad_router = small[:, 2:].transpose(0, 2, 1)

    attention = [place_attention(x, column) for x in attention_sums]
    qkv_grad, out_grad = [jnp.stack([x[k] for x in attention]) for k in range(2)]
    parts = [place_experts(x, column, data_index) for x in expert_sums]
    grad_gate, grad_up, grad_down = [jnp.stack([p[k] for p in parts]) for k in range(3)]
    width = Q_HEADS * HEAD
    return (
        block_output,
        grad_tokens,
        grad_gains,
        qkv_grad[:, :, :width],
        qkv_grad[:, :, width : width + HEAD],
        qkv_grad[:, :, width + HEAD :],
        out_grad,
        grad_router,
        grad_gate,
        grad_up,
        grad_down,
    )


def solution(mesh):
    in_specs = (
        P(("dp", "row"), "col"),
        P(("dp", "row"), "col"),
        P(None, None, "col"),
        P(None, "col", "row"),
        P(None, "col", "row"),
        P(None, "col", "row"),
        P(None, "row", "col"),
        P(None, "col", None),
        P(None, None, "col", "row"),
        P(None, None, "col", "row"),
        P(None, None, "row", "col"),
        P(None, "dp", None),
        P(),
        P(),
    )
    out_specs = (
        P(("dp", "row"), "col"),
        P(("dp", "row"), "col"),
        P(None, None, "col"),
        P(None, ("col", "dp"), "row"),
        P(None, ("col", "dp"), "row"),
        P(None, ("col", "dp"), "row"),
        P(None, ("row", "dp"), "col"),
        P(None, "col", None),
        P(None, None, ("col", "dp"), "row"),
        P(None, None, ("col", "dp"), "row"),
        P(None, None, ("row", "dp"), "col"),
    )
    return jax.shard_map(shards, mesh=mesh, in_specs=in_specs, out_specs=out_specs, check_vma=False)
```

```python
import jax
import jax.numpy as jnp
from jax import lax
from jax.sharding import PartitionSpec as P

D = 1536
HALF = D // 2
HEAD = 128
Q_HEADS = 6
EXPERTS = 8
MINE = 4
FF = 384
LAYERS = 2
TOK_DP = 512
QUARTER = 128
EPSILON = 1e-06
ROPE_THETA = 1000000.0
MASKED_SCORE = -1e30
ACROSS = (((1,), (1,)), ((), ()))
DOWNWARD = (((0,), (0,)), ((), ()))
SWAP = [(0, 1), (1, 0)]
DIAGONAL = [(0, 3), (1, 2), (2, 1), (3, 0)]
N_DP = 32
BF16 = jnp.bfloat16
F32 = jnp.float32


def dot(a, b):
    return jnp.dot(a, b, preferred_element_type=F32)


def dot_across(a, b):
    return lax.dot_general(a, b, ACROSS, preferred_element_type=F32)


def dot_down(a, b):
    return lax.dot_general(a, b, DOWNWARD, preferred_element_type=F32)


def over_row(x):
    return lax.ppermute(x, "row", SWAP)


def over_col(x):
    return lax.ppermute(x, "col", SWAP)


def over_both(x):
    return lax.ppermute(x, ("row", "col"), DIAGONAL)


def over_dp(x, target):
    return lax.ppermute(x, "dp", [(i, target(i)) for i in range(N_DP)])


def by_col(column, own, other, axis):
    return jnp.where(
        column == 0,
        jnp.concatenate([own, other], axis=axis),
        jnp.concatenate([other, own], axis=axis),
    )


def half_of(x, index, axis):
    size = x.shape[axis] // 2
    return lax.dynamic_slice_in_dim(x, index * size, size, axis=axis)


def halves(x):
    return [x[:, :HALF], x[:, HALF:]]


def turned(x):
    return jnp.concatenate([x[:, HALF:], x[:, :HALF]], axis=1)


def after(value, *earlier):
    return lax.optimization_barrier((value, *earlier))[0]


def pack(parts):
    return jnp.concatenate([x.astype(BF16) for x in parts], axis=1)


def to_quarter(block, column):
    own = half_of(block, column, 0)
    return jnp.concatenate([own, over_col(half_of(block, 1 - column, 0))], axis=1)


def from_quarter(block, column):
    own, other = halves(block)
    return by_col(column, own, over_col(other), 0)


def gather_four(x):
    other = turned(x)
    return jnp.concatenate([x, over_row(x), over_col(other), over_both(other)], axis=0)


def scatter_four(x):
    row, col, both = [x[i * QUARTER : (i + 1) * QUARTER].astype(BF16) for i in range(1, 4)]
    return (x[:QUARTER], over_row(row), over_col(turned(col)), over_both(turned(both)))


def total(parts):
    return sum(x.astype(F32) for x in parts)


def gather_two(x):
    return jnp.concatenate([x, over_row(x)], axis=0)


def scatter_two(parts):
    own = jnp.concatenate([x[:QUARTER] for x in parts], axis=1)
    peer = jnp.concatenate([x[QUARTER:].astype(BF16) for x in parts], axis=1)
    return (own, over_row(peer))


def segments(seq_lengths, seq_owner, data_index):
    owned_len = jnp.where(seq_owner == data_index, seq_lengths, 0)
    seq_ends = jnp.cumsum(owned_len)
    places = jnp.arange(TOK_DP, dtype=jnp.int32)
    finished = (seq_ends[None, :] <= places[:, None]).astype(jnp.int32)
    segment = jnp.sum(finished, axis=1)
    starts = jnp.sum(finished * owned_len[None, :], axis=1)
    valid_row = places < jnp.sum(owned_len)
    position = jnp.where(valid_row, places - starts, 0)
    return (segment, position, valid_row, places)


def rotate(values, cosine, sine):
    half_dim = values.shape[-1] // 2
    former = values[..., :half_dim]
    latter = values[..., half_dim:]
    return jnp.concatenate(
        [former * cosine - latter * sine, latter * cosine + former * sine], axis=-1
    )


def normalize(stream, gain):
    inv_rms = lax.rsqrt(jnp.mean(stream * stream, axis=1, keepdims=True) + EPSILON)
    return (inv_rms, (stream * inv_rms * gain).astype(BF16))


def norm_back(upstream, grad_normed, stream, inv_rms, gain):
    scaled = gain * grad_normed
    dots = jnp.sum(scaled * stream, axis=1, keepdims=True)
    grad_stream = upstream + inv_rms * scaled - stream * (inv_rms * inv_rms * inv_rms * dots / D)
    grad_gain = jnp.sum(grad_normed * stream * inv_rms, axis=0)
    return (grad_stream, grad_gain)


def attention_weights(own, column, core):
    sent = over_col(half_of(own, core, 0))
    swapped = over_dp(sent, lambda i: i ^ 1)
    return jnp.where(
        core == 0,
        jnp.concatenate([sent, swapped], axis=0),
        jnp.concatenate([swapped, sent], axis=0),
    )


def expert_weights(layer, gate, up, down, column, data_index):
    rows = 48
    start = (data_index % 16) * rows

    def piece(weight, side):
        cut = lax.dynamic_slice(weight, (layer, MINE * side, start, 0), (1, MINE, rows, FF))
        return [cut[0, e] for e in range(MINE)]

    def down_piece(side):
        place = (layer, MINE * side + data_index // 8, (data_index % 8) * rows, 0)
        return lax.dynamic_slice(down, place, (1, 1, rows, HALF))[0, 0]

    def packed(side):
        return jnp.concatenate(piece(gate, side) + piece(up, side) + [down_piece(side)], axis=1)

    other = over_col(packed(1 - column))
    own = packed(column)
    gate_up = jnp.where(data_index < 16, own[:, : 2 * D], other[:, : 2 * D])
    piece_all = jnp.concatenate([gate_up, own[:, 2 * D :], other[:, 2 * D :]], axis=1)
    whole = lax.all_gather(piece_all, "dp", axis=0, tiled=True)
    return (other, (whole[:, : 2 * D], whole[:, 2 * D :]))


def attention_forward(stream, gain, qkv_weight, out_weight, geometry):
    cosine, sine, seen_mask, row_valid = geometry
    inv_rms, normed = normalize(stream, gain)
    inputs = gather_two(normed)
    qkv = sum(dot(x, w) for x, w in zip(halves(inputs), qkv_weight))
    rows = inputs.shape[0]
    width = Q_HEADS * HEAD
    key_rot = rotate(qkv[:, width : width + HEAD], cosine, sine).astype(BF16)
    value_low = qkv[:, width + HEAD :].astype(BF16)
    pair = jnp.concatenate([key_rot, value_low], axis=1)
    pair = jnp.concatenate([pair, over_col(pair)], axis=0)
    keys, values = pair[:, :HEAD], pair[:, HEAD:]
    query = qkv[:, :width].reshape(rows, Q_HEADS, HEAD).transpose(1, 0, 2)
    query_rot = rotate(query, cosine, sine).astype(BF16).reshape(Q_HEADS * rows, HEAD)
    scores = dot_across(query_rot, keys).reshape(Q_HEADS, rows, TOK_DP) * HEAD ** (-0.5)
    row_max = jnp.max(jnp.where(seen_mask, scores, MASKED_SCORE), axis=-1, keepdims=True)
    row_max = jnp.where(row_valid, row_max, 0.0)
    exponent = jnp.where(seen_mask, jnp.exp(scores - row_max), 0.0)
    denominator = jnp.sum(exponent, axis=-1, keepdims=True) + jnp.where(row_valid, 0.0, 1.0)
    log_total = row_max + jnp.log(denominator)
    probabilities = (exponent / denominator).astype(BF16).reshape(Q_HEADS * rows, TOK_DP)
    attended = dot(probabilities, values).reshape(Q_HEADS, rows, HEAD)
    attended = attended.transpose(1, 0, 2).reshape(rows, width).astype(BF16)
    branch = total(scatter_two([dot(attended, w) for w in out_weight]))
    cache = (stream, inv_rms, inputs, query_rot, keys, values, log_total, attended)
    return (cache, stream + branch, pair)


def attention_backward(upstream, cache, gain, qkv_weight, out_weight, geometry):
    cosine, sine, seen_mask, row_valid = geometry
    stream, inv_rms, inputs, query_rot, keys, values, log_total, attended = cache
    rows = inputs.shape[0]
    width = Q_HEADS * HEAD
    out_grad = gather_two(upstream.astype(BF16))
    attended_grad = sum(dot_across(x, w) for x, w in zip(halves(out_grad), out_weight)).astype(BF16)
    attended_grad = (
        attended_grad.reshape(rows, Q_HEADS, HEAD).transpose(1, 0, 2).reshape(Q_HEADS * rows, HEAD)
    )
    scores = dot_across(query_rot, keys).reshape(Q_HEADS, rows, TOK_DP) * HEAD ** (-0.5)
    probabilities = jnp.where(seen_mask, jnp.exp(scores - log_total), 0.0)
    prob_grad = dot_across(attended_grad, values).reshape(Q_HEADS, rows, TOK_DP)
    low_prob = probabilities.astype(BF16).reshape(Q_HEADS * rows, TOK_DP)
    value_grad = dot_down(low_prob, attended_grad)
    row_delta = jnp.sum(prob_grad * probabilities, axis=-1, keepdims=True)
    score_grad = (probabilities * (prob_grad - row_delta)).astype(BF16)
    score_grad = score_grad.reshape(Q_HEADS * rows, TOK_DP)
    key_grad = dot_down(score_grad, query_rot) * HEAD ** (-0.5)
    pair = jnp.concatenate([key_grad, value_grad], axis=1)
    pair = pair[:rows] + over_col(pair[rows:].astype(BF16)).astype(F32)
    query_grad = dot(score_grad, keys) * HEAD ** (-0.5)
    query_grad = rotate(query_grad.reshape(Q_HEADS, rows, HEAD), cosine, -sine)
    query_grad = query_grad.transpose(1, 0, 2).reshape(rows, width)
    key_grad = rotate(pair[:, :HEAD], cosine, -sine)
    qkv_grad = jnp.concatenate([query_grad, key_grad, pair[:, HEAD:]], axis=1).astype(BF16)
    parts = scatter_two([dot_across(qkv_grad, w) for w in qkv_weight])
    packed = pack(
        [dot_down(x, qkv_grad) for x in halves(inputs)]
        + [dot_down(attended, x) for x in halves(out_grad)]
    )
    packed, *parts = lax.optimization_barrier((packed, *parts))
    normed_grad = total(parts)
    grad_stream, grad_gain = norm_back(upstream, normed_grad, stream, inv_rms, gain)
    return (grad_stream, packed, grad_gain)


def spread(share):
    rows = share.shape[0]
    return jnp.concatenate(
        [jnp.broadcast_to(share[:, e : e + 1], (rows, FF)) for e in range(MINE)], axis=1
    )


def expert_forward(stream, gain, router, gate_up_weight, down_weight, chosen_mask, column):
    inv_rms, normed = normalize(stream, gain)
    inputs = gather_four(normed)
    logits = dot(inputs, router)
    top = jnp.max(jnp.where(chosen_mask, logits, MASKED_SCORE), axis=1, keepdims=True)
    exponent = jnp.where(chosen_mask, jnp.exp(logits - top), 0.0)
    share = exponent / jnp.sum(exponent, axis=1, keepdims=True)
    mine = lax.dynamic_slice_in_dim(share, column * MINE, MINE, axis=1)
    gate_up = dot(inputs, gate_up_weight)
    gate_value, up_value = gate_up[:, :D], gate_up[:, D:]
    hidden = (spread(mine) * jax.nn.silu(gate_value) * up_value).astype(BF16)
    branch = total(scatter_four(dot(hidden, down_weight)))
    cache = (stream, inv_rms, inputs, gate_up, share, mine, hidden)
    return (cache, stream + branch)


def split_low(values):
    high = values.astype(BF16)
    low = (values - high.astype(F32)).astype(BF16)
    return jnp.concatenate([high, low], axis=1)


def expert_backward(
    upstream, cache, gain, router, gate_up_weight, down_weight, column, gathered=None
):
    stream, inv_rms, inputs, gate_up, share, mine, hidden = cache
    gate_value, up_value = gate_up[:, :D], gate_up[:, D:]
    out_grad = gather_four(upstream.astype(BF16)) if gathered is None else gathered
    hidden_grad = dot_across(out_grad, down_weight)
    sigmoid_gate = jax.nn.sigmoid(gate_value)
    silu_gate = gate_value * sigmoid_gate
    weighed = hidden_grad * silu_gate * up_value
    share_grad = jnp.concatenate(
        [
            jnp.sum(weighed[:, e * FF : (e + 1) * FF], axis=1, keepdims=True)
            for e in range(MINE)
        ],
        axis=1,
    )
    activation_grad = hidden_grad * spread(mine)
    gate_grad = (
        activation_grad * up_value * sigmoid_gate * (1.0 + gate_value * (1.0 - sigmoid_gate))
    )
    gate_up_grad = jnp.concatenate([gate_grad, activation_grad * silu_gate], axis=1).astype(BF16)
    zeros = jnp.zeros_like(share_grad)
    share_grad = by_col(column, share_grad, zeros, 1)
    logits_grad = share * (share_grad - jnp.sum(share * share_grad, axis=1, keepdims=True))
    logits_low = split_low(logits_grad)
    input_grad = dot_across(gate_up_grad, gate_up_weight)
    input_grad = input_grad + dot_across(logits_low, jnp.concatenate([router, router], axis=1))
    parts = scatter_four(input_grad)
    packed = pack(
        [dot_down(x, gate_up_grad) for x in halves(inputs)]
        + [dot_down(x, out_grad) for x in halves(hidden)]
    )
    packed, *parts = lax.optimization_barrier((packed, *parts))
    normed_grad = total(parts)
    router_grad = dot_down(logits_low, inputs)
    router_grad = router_grad[:EXPERTS] + router_grad[EXPERTS:]
    grad_stream, grad_gain = norm_back(upstream, normed_grad, stream, inv_rms, gain)
    return (grad_stream, packed, grad_gain, router_grad)


def sum_over_dp(packed):
    return lax.psum_scatter(packed, "dp", scatter_dimension=0, tiled=True)


def exchange(blocks, size, mine, target):
    own = lax.dynamic_index_in_dim(blocks, mine, 0, keepdims=False).astype(F32)
    for k in range(1, size):
        block = lax.dynamic_index_in_dim(blocks, (mine + k) % size, 0, keepdims=False)
        own = own + over_dp(block, lambda i, k=k: target(i, k)).astype(F32)
    return own


def sum_by_steps(packed, data_index):
    along_x, along_z, core = data_index // 8, data_index // 2 % 4, data_index % 2

    def x_step(blocks):
        return exchange(blocks, 4, along_x, lambda i, k: (i // 8 + k) % 4 * 8 + i % 8)

    def z_step(blocks):
        return exchange(
            blocks, 4, along_z, lambda i, k: i // 8 * 8 + (i // 2 % 4 + k) % 4 * 2 + i % 2
        )

    blocks = packed.reshape(4, 4, 2, 24, -1).transpose(2, 0, 1, 3, 4)
    summed = exchange(blocks, 2, core, lambda i, k: i ^ 1).astype(BF16)
    split = summed.shape[-1] // 2
    former = x_step(summed[..., :split]).astype(BF16)
    latter = z_step(summed[..., split:].transpose(1, 0, 2, 3)).astype(BF16)
    return jnp.concatenate([z_step(former), x_step(latter)], axis=1).astype(BF16)


def sum_everywhere(values):
    values = values + over_row(values)
    for step in (1, 8, 16, 2, 4):
        values = values + over_dp(values, lambda i, step=step: i ^ step)
    return values


def place_attention(summed):
    split = (Q_HEADS + 2) * HEAD
    ends = (0, split, 2 * split, 2 * split + HALF, 2 * split + 2 * HALF)
    parts = [summed[:, a:b] for a, b in zip(ends[:-1], ends[1:])]
    qkv = parts[0].astype(F32) + over_col(parts[1]).astype(F32)
    return (qkv, parts[2].astype(F32) + over_col(parts[3]).astype(F32))


def place_experts(summed, column, data_index):
    own, other = summed[:, : 2 * D], over_col(summed[:, 2 * D : 4 * D])

    def unfold(block):
        return jnp.stack(
            [
                jnp.stack([block[:, (k * MINE + e) * FF : (k * MINE + e + 1) * FF] for e in range(MINE)])
                for k in range(2)
            ]
        )

    gate_up = by_col(column, unfold(own), unfold(other), 1).astype(F32)
    down = summed[:, 4 * D :]
    upper = (data_index >= 16).astype(jnp.int32)
    former = lax.dynamic_slice_in_dim(down, 12 * upper, 12, axis=0)
    latter = lax.dynamic_slice_in_dim(down, 12 - 12 * upper, 12, axis=0)
    former = over_dp(former, lambda i: 2 * (i % 16) + i // 16)
    latter = over_dp(latter, lambda i: 2 * (i % 16) + 1 - i // 16)
    odd = data_index % 2 == 1
    low, high = jnp.where(odd, latter, former), jnp.where(odd, former, latter)
    down = jnp.stack([low[:, :D], high[:, :D], low[:, D:], high[:, D:]])
    down = by_col(column, down[:, :, :HALF], over_col(down[:, :, HALF:]), 0).astype(F32)
    return (gate_up[0], gate_up[1], down)


def shards(
    tokens,
    cotangent,
    norm_gains,
    query_weight,
    key_weight,
    value_weight,
    output_weight,
    router_weight,
    gate_weight,
    up_weight,
    down_weight,
    expert_ids,
    seq_lengths,
    seq_owner,
):
    data_index = lax.axis_index("dp")
    row = lax.axis_index("row")
    column = lax.axis_index("col")
    core = data_index % 2
    expert_parts, attention_parts = [None] * LAYERS, [None] * LAYERS

    def load_experts(i, where):
        return expert_weights(i, gate_weight, up_weight, down_weight, column, where)

    def load_attention(i, where):
        own = jnp.concatenate([query_weight[i], key_weight[i], value_weight[i]], axis=1)
        other = attention_weights(own, column, where)
        out_other = attention_weights(output_weight[i], column, after(where, other))
        return ((own, other), (output_weight[i], out_other))

    first_piece, expert_parts[0] = load_experts(0, data_index)
    stream = to_quarter(tokens, column).astype(F32)
    attention_parts[0] = load_attention(0, after(core, stream))
    gains = norm_gains.reshape(2 * LAYERS, HALF)
    router_own = router_weight.transpose(0, 2, 1).reshape(LAYERS * EXPERTS, HALF)
    small = jnp.concatenate([gains, router_own], axis=0)
    small = jnp.concatenate([small, over_col(small)], axis=1)
    gains = small[: 2 * LAYERS].astype(F32).reshape(LAYERS, 2, D)
    routers = small[2 * LAYERS :].reshape(LAYERS, EXPERTS, D).transpose(0, 2, 1)

    segment, position, valid_row, places = segments(seq_lengths, seq_owner, data_index)
    starts = (
        row * 256 + column * QUARTER,
        (1 - row) * 256 + column * QUARTER,
        row * 256 + (1 - column) * QUARTER,
        (1 - row) * 256 + (1 - column) * QUARTER,
    )

    def arranged(x, axis=0):
        return jnp.concatenate(
            [lax.dynamic_slice_in_dim(x, s, QUARTER, axis=axis) for s in starts], axis=axis
        )

    segment, position, places = arranged(segment), arranged(position), arranged(places)
    valid_row = arranged(valid_row.astype(jnp.int32)) > 0
    ids = arranged(expert_ids, 1)
    chosen_masks = jnp.any(
        ids[:, :, :, None] == jnp.arange(EXPERTS, dtype=jnp.int32)[None, None, None, :], axis=2
    )
    rows = 2 * QUARTER
    frequency = jnp.power(
        ROPE_THETA, jnp.arange(HEAD // 2, dtype=F32) * (-2.0 / HEAD)
    )
    angle = position[:rows].astype(F32)[:, None] * frequency[None, :]
    seen_mask = (
        (segment[:rows, None] == segment[None, :])
        & (places[None, :] <= places[:rows, None])
        & valid_row[:rows, None]
    )
    geometry = (jnp.cos(angle), jnp.sin(angle), seen_mask[None], valid_row[:rows][None, :, None])

    caches = []
    gathered = None
    for i in range(LAYERS):
        attention_cache, stream, pair = attention_forward(
            stream, gains[i, 0], *attention_parts[i], geometry
        )
        if i == 0:
            _, expert_parts[1] = load_experts(1, after(data_index, first_piece, pair))
            attention_parts[1] = load_attention(1, after(core, pair))
        expert_cache, stream = expert_forward(
            stream, gains[i, 1], routers[i], *expert_parts[i], chosen_masks[i], column
        )
        if i == 0:
            upstream = to_quarter(after(cotangent, expert_cache[2]), column)
            gathered = gather_four(upstream)
        caches.append((attention_cache, expert_cache))
    block_output = from_quarter(stream.astype(BF16), column)
    upstream = upstream.astype(F32)
    attention_sums, expert_sums, smalls = [None] * LAYERS, [None] * LAYERS, [None] * LAYERS
    waiting = None
    for i in reversed(range(LAYERS)):
        attention_cache, expert_cache = caches[i]
        upstream, packed, expert_gain, router_grad = expert_backward(
            upstream,
            expert_cache,
            gains[i, 1],
            routers[i],
            *expert_parts[i],
            column,
            gathered if i == LAYERS - 1 else None,
        )
        if waiting is None:
            expert_sums[i] = sum_over_dp(packed)
        else:
            summed = sum_over_dp(pack([packed, waiting]))
            expert_sums[i] = summed[:, : 6 * D]
            attention_sums[i + 1] = summed[:, 6 * D :]
        upstream, packed, attention_gain = attention_backward(
            upstream, attention_cache, gains[i, 0], *attention_parts[i], geometry
        )
        if i > 0:
            waiting = packed
        else:
            attention_sums[i] = sum_by_steps(packed, data_index)
        smalls[i] = jnp.concatenate([attention_gain[None], expert_gain[None], router_grad], axis=0)
    grad_tokens = from_quarter(upstream.astype(BF16), column)

    small = jnp.concatenate(smalls, axis=0)
    small = small[:, :HALF] + over_col(small[:, HALF:])
    small = sum_everywhere(small).reshape(LAYERS, 2 + EXPERTS, HALF)
    grad_gains = small[:, :2]
    grad_router = small[:, 2:].transpose(0, 2, 1)

    attention = [place_attention(x) for x in attention_sums]
    qkv_grad, out_grad = [jnp.stack([x[k] for x in attention]) for k in range(2)]
    parts = [place_experts(x, column, data_index) for x in expert_sums]
    grad_gate, grad_up, grad_down = [jnp.stack([p[k] for p in parts]) for k in range(3)]
    width = Q_HEADS * HEAD
    return (
        block_output,
        grad_tokens,
        grad_gains,
        qkv_grad[:, :, :width],
        qkv_grad[:, :, width : width + HEAD],
        qkv_grad[:, :, width + HEAD :],
        out_grad,
        grad_router,
        grad_gate,
        grad_up,
        grad_down,
    )


def solution(mesh):
    in_specs = (
        P(("dp", "row"), "col"),
        P(("dp", "row"), "col"),
        P(None, None, "col"),
        P(None, "col", "row"),
        P(None, "col", "row"),
        P(None, "col", "row"),
        P(None, "row", "col"),
        P(None, "col", None),
        P(None, None, "col", "row"),
        P(None, None, "col", "row"),
        P(None, None, "row", "col"),
        P(None, "dp", None),
        P(),
        P(),
    )
    out_specs = (
        P(("dp", "row"), "col"),
        P(("dp", "row"), "col"),
        P(None, None, "col"),
        P(None, ("col", "dp"), "row"),
        P(None, ("col", "dp"), "row"),
        P(None, ("col", "dp"), "row"),
        P(None, ("row", "dp"), "col"),
        P(None, "col", None),
        P(None, None, ("col", "dp"), "row"),
        P(None, None, ("col", "dp"), "row"),
        P(None, None, ("row", "dp"), "col"),
    )
    return jax.shard_map(shards, mesh=mesh, in_specs=in_specs, out_specs=out_specs, check_vma=False)
```

```python
import jax
import jax.numpy as jnp
import numpy as np
from jax import lax
from jax.experimental import pallas as pl
from jax.experimental.pallas import tpu as pltpu
from jax.sharding import PartitionSpec as P

D = 1536
HALF = D // 2
HEAD = 128
Q_HEADS = 6
EXPERTS = 8
MINE = 4
FF = 384
LAYERS = 2
TOK_DP = 512
QUARTER = 128
EPSILON = 1e-06
ROPE_THETA = 1000000.0
MASKED_SCORE = -1e30
ACROSS = (((1,), (1,)), ((), ()))
DOWNWARD = (((0,), (0,)), ((), ()))
SWAP = [(0, 1), (1, 0)]
DIAGONAL = [(0, 3), (1, 2), (2, 1), (3, 0)]
N_DP = 32
SAME_CORE = [[2 * k + core for k in range(16)] for core in range(2)]
PIECE = 48
CORE_ROWS = 384
QKV = (Q_HEADS + 2) * HEAD
VMEM_LIMIT = 48 << 20
WIDE = 512
STEPS = D // WIDE
PARTS = WIDE // 128
BF16 = jnp.bfloat16
F32 = jnp.float32


def whole(shape):
    return pl.BlockSpec(shape, lambda j: (0,) * len(shape))


BLOCK = (QUARTER, D)
ALL = (TOK_DP, D)
LANES = (TOK_DP, 128)
SLAB = pl.BlockSpec((TOK_DP, WIDE), lambda j: (0, j))


def dot(a, b):
    return jnp.dot(a, b, preferred_element_type=F32)


def dot_across(a, b):
    return lax.dot_general(a, b, ACROSS, preferred_element_type=F32)


def dot_down(a, b):
    return lax.dot_general(a, b, DOWNWARD, preferred_element_type=F32)


def over_row(x):
    return lax.ppermute(x, "row", SWAP)


def over_col(x):
    return lax.ppermute(x, "col", SWAP)


def over_both(x):
    return lax.ppermute(x, ("row", "col"), DIAGONAL)


def over_dp(x, target):
    return lax.ppermute(x, "dp", [(i, target(i)) for i in range(N_DP)])


def by_col(column, own, other, axis):
    return jnp.where(
        column == 0,
        jnp.concatenate([own, other], axis=axis),
        jnp.concatenate([other, own], axis=axis),
    )


def half_of(x, index, axis):
    size = x.shape[axis] // 2
    return lax.dynamic_slice_in_dim(x, index * size, size, axis=axis)


def halves(x):
    return [x[:, :HALF], x[:, HALF:]]


def turned(x):
    return jnp.concatenate([x[:, HALF:], x[:, :HALF]], axis=1)


def tied(*values):
    return lax.optimization_barrier(values)


def pack(parts):
    return jnp.concatenate([x.astype(BF16) for x in parts], axis=1)


def to_quarter(block, column):
    own = half_of(block, column, 0)
    return jnp.concatenate([own, over_col(half_of(block, 1 - column, 0))], axis=1)


def from_quarter(block, column):
    own, other = halves(block)
    return by_col(column, own, over_col(other), 0)


def gather_four(x):
    other = turned(x)
    return (x, over_row(x), over_col(other), over_both(other))


def total(parts):
    return sum(x.astype(F32) for x in parts)


def gather_two(x):
    return (x, over_row(x))


def segments(seq_lengths, seq_owner, data_index):
    owned_len = jnp.where(seq_owner == data_index, seq_lengths, 0)
    seq_ends = jnp.cumsum(owned_len)
    places = jnp.arange(TOK_DP, dtype=jnp.int32)
    finished = (seq_ends[None, :] <= places[:, None]).astype(jnp.int32)
    segment = jnp.sum(finished, axis=1)
    starts = jnp.sum(finished * owned_len[None, :], axis=1)
    valid_row = places < jnp.sum(owned_len)
    position = jnp.where(valid_row, places - starts, 0)
    return (segment, position, valid_row, places)


def normalize(stream, gain):
    inv_rms = lax.rsqrt(jnp.mean(stream * stream, axis=1, keepdims=True) + EPSILON)
    return (inv_rms, (stream * inv_rms * gain).astype(BF16))


def norm_back(upstream, grad_normed, stream, inv_rms, gain):
    scaled = gain * grad_normed
    dots = jnp.sum(scaled * stream, axis=1, keepdims=True)
    grad_stream = upstream + inv_rms * scaled - stream * (inv_rms * inv_rms * inv_rms * dots / D)
    return grad_stream


def pieces_kernel(layer, place, gate, up, down, query, key, value, out, *rest):
    own, other, *extra, sems = rest
    column = lax.axis_index("col")
    index = place[0]
    start = pl.multiple_of((index % 16) * PIECE, 16)
    down_start = pl.multiple_of((index % 8) * PIECE, 16)
    width = Q_HEADS * HEAD
    moves = []
    for side, target in ((column, own), (1 - column, other)):
        for k, weight in enumerate((gate, up)):
            for e in range(MINE):
                moves.append(
                    (
                        weight.at[layer, side * MINE + e, pl.ds(start, PIECE), :],
                        target.at[:, pl.ds((k * MINE + e) * FF, FF)],
                    )
                )
        moves.append(
            (
                down.at[layer, side * MINE + index // 8, pl.ds(down_start, PIECE), :],
                target.at[:, pl.ds(2 * D, HALF)],
            )
        )
    if extra:
        qkv_own, out_own, out_send, *parts = extra
        upper = pl.multiple_of(index % 2 * CORE_ROWS, 128)
        out_start = pl.multiple_of(index // 2 * PIECE, 16)
        offset = 0
        for weight, size in ((query, width), (key, HEAD), (value, HEAD)):
            columns = pl.ds(offset, size)
            moves.append((weight.at[layer], qkv_own.at[:, columns]))
            for k, target in enumerate(parts):
                moves.append((weight.at[k, pl.ds(start, PIECE), :], target.at[:, columns]))
            offset += size
        moves.append((out.at[layer], out_own))
        moves.append((out.at[layer, pl.ds(upper, CORE_ROWS), :], out_send))
        for k, target in enumerate(parts):
            moves.append(
                (
                    out.at[k, pl.ds(out_start, PIECE), pl.ds(upper, CORE_ROWS)],
                    target.at[:, pl.ds(QKV, CORE_ROWS)],
                )
            )
    copies = [pltpu.make_async_copy(a, b, sems.at[i]) for i, (a, b) in enumerate(moves)]
    for copy in copies:
        copy.start()
    for copy in copies:
        copy.wait()


def take_pieces(layer, place, weights, first):
    shapes = [(PIECE, 2 * D + HALF)] * 2
    if first:
        shapes += [(HALF, QKV), (HALF, HALF), (CORE_ROWS, HALF)]
        shapes += [(PIECE, QKV + CORE_ROWS)] * LAYERS
    anywhere = pl.BlockSpec(memory_space=pl.ANY)
    inside = pl.BlockSpec(memory_space=pltpu.VMEM)
    return pl.pallas_call(
        lambda *refs: pieces_kernel(layer, *refs),
        out_shape=[jax.ShapeDtypeStruct(x, BF16) for x in shapes],
        in_specs=[pl.BlockSpec(memory_space=pltpu.SMEM)] + [anywhere] * 7,
        out_specs=[inside] * len(shapes),
        scratch_shapes=[pltpu.SemaphoreType.DMA((31,))],
        compiler_params=pltpu.CompilerParams(vmem_limit_bytes=VMEM_LIMIT),
        name="take_pieces",
    )(place.reshape(1), *weights)


def gather_all(piece):
    return lax.all_gather(piece, "dp", axis=0, tiled=True)


def expert_piece(own, other, data_index):
    gate_up = jnp.where(data_index < 16, own[:, : 2 * D], other[:, : 2 * D])
    return jnp.concatenate([gate_up, own[:, 2 * D :], other[:, 2 * D :]], axis=1)


def attention_piece(own, other, data_index):
    qkv = jnp.where(data_index < 16, own[:, :QKV], other[:, :QKV])
    return jnp.concatenate([qkv, own[:, QKV:], other[:, QKV:]], axis=1)


def attention_whole(gathered):
    outs = []
    for k in range(2):
        part = gathered[:, QKV + k * CORE_ROWS : QKV + (k + 1) * CORE_ROWS]
        part = part.reshape(16, 2, PIECE, CORE_ROWS).transpose(0, 2, 1, 3)
        outs.append(part.reshape(HALF, HALF))
    return (gathered, outs)


def turn(x, cosine, sine):
    return x * cosine + pltpu.roll(x, HEAD // 2, 1) * sine


def rotate_kernel(cosine, sine, *rest):
    *parts, query, pair = rest
    values = parts[0][...]
    for x in parts[1:]:
        values = values + x[...].astype(F32)
    for h in range(Q_HEADS + 1):
        target, column = (query, h * HEAD) if h < Q_HEADS else (pair, 0)
        rotated = turn(values[:, h * HEAD : (h + 1) * HEAD], cosine[...], sine[...])
        target[:, column : column + HEAD] = rotated.astype(BF16)
    pair[:, HEAD:] = values[:, (Q_HEADS + 1) * HEAD :].astype(BF16)


def local_call(kernel, shapes, operands, name, specs=None):
    outs = [jax.ShapeDtypeStruct(*x) for x in shapes]
    specs = specs or {}
    return pl.pallas_call(
        kernel,
        grid=(1,),
        in_specs=[specs.get(k) or whole(x.shape) for k, x in enumerate(operands)],
        out_specs=[whole(x.shape) for x in outs],
        out_shape=outs,
        compiler_params=pltpu.CompilerParams(vmem_limit_bytes=VMEM_LIMIT),
        cost_estimate=pl.CostEstimate(flops=4 << 30, bytes_accessed=8 << 20, transcendentals=1 << 20),
        name=name,
    )(*operands)


PAIR_ROWS = 2 * QUARTER


def rotate_parts(parts, geometry):
    cosine, sine = geometry[:2]
    return local_call(
        rotate_kernel,
        [((PAIR_ROWS, Q_HEADS * HEAD), BF16), ((PAIR_ROWS, 2 * HEAD), BF16)],
        [cosine, sine, *parts],
        "rotate_heads",
    )


def keys_values(own, far):
    return [
        jnp.concatenate([x[:, k * HEAD : (k + 1) * HEAD] for x in (own, far)], axis=0)
        for k in range(2)
    ]


def attention_kernel(query, own, far, seen, valid, side, *rest):
    out_own, out_first, out_second, attended, log_total, near, peer = rest
    keys, values = keys_values(own[...], far[...])
    mask = seen[...] > 0.0
    real = valid[...]
    lanes = lax.broadcasted_iota(jnp.int32, (PAIR_ROWS, 128), 1)
    logs = jnp.zeros((PAIR_ROWS, 128), F32)
    for h in range(Q_HEADS):
        columns = slice(h * HEAD, (h + 1) * HEAD)
        scores = dot_across(query[:, columns], keys) * HEAD ** (-0.5)
        scores = jnp.where(mask, scores, MASKED_SCORE)
        top = jnp.where(real > 0.0, jnp.max(scores, axis=1, keepdims=True), 0.0)
        exponent = jnp.where(mask, jnp.exp(scores - top), 0.0)
        denominator = jnp.sum(exponent, axis=1, keepdims=True) + (1.0 - real)
        attended[:, columns] = dot((exponent / denominator).astype(BF16), values).astype(BF16)
        logs = jnp.where(lanes == h, top + jnp.log(denominator), logs)
    log_total[...] = logs
    first, second = attended[:, :CORE_ROWS], attended[:, CORE_ROWS:]
    straight = side[0, 0] == 0
    left = jnp.where(straight, first, second)
    right = jnp.where(straight, second, first)
    for k, x in enumerate(
        (dot(attended[...], out_own[...]), dot(left, out_first[...]) + dot(right, out_second[...]))
    ):
        columns = slice(k * HALF, (k + 1) * HALF)
        near[:, columns] = x[:QUARTER]
        peer[:, columns] = x[QUARTER:].astype(BF16)


def attention_forward(parts, geometry, meanwhile):
    _, _, seen, valid = geometry
    query, pair = rotate_parts(parts, geometry)
    far = over_col(pair)
    pair, far, (side, *out_parts) = meanwhile(pair, far)
    side = jnp.broadcast_to(jnp.asarray(side, jnp.int32), (1, 1))
    smem = pl.BlockSpec(memory_space=pltpu.SMEM)
    attended, log_total, near, peer = local_call(
        attention_kernel,
        [
            ((PAIR_ROWS, Q_HEADS * HEAD), BF16),
            ((PAIR_ROWS, 128), F32),
            (BLOCK, F32),
            (BLOCK, BF16),
        ],
        [query, pair, far, seen, valid, side, *out_parts],
        "attention_forward",
        {5: smem},
    )
    return ((query, pair, far, log_total, attended), (near, over_row(peer)))


def attention_back_kernel(cosine, sine, seen, upstream, peer, out_own, out_other, *rest):
    query, own, far, log_total, out_grad, query_grad, pair_own, pair_far = rest
    out_grad[:QUARTER, :] = upstream[...]
    out_grad[QUARTER:, :] = peer[...]
    keys, values = keys_values(own[...], far[...])
    mask = seen[...] > 0.0
    attended_grad = dot_across(out_grad[:, :HALF], out_own[...])
    attended_grad = (attended_grad + dot_across(out_grad[:, HALF:], out_other[...])).astype(BF16)
    key_grad = jnp.zeros((TOK_DP, HEAD), F32)
    value_grad = jnp.zeros((TOK_DP, HEAD), F32)
    for h in range(Q_HEADS):
        columns = slice(h * HEAD, (h + 1) * HEAD)
        head, grad = query[:, columns], attended_grad[:, columns]
        scores = dot_across(head, keys) * HEAD ** (-0.5)
        shift = log_total[:, h : h + 1]
        weights = jnp.where(mask, jnp.exp(scores - shift), 0.0)
        weight_grad = dot_across(grad, values)
        value_grad += dot_down(weights.astype(BF16), grad)
        inner = jnp.sum(weight_grad * weights, axis=1, keepdims=True)
        score_grad = (weights * (weight_grad - inner)).astype(BF16)
        key_grad += dot_down(score_grad, head)
        part = turn(dot(score_grad, keys) * HEAD ** (-0.5), cosine[...], -sine[...])
        query_grad[:, columns] = part.astype(BF16)
    key_grad = key_grad * HEAD ** (-0.5)
    pair_own[:, :HEAD] = key_grad[:PAIR_ROWS]
    pair_own[:, HEAD:] = value_grad[:PAIR_ROWS]
    pair_far[:, :HEAD] = key_grad[PAIR_ROWS:].astype(BF16)
    pair_far[:, HEAD:] = value_grad[PAIR_ROWS:].astype(BF16)


def input_grad_kernel(cosine, sine, query_grad, own, far, inputs, weight, *rest):
    qkv_grad, near, peer, grad_gain = rest
    pair = own[...] + far[...].astype(F32)
    qkv_grad[:, : Q_HEADS * HEAD] = query_grad[...]
    key_grad = turn(pair[:, :HEAD], cosine[...], -sine[...])
    qkv_grad[:, Q_HEADS * HEAD : QKV - HEAD] = key_grad.astype(BF16)
    qkv_grad[:, QKV - HEAD :] = pair[:, HEAD:].astype(BF16)
    partial = dot_across(qkv_grad[...], weight[...])
    near[...] = partial[:QUARTER]
    peer[...] = partial[QUARTER:].astype(BF16)
    grad_gain[...] = jnp.sum(inputs[...].astype(F32) * partial, axis=0, keepdims=True)


def attention_grads_kernel(inputs, attended, qkv_grad, out_grad, order, send, keep):
    def product(left, right, column):
        turned_left = dot_across(order[...], left).astype(BF16)
        result = dot(turned_left, right).astype(BF16)
        columns = slice(column, column + result.shape[1])
        send[:, columns] = result[:CORE_ROWS]
        keep[:, columns] = result[CORE_ROWS:]

    for k in range(2):
        half = slice(k * HALF, (k + 1) * HALF)
        product(inputs[:, half], qkv_grad[...], k * (QKV + HALF))
        product(attended[...], out_grad[:, half], k * (QKV + HALF) + QKV)


def attention_grads(*operands):
    return pl.pallas_call(
        attention_grads_kernel,
        out_shape=[jax.ShapeDtypeStruct((CORE_ROWS, 2 * (QKV + HALF)), BF16)] * 2,
        compiler_params=pltpu.CompilerParams(vmem_limit_bytes=VMEM_LIMIT),
        cost_estimate=pl.CostEstimate(
            flops=4 * QUARTER * HALF * 6 * HALF, bytes_accessed=10 << 20, transcendentals=0
        ),
        name="attention_weight_grads",
    )(*operands)


def attention_backward(upstream, cache, gain, weights, geometry, order, meanwhile, finish):
    cosine, sine, seen, _ = geometry
    stream, inv_rms, inputs, query, pair, far, log_total, attended = cache
    gathered, out_weight = weights
    out_grads = meanwhile(gather_two(upstream.astype(BF16)))
    width = Q_HEADS * HEAD
    out_grad, query_grad, pair_own, pair_far = local_call(
        attention_back_kernel,
        [
            ((PAIR_ROWS, D), BF16),
            ((PAIR_ROWS, width), BF16),
            ((PAIR_ROWS, 2 * HEAD), F32),
            ((PAIR_ROWS, 2 * HEAD), BF16),
        ],
        [cosine, sine, seen, *out_grads, *out_weight, query, pair, far, log_total],
        "attention_backward",
    )
    qkv_grad, near, peer, grad_gain = local_call(
        input_grad_kernel,
        [((PAIR_ROWS, QKV), BF16), (BLOCK, F32), (BLOCK, BF16), ((1, D), F32)],
        [cosine, sine, query_grad, pair_own, over_col(pair_far), inputs, gathered],
        "attention_input_grad",
        {6: pl.BlockSpec((D, QKV), lambda j: (0, 0))},
    )
    parts = (near, over_row(peer))
    packed = attention_grads(inputs, attended, qkv_grad, out_grad, order)
    parts = finish(parts, packed, grad_gain[0] / gain)
    return norm_back(upstream, total(parts), stream, inv_rms, gain)


def send_blocks(values, own, row, col, both):
    own[...] = values[:QUARTER, :]
    row[...] = values[QUARTER : 2 * QUARTER, :].astype(BF16)
    for k, target in ((2, col), (3, both)):
        block = values[k * QUARTER : (k + 1) * QUARTER, :].astype(BF16)
        target[:, :HALF] = block[:, HALF:]
        target[:, HALF:] = block[:, :HALF]


def join_blocks(blocks, target):
    for k, block in enumerate(blocks):
        target[k * QUARTER : (k + 1) * QUARTER, :] = block[...]


def share_of(share, step, k):
    lanes = lax.broadcasted_iota(jnp.int32, share.shape, 1)
    mine = lanes == lax.axis_index("col") * MINE + (step * PARTS + k) // 3
    return (mine, jnp.sum(jnp.where(mine, share, 0.0), axis=1, keepdims=True))


def forward_kernel(x0, x1, x2, x3, chosen, router, wg, wu, wd, *rest):
    inputs, gate, up, hidden, share, own, row, col, both, total_ref = rest
    step = pl.program_id(0)

    @pl.when(step == 0)
    def _():
        join_blocks((x0, x1, x2, x3), inputs)
        logits = dot_across(inputs[...], router[...])
        picked = chosen[...] > 0.0
        top = jnp.max(jnp.where(picked, logits, MASKED_SCORE), axis=1, keepdims=True)
        exponent = jnp.where(picked, jnp.exp(jnp.where(picked, logits - top, 0.0)), 0.0)
        share[...] = exponent / jnp.sum(exponent, axis=1, keepdims=True)

    x = inputs[...]
    gate_value = dot(x, wg[...])
    up_value = dot(x, wu[...])
    gate[...] = gate_value
    up[...] = up_value
    low = (gate_value / (1.0 + jnp.exp(-gate_value))) * up_value
    for k in range(PARTS):
        part = slice(k * 128, (k + 1) * 128)
        hidden[:, part] = (share_of(share[...], step, k)[1] * low[:, part]).astype(BF16)
    result = dot(hidden[...], wd[...])

    @pl.when(step == 0)
    def _():
        total_ref[...] = result

    @pl.when(step > 0)
    def _():
        total_ref[...] += result

    @pl.when(step == STEPS - 1)
    def _():
        send_blocks(total_ref[...], own, row, col, both)


def weight_specs():
    return [
        pl.BlockSpec((D, WIDE), lambda j: (0, j)),
        pl.BlockSpec((D, WIDE), lambda j: (0, STEPS + j)),
        pl.BlockSpec((WIDE, D), lambda j: (j, 2)),
    ]


COST = pl.CostEstimate(flops=6 * TOK_DP * D * D, bytes_accessed=24 << 20, transcendentals=TOK_DP * D)


def send_four(blocks):
    own, row, col, both = blocks
    return (own, over_row(row), over_col(col), over_both(both))


def expert_forward(stream, gain, router, weights, chosen, meanwhile):
    inv_rms, normed = normalize(stream, gain)
    gathered = meanwhile(gather_four(normed))
    weights = weights[0]
    out = pl.pallas_call(
        forward_kernel,
        grid=(STEPS,),
        in_specs=[whole(BLOCK)] * 4 + [whole(LANES), whole((128, D))] + weight_specs(),
        out_specs=[whole(ALL), SLAB, SLAB, SLAB, whole(LANES)] + [whole(BLOCK)] * 4,
        out_shape=[
            jax.ShapeDtypeStruct(ALL, BF16),
            jax.ShapeDtypeStruct(ALL, F32),
            jax.ShapeDtypeStruct(ALL, F32),
            jax.ShapeDtypeStruct(ALL, BF16),
            jax.ShapeDtypeStruct(LANES, F32),
            jax.ShapeDtypeStruct(BLOCK, F32),
        ]
        + [jax.ShapeDtypeStruct(BLOCK, BF16)] * 3,
        scratch_shapes=[pltpu.VMEM(ALL, F32)],
        compiler_params=pltpu.CompilerParams(vmem_limit_bytes=VMEM_LIMIT),
        cost_estimate=COST,
        name="experts_forward",
    )(*gathered, chosen, router, weights, weights, weights)
    inputs, gate, up, hidden, share, own, row, col, both = out
    return ((stream, inv_rms, inputs, gate, up, share, hidden), (own, row, col, both))


def backward_kernel(y0, y1, y2, y3, gate, up, share, router, wg, wu, wd, *rest):
    grads, gate_grad, up_grad, logits_grad, own, row, col, both, total_ref, share_grad = rest
    step = pl.program_id(0)

    @pl.when(step == 0)
    def _():
        join_blocks((y0, y1, y2, y3), grads)
        share_grad[...] = jnp.zeros_like(share_grad)

    hidden_grad = dot_across(grads[...], wd[...])
    gate_value, up_value = gate[...], up[...]
    sigmoid = 1.0 / (1.0 + jnp.exp(-gate_value))
    silu = gate_value * sigmoid
    weighed = hidden_grad * silu * up_value
    slope = hidden_grad * up_value * sigmoid * (1.0 + gate_value * (1.0 - sigmoid))
    through_up = hidden_grad * silu
    for k in range(PARTS):
        part = slice(k * 128, (k + 1) * 128)
        lanes, mine = share_of(share[...], step, k)
        share_grad[...] += jnp.where(
            lanes, jnp.sum(weighed[:, part], axis=1, keepdims=True), 0.0
        )
        gate_grad[:, part] = (mine * slope[:, part]).astype(BF16)
        up_grad[:, part] = (mine * through_up[:, part]).astype(BF16)
    low_gate, low_up = gate_grad[...], up_grad[...]
    result = dot_across(low_gate, wg[...]) + dot_across(low_up, wu[...])

    @pl.when(step == 0)
    def _():
        total_ref[...] = result

    @pl.when(step > 0)
    def _():
        total_ref[...] += result

    @pl.when(step == STEPS - 1)
    def _():
        part = share_grad[...]
        inner = jnp.sum(share[...] * part, axis=1, keepdims=True)
        exact = share[...] * (part - inner)
        high = exact.astype(BF16)
        low = (exact - high.astype(F32)).astype(BF16)
        logits_grad[:, :128] = high
        logits_grad[:, 128:] = low
        through = dot(high, router[...]) + dot(low, router[...])
        send_blocks(total_ref[...] + through, own, row, col, both)


def grads_kernel(inputs, hidden, gate_grad, up_grad, out_grad, order_x, order_h, *rest):
    *arrived, packed, turned_ref = rest
    step = pl.program_id(0)

    for at in range(6):

        @pl.when(step == at)
        def _(at=at):
            if at in (0, 2):
                turned_ref[...] = dot_across(order_x[...], inputs[...]).astype(BF16)
            if at >= 4:
                turned_ref[...] = dot_across(order_h[...], hidden[...]).astype(BF16)
            right = (gate_grad, up_grad, gate_grad, up_grad, out_grad, out_grad)[at]
            result = dot(turned_ref[...], right[...])
            for x in arrived:
                result = result + x[...].astype(F32)
            packed[...] = result.astype(packed.dtype)


def weight_grads(inputs, hidden, gate_grad, up_grad, out_grad, orders, half, arrived):
    def left(place):
        return pl.BlockSpec((TOK_DP, HALF), lambda j: (0, place(j)))

    tile = pl.BlockSpec((CORE_ROWS, D), lambda j: (0, j))
    rows = pl.BlockSpec((CORE_ROWS, HALF), lambda j: (half, 0))
    return pl.pallas_call(
        grads_kernel,
        grid=(6,),
        in_specs=[
            left(lambda j: jnp.minimum(j // 2, 1)),
            left(lambda j: jnp.maximum(j - 4, 0)),
        ]
        + [whole(ALL)] * 3
        + [rows] * 2
        + [tile] * len(arrived),
        out_specs=tile,
        out_shape=jax.ShapeDtypeStruct((CORE_ROWS, 6 * D), F32 if arrived else BF16),
        scratch_shapes=[pltpu.VMEM((CORE_ROWS, TOK_DP), BF16)],
        compiler_params=pltpu.CompilerParams(vmem_limit_bytes=VMEM_LIMIT),
        cost_estimate=pl.CostEstimate(
            flops=4 * TOK_DP * D * D, bytes_accessed=24 << 20, transcendentals=0
        ),
        name="expert_weight_grads",
    )(inputs, hidden, gate_grad, up_grad, out_grad, *orders, *arrived)


def expert_backward(upstream, cache, gain, router, weights, orders, gathered, settle):
    stream, inv_rms, inputs, gate, up, share, hidden = cache
    out = pl.pallas_call(
        backward_kernel,
        grid=(STEPS,),
        in_specs=[whole(BLOCK)] * 4
        + [SLAB, SLAB, whole(LANES), whole((128, D))]
        + weight_specs(),
        out_specs=[whole(ALL), SLAB, SLAB, whole((TOK_DP, 256))] + [whole(BLOCK)] * 4,
        out_shape=[jax.ShapeDtypeStruct(ALL, BF16)] * 3
        + [jax.ShapeDtypeStruct((TOK_DP, 256), BF16), jax.ShapeDtypeStruct(BLOCK, F32)]
        + [jax.ShapeDtypeStruct(BLOCK, BF16)] * 3,
        scratch_shapes=[pltpu.VMEM(ALL, F32), pltpu.VMEM(LANES, F32)],
        compiler_params=pltpu.CompilerParams(vmem_limit_bytes=VMEM_LIMIT),
        cost_estimate=COST,
        name="experts_backward",
    )(*gathered, gate, up, share, router, weights, weights, weights)
    out_grad, gate_grad, up_grad, logits_grad, own, row, col, both = out
    parts = settle(send_four((own, row, col, both)))
    operands = (inputs, hidden, gate_grad, up_grad, out_grad, orders)
    packed = weight_grads(*operands, 0, [])
    packed, *parts = tied(packed, *parts)
    arrived = over_dp(packed, lambda i: i ^ 1)
    normed_grad = total(parts)
    router_grad = dot_down(logits_grad, inputs)
    router_grad = router_grad[:EXPERTS] + router_grad[128 : 128 + EXPERTS]
    grad_stream = norm_back(upstream, normed_grad, stream, inv_rms, gain)
    grad_gain = jnp.sum(normed_grad * stream * inv_rms, axis=0)


    def finish(*values):
        return tied(weight_grads(*operands, 1, [arrived]), *values)

    return (grad_stream, finish, grad_gain, router_grad)


def exchange_orders(data_index):
    along_x, along_z, core = data_index // 8, data_index // 2 % 4, data_index % 2
    rows = np.arange(HALF, dtype=np.int32)
    block, inner = rows // 24, rows % 24
    side = jnp.where(block < 16, 1 - core, core)
    straight = block % 16 * 2 + side
    target = (along_x + block // 4) % 4 * 8 + (along_z + block) % 4 * 2 + side
    source = jnp.arange(HALF, dtype=jnp.int32)
    by_core, units, by_steps = [
        (x[:, None] == source[None, :]).astype(BF16)
        for x in (
            straight * 24 + inner,
            inner // 12 * FF + straight * 12 + inner % 12,
            target * 24 + inner,
        )
    ]
    return ([by_core, units], by_steps)


def shift_x(x, k):
    return over_dp(x, lambda i: (i // 8 + k) % 4 * 8 + i % 8)


def shift_z(x, k):
    return over_dp(x, lambda i: i // 8 * 8 + (i // 2 % 4 + k) % 4 * 2 + i % 2)


def sum_pairs(*sets):
    got = [over_dp(x[0], lambda i: i ^ 1) for x in sets]
    return [total((x[1], y)).astype(BF16) for x, y in zip(sets, got)]


def sum_round(values, shifts):
    rows = values[0].shape[0] // 4
    blocks = [[x[k * rows : (k + 1) * rows] for k in range(4)] for x in values]
    got = [
        [x[0]] + [shift(x[k], k) for k in range(1, 4)] for x, shift in zip(blocks, shifts)
    ]
    return [total(x).astype(BF16) for x in got]


def sum_over_cores(values):
    return lax.psum_scatter(
        values, "dp", scatter_dimension=0, tiled=True, axis_index_groups=SAME_CORE
    )


def sum_everywhere(values):
    values = values + over_row(values)
    for step in (1, 8, 16, 2, 4):
        values = values + over_dp(values, lambda i, step=step: i ^ step)
    return values


def place(expert_own, expert_other, attention, column):
    wide = 2 * D
    far = [expert_other[:, :wide]] if expert_other is not None else []
    far += [other for _, other in attention]
    if expert_own is not None:
        far += [expert_own[:, wide:][:, HALF:], expert_other[:, wide:][:, HALF:]]
    got = over_col(jnp.concatenate(far, axis=1))
    ends, offset = [], 0
    for x in far:
        ends.append(got[:, offset : offset + x.shape[1]])
        offset += x.shape[1]
    results = []
    if expert_own is not None:
        gate_up = [
            jnp.stack([block[:, e * FF : (e + 1) * FF] for e in range(2 * MINE)])
            for block in (expert_own[:, :wide], ends[0])
        ]
        near = [x[:, wide : wide + HALF] for x in (expert_own, expert_other)]
        down = [
            jnp.stack([x[k * 12 : (k + 1) * 12] for x in pair for k in range(2)])
            for pair in (near, ends[-2:])
        ]
        results = [
            by_col(column, gate_up[0][k * MINE : (k + 1) * MINE], gate_up[1][k * MINE : (k + 1) * MINE], 0)
            for k in range(2)
        ] + [by_col(column, *down, 0)]
        results = [x.astype(F32) for x in results]
        ends = ends[1:-2]
    sums = [total((own, x)) for (own, _), x in zip(attention, ends)]
    return (results, [(x[:, :QKV], x[:, QKV:]) for x in sums])


def shards(
    tokens,
    cotangent,
    norm_gains,
    query_weight,
    key_weight,
    value_weight,
    output_weight,
    router_weight,
    gate_weight,
    up_weight,
    down_weight,
    expert_ids,
    seq_lengths,
    seq_owner,
):
    data_index = lax.axis_index("dp")
    row = lax.axis_index("row")
    column = lax.axis_index("col")
    core = data_index % 2
    weights = (
        gate_weight, up_weight, down_weight, query_weight, key_weight, value_weight, output_weight
    )

    squares = jnp.sum(jnp.square(tokens.astype(F32)), axis=1)
    small = jnp.concatenate(
        [
            norm_gains.reshape(2 * LAYERS, HALF).astype(F32),
            router_weight.transpose(0, 2, 1).reshape(LAYERS * EXPERTS, HALF).astype(F32),
            jnp.pad(squares, (0, HALF - 2 * QUARTER))[None],
        ],
        axis=0,
    )
    small, index = tied(small, data_index)
    small_far = over_col(small)
    own, other, qkv_own, out_own, out_send, *attention_own = take_pieces(0, index, weights, True)
    squares = small[-1, : 2 * QUARTER] + small_far[-1, : 2 * QUARTER]
    inv_rms = lax.rsqrt(squares / D + EPSILON)[:, None]
    normed = (tokens.astype(F32) * inv_rms * small[0]).astype(BF16)
    normed_pair = (normed, over_row(normed))
    piece = expert_piece(own, over_col(other), data_index)
    piece, out_send, *normed_pair = tied(piece, out_send, *normed_pair)
    expert_parts = [gather_all(piece)]
    near, away = [
        jnp.concatenate([half_of(x, side, 0) for x in normed_pair], axis=0)
        for side in (column, 1 - column)
    ]
    partial = dot(jnp.concatenate([near, away], axis=0), qkv_own)
    qkv_far = over_col(partial[2 * QUARTER :].astype(BF16))
    out_sent = over_col(out_send)
    qkv = partial[: 2 * QUARTER]
    qkv, data_index, seq_lengths, expert_ids = tied(qkv, data_index, seq_lengths, expert_ids)
    loaded = take_pieces(1, data_index, weights, False)
    small = jnp.concatenate([small[:-1], small_far[:-1]], axis=1)
    gains = small[: 2 * LAYERS].reshape(LAYERS, 2, D)
    routers = small[2 * LAYERS :].reshape(LAYERS, EXPERTS, D).astype(BF16)
    routers = jnp.pad(routers, ((0, 0), (0, 128 - EXPERTS), (0, 0)))

    segment, position, valid_row, places = segments(seq_lengths, seq_owner, data_index)
    starts = (
        row * 256 + column * QUARTER,
        (1 - row) * 256 + column * QUARTER,
        row * 256 + (1 - column) * QUARTER,
        (1 - row) * 256 + (1 - column) * QUARTER,
    )

    def arranged(x, axis=0):
        return jnp.concatenate(
            [lax.dynamic_slice_in_dim(x, s, QUARTER, axis=axis) for s in starts], axis=axis
        )

    segment, position, places = arranged(segment), arranged(position), arranged(places)
    valid_row = arranged(valid_row.astype(jnp.int32)) > 0
    ids = arranged(expert_ids, 1)
    lanes = jnp.arange(128, dtype=jnp.int32)
    chosen = jnp.any(ids[:, :, :, None] == lanes, axis=2).astype(F32)
    rows = 2 * QUARTER
    frequency = jnp.power(
        ROPE_THETA, jnp.arange(HEAD // 2, dtype=F32) * (-2.0 / HEAD)
    )
    angle = position[:rows].astype(F32)[:, None] * frequency[None, :]
    seen_mask = (
        (segment[:rows, None] == segment[None, :])
        & (places[None, :] <= places[:rows, None])
        & valid_row[:rows, None]
    )
    cosine, sine = jnp.cos(angle), jnp.sin(angle)
    geometry = (
        jnp.concatenate([cosine, cosine], axis=1),
        jnp.concatenate([-sine, sine], axis=1),
        seen_mask.astype(F32),
        valid_row[:rows].astype(F32)[:, None],
    )

    by_core, by_steps = exchange_orders(data_index)
    attention_other = [None] * LAYERS

    def first_out(pair, pair_far):
        nonlocal out_sent, by_core, by_steps, routers, chosen, far, loaded
        values = tied(
            pair, pair_far, out_sent, tokens, attention_own[1], by_steps, routers, chosen,
            *by_core, *loaded
        )
        pair, pair_far, out_sent, rest, attention_own[1], by_steps, routers, chosen = values[:8]
        by_core, loaded = values[8:10], list(values[10:])
        attention_other[1] = over_col(attention_own[1])
        far = to_quarter(rest, column)[:, HALF:]
        return (pair, pair_far, (core, out_own, out_sent, over_dp(out_sent, lambda i: i ^ 1)))

    far = None
    cache, parts = attention_forward([qkv, qkv_far], geometry, first_out)
    stream = jnp.concatenate([half_of(tokens, column, 0), far], axis=1).astype(F32)
    quarter_rms = half_of(inv_rms, column, 0)
    far_normed = (far.astype(F32) * quarter_rms * gains[0, 0, HALF:]).astype(BF16)
    attention_caches = [(stream, quarter_rms, None) + cache]
    stream = stream + total(parts)
    second_attention = attention_piece(attention_own[1], attention_other[1], data_index)

    def load_second(gathered):
        nonlocal second_attention, upstream
        upstream = to_quarter(cotangent, column)
        second_attention, expert_parts[0], loaded[1], upstream, *gathered = tied(
            second_attention, expert_parts[0], loaded[1], upstream, *gathered
        )
        loaded.append(over_col(loaded[1]))
        return gathered

    upstream = None
    expert_cache, sends = expert_forward(
        stream, gains[0, 1], routers[0], expert_parts, chosen[0], load_second
    )
    stream = stream + total(send_four(sends))
    caches = [expert_cache]
    second_weights = attention_whole(gather_all(second_attention))
    second_piece = expert_piece(loaded[0], loaded[2], data_index)

    inv_rms, normed = normalize(stream, gains[1, 0])
    inputs = jnp.concatenate(gather_two(normed), axis=0)
    qkv, second_piece = tied(dot(inputs, second_weights[0][:, :QKV]), second_piece)
    expert_parts.append(gather_all(second_piece))
    first_inputs = []

    def start_back(pair, pair_far):
        pair, pair_far, attention_own[0], source = tied(
            pair, pair_far, attention_own[0], far_normed
        )
        attention_other[0] = over_col(attention_own[0])
        first_inputs.append(source)
        first_inputs.append(over_row(source))
        out_own, out_other = second_weights[1]
        return (pair, pair_far, (0, out_own, out_other[:CORE_ROWS], out_other[CORE_ROWS:]))

    cache, parts = attention_forward([qkv], geometry, start_back)
    attention_caches.append((stream, inv_rms, inputs) + cache)
    inputs = jnp.concatenate([near, jnp.concatenate(first_inputs, axis=0)], axis=1)
    attention_caches[0] = attention_caches[0][:2] + (inputs,) + attention_caches[0][3:]
    stream = stream + total(parts)
    first_attention = attention_piece(attention_own[0], attention_other[0], data_index)

    def load_last(gathered):
        nonlocal first_attention, upstream
        first_attention, expert_parts[1], upstream, *gathered = tied(
            first_attention, expert_parts[1], upstream, *gathered
        )
        return gathered

    expert_cache, sends = expert_forward(
        stream, gains[1, 1], routers[1], expert_parts[1:], chosen[1], load_last
    )
    caches.append(expert_cache)
    first_whole = gather_all(first_attention)
    gathered = gather_four(upstream)

    upstream, finish_second, expert_gain, router_grad = expert_backward(
        upstream.astype(F32),
        caches[1],
        gains[1, 1],
        routers[1],
        expert_parts[1],
        by_core,
        gathered,
        lambda x: x,
    )
    smalls = [None, expert_gain[None], router_grad]
    waiting = None

    def start_first(out_grads):
        nonlocal first_whole, expert_sum
        expert_sum, first_whole, *out_grads = finish_second(first_whole, *out_grads)
        expert_sum = sum_over_cores(expert_sum)
        return out_grads

    expert_sum = None

    def keep(parts, packed, attention_gain):
        nonlocal waiting
        waiting = packed
        smalls[0] = attention_gain[None]
        return parts

    upstream = attention_backward(
        upstream,
        attention_caches[1],
        gains[1, 0],
        second_weights,
        geometry,
        by_steps,
        start_first,
        keep,
    )
    gathered = gather_four(upstream.astype(BF16))
    second_sum = sum_pairs(waiting)
    second_sum, *gathered = tied(*second_sum, *gathered)
    second_sum = sum_round([second_sum], (shift_x,))

    def settle(parts):
        nonlocal second_sum
        second_sum, *parts = tied(*second_sum, *parts)
        second_sum = sum_round([second_sum], (shift_z,))[0]
        return parts

    upstream, finish_first, expert_gain, router_grad = expert_backward(
        upstream,
        caches[0],
        gains[0, 1],
        routers[0],
        expert_parts[0],
        by_core,
        gathered,
        settle,
    )
    first_weights = attention_whole(first_whole)
    first_sum = None
    last = None

    def start_sum(out_grads):
        nonlocal sends, first_sum, expert_sum
        values = finish_first(expert_sum, *sends, *out_grads)
        first_sum, expert_sum, sends, out_grads = values[0], values[1], values[2:6], values[6:]
        first_sum = sum_over_cores(first_sum)
        return out_grads

    def keep_last(parts, packed, attention_gain):
        nonlocal last, second_sum
        *last, second_sum, own, peer = tied(*packed, second_sum, *parts)
        last = sum_pairs(last)
        smalls[:0] = [attention_gain[None], expert_gain[None], router_grad]
        return (own, peer)

    upstream = attention_backward(
        upstream,
        attention_caches[0],
        gains[0, 0],
        first_weights,
        geometry,
        by_steps,
        start_sum,
        keep_last,
    )
    block_output = from_quarter((stream + total(send_four(sends))).astype(BF16), column)
    small = jnp.concatenate(smalls, axis=0)
    small = small[:, :HALF] + over_col(small[:, HALF:])
    small = sum_everywhere(small).reshape(LAYERS, 2 + EXPERTS, HALF)
    small, expert_sum, last = tied(small, expert_sum, *last)

    def columns(values):
        return [
            jnp.concatenate(
                [
                    values[:, k * 2 * D : (k + 1) * 2 * D],
                    values[:, (4 + k) * D : (5 + k) * D],
                ],
                axis=1,
            ).astype(BF16)
            for k in range(2)
        ]

    last = sum_round([last], (shift_x,))
    second, _ = place(*columns(expert_sum), [], column)
    last, *second = tied(*last, *second)
    last = sum_round([last], (shift_z,))[0]
    half = QKV + HALF
    first, ((qkv_second, out_second), (qkv_first, out_first)) = place(
        *columns(first_sum), [(x[:, :half], x[:, half:]) for x in (second_sum, last)], column
    )
    grad_tokens = from_quarter(upstream.astype(BF16), column)

    grad_gains = small[:, :2]
    grad_router = small[:, 2:].transpose(0, 2, 1)

    qkv_grad = jnp.stack([qkv_first, qkv_second])
    out_grad = jnp.stack([out_first, out_second])
    grad_gate, grad_up, grad_down = [jnp.stack([x, y]) for x, y in zip(first, second)]
    width = Q_HEADS * HEAD
    return (
        block_output,
        grad_tokens,
        grad_gains,
        qkv_grad[:, :, :width],
        qkv_grad[:, :, width : width + HEAD],
        qkv_grad[:, :, width + HEAD :],
        out_grad,
        grad_router,
        grad_gate,
        grad_up,
        grad_down,
    )


def solution(mesh):
    in_specs = (
        P(("dp", "row"), "col"),
        P(("dp", "row"), "col"),
        P(None, None, "col"),
        P(None, "col", "row"),
        P(None, "col", "row"),
        P(None, "col", "row"),
        P(None, "row", "col"),
        P(None, "col", None),
        P(None, None, "col", "row"),
        P(None, None, "col", "row"),
        P(None, None, "row", "col"),
        P(None, "dp", None),
        P(),
        P(),
    )
    out_specs = (
        P(("dp", "row"), "col"),
        P(("dp", "row"), "col"),
        P(None, None, "col"),
        P(None, ("col", "dp"), "row"),
        P(None, ("col", "dp"), "row"),
        P(None, ("col", "dp"), "row"),
        P(None, ("row", "dp"), "col"),
        P(None, "col", None),
        P(None, None, ("col", "dp"), "row"),
        P(None, None, ("col", "dp"), "row"),
        P(None, None, ("row", "dp"), "col"),
    )
    return jax.shard_map(shards, mesh=mesh, in_specs=in_specs, out_specs=out_specs, check_vma=False)
```

```python
import jax
import jax.numpy as jnp
import numpy as np
from jax import lax
from jax.experimental import pallas as pl
from jax.experimental.pallas import tpu as pltpu
from jax.sharding import PartitionSpec as P

D = 1536
HALF = D // 2
HEAD = 128
Q_HEADS = 6
EXPERTS = 8
MINE = 4
FF = 384
LAYERS = 2
TOK_DP = 512
QUARTER = 128
EPSILON = 1e-06
ROPE_THETA = 1000000.0
MASKED_SCORE = -1e30
ACROSS = (((1,), (1,)), ((), ()))
DOWNWARD = (((0,), (0,)), ((), ()))
SWAP = [(0, 1), (1, 0)]
DIAGONAL = [(0, 3), (1, 2), (2, 1), (3, 0)]
N_DP = 32
SAME_CORE = [[2 * k + core for k in range(16)] for core in range(2)]
PIECE = 48
CORE_ROWS = 384
QKV = (Q_HEADS + 2) * HEAD
VMEM_LIMIT = 48 << 20
WIDE = 512
STEPS = D // WIDE
PARTS = WIDE // 128
BF16 = jnp.bfloat16
F32 = jnp.float32


def whole(shape):
    return pl.BlockSpec(shape, lambda j: (0,) * len(shape))


BLOCK = (QUARTER, D)
ALL = (TOK_DP, D)
LANES = (TOK_DP, 128)
SLAB = pl.BlockSpec((TOK_DP, WIDE), lambda j: (0, j))


def dot(a, b):
    return jnp.dot(a, b, preferred_element_type=F32)


def dot_across(a, b):
    return lax.dot_general(a, b, ACROSS, preferred_element_type=F32)


def dot_down(a, b):
    return lax.dot_general(a, b, DOWNWARD, preferred_element_type=F32)


def over_row(x):
    return lax.ppermute(x, "row", SWAP)


def over_col(x):
    return lax.ppermute(x, "col", SWAP)


def over_both(x):
    return lax.ppermute(x, ("row", "col"), DIAGONAL)


def over_dp(x, target):
    return lax.ppermute(x, "dp", [(i, target(i)) for i in range(N_DP)])


def by_col(column, own, other, axis):
    return jnp.where(
        column == 0,
        jnp.concatenate([own, other], axis=axis),
        jnp.concatenate([other, own], axis=axis),
    )


def half_of(x, index, axis):
    size = x.shape[axis] // 2
    return lax.dynamic_slice_in_dim(x, index * size, size, axis=axis)


def halves(x):
    return [x[:, :HALF], x[:, HALF:]]


def turned(x):
    return jnp.concatenate([x[:, HALF:], x[:, :HALF]], axis=1)


def tied(*values):
    return lax.optimization_barrier(values)


def later(index, value):
    return index + (value[0, 0].astype(F32) * 0.0).astype(jnp.int32)


def pack(parts):
    return jnp.concatenate([x.astype(BF16) for x in parts], axis=1)


def to_quarter(block, column):
    own = half_of(block, column, 0)
    return jnp.concatenate([own, over_col(half_of(block, 1 - column, 0))], axis=1)


def from_quarter(block, column):
    own, other = halves(block)
    return by_col(column, own, over_col(other), 0)


def gather_four(x):
    other = turned(x)
    return (x, over_row(x), over_col(other), over_both(other))


def total(parts):
    return sum(x.astype(F32) for x in parts)


def gather_two(x):
    return (x, over_row(x))


def segments(seq_lengths, seq_owner, data_index):
    owned_len = jnp.where(seq_owner == data_index, seq_lengths, 0)
    seq_ends = jnp.cumsum(owned_len)
    places = jnp.arange(TOK_DP, dtype=jnp.int32)
    finished = (seq_ends[None, :] <= places[:, None]).astype(jnp.int32)
    segment = jnp.sum(finished, axis=1)
    starts = jnp.sum(finished * owned_len[None, :], axis=1)
    valid_row = places < jnp.sum(owned_len)
    position = jnp.where(valid_row, places - starts, 0)
    return (segment, position, valid_row, places)


def normalize(stream, gain):
    inv_rms = lax.rsqrt(jnp.mean(stream * stream, axis=1, keepdims=True) + EPSILON)
    return (inv_rms, (stream * inv_rms * gain).astype(BF16))


def norm_back(upstream, grad_normed, stream, inv_rms, gain):
    scaled = gain * grad_normed
    dots = jnp.sum(scaled * stream, axis=1, keepdims=True)
    grad_stream = upstream + inv_rms * scaled - stream * (inv_rms * inv_rms * inv_rms * dots / D)
    return grad_stream


def pieces_kernel(layer, place, gate, up, down, query, key, value, out, *rest):
    own, other, *extra, sems = rest
    column = lax.axis_index("col")
    index = place[0]
    start = pl.multiple_of((index % 16) * PIECE, 16)
    down_start = pl.multiple_of((index % 8) * PIECE, 16)
    upper = pl.multiple_of(index % 2 * CORE_ROWS, 128)
    out_start = pl.multiple_of(index // 2 * PIECE, 16)
    heads = ((query, Q_HEADS * HEAD), (key, HEAD), (value, HEAD))
    moves = []
    for side, target in ((column, own), (1 - column, other)):
        for k, weight in enumerate((gate, up)):
            for e in range(MINE):
                moves.append(
                    (
                        weight.at[layer, side * MINE + e, pl.ds(start, PIECE), :],
                        target.at[:, pl.ds((k * MINE + e) * FF, FF)],
                    )
                )
        moves.append(
            (
                down.at[layer, side * MINE + index // 8, pl.ds(down_start, PIECE), :],
                target.at[:, pl.ds(2 * D, HALF)],
            )
        )
        moves.append(
            (
                out.at[1 - layer, pl.ds(out_start, PIECE), pl.ds(upper, CORE_ROWS)],
                target.at[:, pl.ds(2 * D + HALF, CORE_ROWS)],
            )
        )
        offset = 2 * D + HALF + CORE_ROWS
        for weight, size in heads:
            moves.append(
                (weight.at[1 - layer, pl.ds(start, PIECE), :], target.at[:, pl.ds(offset, size)])
            )
            offset += size
    if extra:
        qkv_own, out_own, out_send = extra
        offset = 0
        for weight, size in heads:
            moves.append((weight.at[layer], qkv_own.at[:, pl.ds(offset, size)]))
            offset += size
        moves.append((out.at[layer], out_own))
        moves.append((out.at[layer, pl.ds(upper, CORE_ROWS), :], out_send))
    copies = [pltpu.make_async_copy(a, b, sems.at[i]) for i, (a, b) in enumerate(moves)]
    for copy in copies:
        copy.start()
    for copy in copies:
        copy.wait()


def take_pieces(layer, place, weights, first):
    shapes = [(PIECE, 2 * D + HALF + CORE_ROWS + QKV)] * 2
    if first:
        shapes += [(HALF, QKV), (HALF, HALF), (CORE_ROWS, HALF)]
    anywhere = pl.BlockSpec(memory_space=pltpu.HBM)
    inside = pl.BlockSpec(memory_space=pltpu.VMEM)
    return pl.pallas_call(
        lambda *refs: pieces_kernel(layer, *refs),
        out_shape=[jax.ShapeDtypeStruct(x, BF16) for x in shapes],
        in_specs=[pl.BlockSpec(memory_space=pltpu.SMEM)] + [anywhere] * 7,
        out_specs=[inside] * len(shapes),
        scratch_shapes=[pltpu.SemaphoreType.DMA((31,))],
        compiler_params=pltpu.CompilerParams(vmem_limit_bytes=VMEM_LIMIT),
        name="take_pieces",
    )(place.reshape(1), *weights)


def gather_all(piece):
    return lax.all_gather(piece, "dp", axis=0, tiled=True)


def piece_kernel(place, own, other, packed):
    gate_up = 2 * D
    outs = gate_up + HALF
    qkv = outs + CORE_ROWS
    near = place[0] < 16
    packed[:, :gate_up] = jnp.where(near, own[:, :gate_up], other[:, :gate_up])
    offset = gate_up
    for lower, upper in ((gate_up, outs), (outs, qkv)):
        for x in (own, other):
            packed[:, offset : offset + upper - lower] = x[:, lower:upper]
            offset += upper - lower
    packed[:, offset:] = jnp.where(near, own[:, qkv:], other[:, qkv:])


def whole_piece(own, other, data_index):
    return local_call(
        piece_kernel,
        [((PIECE, 3 * D + HALF + QKV), BF16)],
        [data_index.reshape(1), own, other],
        "whole_piece",
        {0: pl.BlockSpec(memory_space=pltpu.SMEM)},
    )[0]


def first_product_kernel(own, peer, weight, near, away, near_rows):
    column = lax.axis_index("col")
    for k, side in enumerate((column, 1 - column)):
        start = pl.multiple_of(side * QUARTER, QUARTER)
        rows = jnp.concatenate([x[pl.ds(start, QUARTER), :] for x in (own, peer)], axis=0)
        result = dot(rows, weight[...])
        if k == 0:
            near_rows[...] = rows
            near[...] = result
        else:
            away[...] = result.astype(BF16)


def first_product(own, peer, weight):
    return local_call(
        first_product_kernel,
        [((PAIR_ROWS, QKV), F32), ((PAIR_ROWS, QKV), BF16), ((PAIR_ROWS, HALF), BF16)],
        [own, peer, weight],
        "first_product",
    )


OUT_SPEC = pl.BlockSpec((D, HALF), lambda j: (0, 6))
QKV_SPECS = [pl.BlockSpec((D, 256), lambda j, k=k: (0, 21 + k)) for k in range(4)]


def output_weight(gathered, target):
    for k in range(2):
        for row in range(16):
            for side in range(2):
                start = (row * 2 + side) * PIECE
                target[
                    row * PIECE : (row + 1) * PIECE,
                    k * HALF + side * CORE_ROWS : k * HALF + (side + 1) * CORE_ROWS,
                ] = gathered[start : start + PIECE, k * CORE_ROWS : (k + 1) * CORE_ROWS]


def turn(x, cosine, sine):
    return x * cosine + pltpu.roll(x, HEAD // 2, 1) * sine


def write_heads(values, cosine, sine, query, pair):
    for h in range(Q_HEADS + 1):
        target, column = (query, h * HEAD) if h < Q_HEADS else (pair, 0)
        rotated = turn(values[:, h * HEAD : (h + 1) * HEAD], cosine[...], sine[...])
        target[:, column : column + HEAD] = rotated.astype(BF16)
    pair[:, HEAD:] = values[:, (Q_HEADS + 1) * HEAD :].astype(BF16)


def first_heads_kernel(cosine, sine, near, far, query, pair):
    write_heads(near[...] + far[...].astype(F32), cosine, sine, query, pair)


def heads_kernel(cosine, sine, own, peer, *rest):
    *weights, query, pair, inputs = rest
    inputs[:QUARTER, :] = own[...]
    inputs[QUARTER:, :] = peer[...]
    values = jnp.concatenate([dot(inputs[...], w[...]) for w in weights], axis=1)
    write_heads(values, cosine, sine, query, pair)


def local_call(kernel, shapes, operands, name, specs=None, scratch=()):
    outs = [jax.ShapeDtypeStruct(*x) for x in shapes]
    specs = specs or {}
    return pl.pallas_call(
        kernel,
        grid=(1,),
        in_specs=[specs.get(k) or whole(x.shape) for k, x in enumerate(operands)],
        out_specs=[whole(x.shape) for x in outs],
        out_shape=outs,
        scratch_shapes=scratch,
        compiler_params=pltpu.CompilerParams(vmem_limit_bytes=VMEM_LIMIT),
        cost_estimate=pl.CostEstimate(flops=4 << 30, bytes_accessed=8 << 20, transcendentals=1 << 20),
        name=name,
    )(*operands)


PAIR_ROWS = 2 * QUARTER
HEAD_SHAPES = [((PAIR_ROWS, Q_HEADS * HEAD), BF16), ((PAIR_ROWS, 2 * HEAD), BF16)]
OUT_SCRATCH = [pltpu.VMEM((HALF, D), BF16)]


def first_heads(near, far, geometry):
    return local_call(first_heads_kernel, HEAD_SHAPES, [*geometry[:2], near, far], "first_heads")


def make_heads(own, peer, weights, geometry):
    return local_call(
        heads_kernel,
        HEAD_SHAPES + [((PAIR_ROWS, D), BF16)],
        [*geometry[:2], own, peer] + [weights] * 4,
        "make_heads",
        {4 + k: x for k, x in enumerate(QKV_SPECS)},
    )


def keys_values(own, far):
    return [
        jnp.concatenate([x[:, k * HEAD : (k + 1) * HEAD] for x in (own, far)], axis=0)
        for k in range(2)
    ]


def attention_kernel(query, own, far, seen, valid, *rest):
    *side_outs, attended, log_total, near, peer, out_weight = rest
    keys, values = keys_values(own[...], far[...])
    mask = seen[...] > 0.0
    real = valid[...]
    lanes = lax.broadcasted_iota(jnp.int32, (PAIR_ROWS, 128), 1)
    logs = jnp.zeros((PAIR_ROWS, 128), F32)
    for h in range(Q_HEADS):
        columns = slice(h * HEAD, (h + 1) * HEAD)
        scores = dot_across(query[:, columns], keys) * HEAD ** (-0.5)
        scores = jnp.where(mask, scores, MASKED_SCORE)
        top = jnp.where(real > 0.0, jnp.max(scores, axis=1, keepdims=True), 0.0)
        exponent = jnp.where(mask, jnp.exp(scores - top), 0.0)
        denominator = jnp.sum(exponent, axis=1, keepdims=True) + (1.0 - real)
        attended[:, columns] = dot((exponent / denominator).astype(BF16), values).astype(BF16)
        logs = jnp.where(lanes == h, top + jnp.log(denominator), logs)
    log_total[...] = logs
    if len(side_outs) == 1:
        output_weight(side_outs[0], out_weight)
    else:
        out_own, out_first, out_second = side_outs
        straight = lax.axis_index("dp") % 2 == 0
        first, second = out_first[...], out_second[...]
        out_weight[:, :HALF] = out_own[...]
        out_weight[:CORE_ROWS, HALF:] = jnp.where(straight, first, second)
        out_weight[CORE_ROWS:, HALF:] = jnp.where(straight, second, first)
    branch = dot(attended[...], out_weight[...])
    near[...] = branch[:QUARTER]
    peer[...] = branch[QUARTER:].astype(BF16)


def attention_forward(query, pair, geometry, meanwhile):
    _, _, seen, valid = geometry
    far = over_col(pair)
    pair, far, out_parts = meanwhile(pair, far)
    attended, log_total, near, peer = local_call(
        attention_kernel,
        [
            ((PAIR_ROWS, Q_HEADS * HEAD), BF16),
            ((PAIR_ROWS, 128), F32),
            (BLOCK, F32),
            (BLOCK, BF16),
        ],
        [query, pair, far, seen, valid, *out_parts],
        "attention_forward",
        {5: OUT_SPEC} if len(out_parts) == 1 else None,
        OUT_SCRATCH,
    )
    return ((query, pair, far, log_total, attended), (near, over_row(peer)))


def attention_back_kernel(cosine, sine, seen, upstream, peer, gathered, *rest):
    query, own, far, log_total, out_grad, query_grad, pair_own, pair_far, out_weight = rest
    out_grad[:QUARTER, :] = upstream[...]
    out_grad[QUARTER:, :] = peer[...]
    output_weight(gathered, out_weight)
    keys, values = keys_values(own[...], far[...])
    mask = seen[...] > 0.0
    attended_grad = dot_across(out_grad[...], out_weight[...]).astype(BF16)
    key_grad = jnp.zeros((TOK_DP, HEAD), F32)
    value_grad = jnp.zeros((TOK_DP, HEAD), F32)
    for h in range(Q_HEADS):
        columns = slice(h * HEAD, (h + 1) * HEAD)
        head, grad = query[:, columns], attended_grad[:, columns]
        scores = dot_across(head, keys) * HEAD ** (-0.5)
        shift = log_total[:, h : h + 1]
        weights = jnp.where(mask, jnp.exp(scores - shift), 0.0)
        weight_grad = dot_across(grad, values)
        value_grad += dot_down(weights.astype(BF16), grad)
        inner = jnp.sum(weight_grad * weights, axis=1, keepdims=True)
        score_grad = (weights * (weight_grad - inner)).astype(BF16)
        key_grad += dot_down(score_grad, head)
        part = turn(dot(score_grad, keys) * HEAD ** (-0.5), cosine[...], -sine[...])
        query_grad[:, columns] = part.astype(BF16)
    key_grad = key_grad * HEAD ** (-0.5)
    pair_own[:, :HEAD] = key_grad[:PAIR_ROWS]
    pair_own[:, HEAD:] = value_grad[:PAIR_ROWS]
    pair_far[:, :HEAD] = key_grad[PAIR_ROWS:].astype(BF16)
    pair_far[:, HEAD:] = value_grad[PAIR_ROWS:].astype(BF16)


def input_grad_kernel(cosine, sine, query_grad, own, far, inputs, *rest):
    *weights, qkv_grad, near, peer, grad_gain = rest
    pair = own[...] + far[...].astype(F32)
    qkv_grad[:, : Q_HEADS * HEAD] = query_grad[...]
    key_grad = turn(pair[:, :HEAD], cosine[...], -sine[...])
    qkv_grad[:, Q_HEADS * HEAD : QKV - HEAD] = key_grad.astype(BF16)
    qkv_grad[:, QKV - HEAD :] = pair[:, HEAD:].astype(BF16)
    partial = sum(
        dot_across(qkv_grad[:, k * 256 : (k + 1) * 256], w[...]) for k, w in enumerate(weights)
    )
    near[...] = partial[:QUARTER]
    peer[...] = partial[QUARTER:].astype(BF16)
    grad_gain[...] = jnp.sum(inputs[...].astype(F32) * partial, axis=0, keepdims=True)


def attention_grads_kernel(inputs, attended, qkv_grad, out_grad, order, send, keep):
    def product(left, right, column):
        turned_left = dot_across(order[...], left).astype(BF16)
        result = dot(turned_left, right).astype(BF16)
        columns = slice(column, column + result.shape[1])
        send[:, columns] = result[:CORE_ROWS]
        keep[:, columns] = result[CORE_ROWS:]

    for k in range(2):
        half = slice(k * HALF, (k + 1) * HALF)
        product(inputs[:, half], qkv_grad[...], k * (QKV + HALF))
        product(attended[...], out_grad[:, half], k * (QKV + HALF) + QKV)


def attention_grads(*operands):
    return pl.pallas_call(
        attention_grads_kernel,
        out_shape=[jax.ShapeDtypeStruct((CORE_ROWS, 2 * (QKV + HALF)), BF16)] * 2,
        compiler_params=pltpu.CompilerParams(vmem_limit_bytes=VMEM_LIMIT),
        cost_estimate=pl.CostEstimate(
            flops=4 * QUARTER * HALF * 6 * HALF, bytes_accessed=10 << 20, transcendentals=0
        ),
        name="attention_weight_grads",
    )(*operands)


def attention_backward(upstream, cache, gain, weights, geometry, meanwhile, between, finish):
    cosine, sine, seen, _ = geometry
    stream, inv_rms, inputs, query, pair, far, log_total, attended = cache
    out_grads = meanwhile(gather_two(upstream.astype(BF16)))
    width = Q_HEADS * HEAD
    out_grad, query_grad, pair_own, pair_far = local_call(
        attention_back_kernel,
        [
            ((PAIR_ROWS, D), BF16),
            ((PAIR_ROWS, width), BF16),
            ((PAIR_ROWS, 2 * HEAD), F32),
            ((PAIR_ROWS, 2 * HEAD), BF16),
        ],
        [cosine, sine, seen, *out_grads, weights, query, pair, far, log_total],
        "attention_backward",
        {5: OUT_SPEC},
        OUT_SCRATCH,
    )
    qkv_grad, near, peer, grad_gain = local_call(
        input_grad_kernel,
        [((PAIR_ROWS, QKV), BF16), (BLOCK, F32), (BLOCK, BF16), ((1, D), F32)],
        [cosine, sine, query_grad, pair_own, over_col(between(pair_far)), inputs] + [weights] * 4,
        "attention_input_grad",
        {6 + k: x for k, x in enumerate(QKV_SPECS)},
    )
    parts = (near, over_row(peer))
    operands = (inputs, attended, qkv_grad, out_grad)
    parts = finish(parts, operands, grad_gain[0] / gain)
    return norm_back(upstream, total(parts), stream, inv_rms, gain)


def send_blocks(values, own, row, col, both):
    own[...] = values[:QUARTER, :]
    row[...] = values[QUARTER : 2 * QUARTER, :].astype(BF16)
    for k, target in ((2, col), (3, both)):
        block = values[k * QUARTER : (k + 1) * QUARTER, :].astype(BF16)
        target[:, :HALF] = block[:, HALF:]
        target[:, HALF:] = block[:, :HALF]


def join_blocks(blocks, target):
    for k, block in enumerate(blocks):
        target[k * QUARTER : (k + 1) * QUARTER, :] = block[...]


def share_of(share, step, k):
    lanes = lax.broadcasted_iota(jnp.int32, share.shape, 1)
    mine = lanes == lax.axis_index("col") * MINE + (step * PARTS + k) // 3
    return (mine, jnp.sum(jnp.where(mine, share, 0.0), axis=1, keepdims=True))


def forward_kernel(x0, x1, x2, x3, chosen, router, wg, wu, *rest):
    *down, inputs, gate, up, hidden, share = rest[: 6 if len(rest) > 5 else 5]
    sends = rest[6:]
    step = pl.program_id(0)

    @pl.when(step == 0)
    def _():
        join_blocks((x0, x1, x2, x3), inputs)
        logits = dot_across(inputs[...], router[...])
        picked = chosen[...] > 0.0
        top = jnp.max(jnp.where(picked, logits, MASKED_SCORE), axis=1, keepdims=True)
        exponent = jnp.where(picked, jnp.exp(jnp.where(picked, logits - top, 0.0)), 0.0)
        share[...] = exponent / jnp.sum(exponent, axis=1, keepdims=True)

    x = inputs[...]
    gate_value = dot(x, wg[...])
    up_value = dot(x, wu[...])
    gate[...] = gate_value
    up[...] = up_value
    low = (gate_value / (1.0 + jnp.exp(-gate_value))) * up_value
    for k in range(PARTS):
        part = slice(k * 128, (k + 1) * 128)
        hidden[:, part] = (share_of(share[...], step, k)[1] * low[:, part]).astype(BF16)
    if not down:
        return
    *sends, total_ref = sends
    result = dot(hidden[...], down[0][...])

    @pl.when(step == 0)
    def _():
        total_ref[...] = result

    @pl.when(step > 0)
    def _():
        total_ref[...] += result

    @pl.when(step == STEPS - 1)
    def _():
        send_blocks(total_ref[...], *sends)


def weight_specs():
    return [
        pl.BlockSpec((D, WIDE), lambda j: (0, j)),
        pl.BlockSpec((D, WIDE), lambda j: (0, STEPS + j)),
        pl.BlockSpec((WIDE, D), lambda j: (j, 2)),
    ]


COST = pl.CostEstimate(flops=6 * TOK_DP * D * D, bytes_accessed=24 << 20, transcendentals=TOK_DP * D)


def send_four(blocks):
    own, row, col, both = blocks
    return (own, over_row(row), over_col(col), over_both(both))


def expert_forward(stream, gain, router, weights, chosen, meanwhile, last):
    inv_rms, normed = normalize(stream, gain)
    gathered = meanwhile(gather_four(normed))
    weights = weights[0]
    count = 2 if last else 3
    sends = [] if last else [jax.ShapeDtypeStruct(BLOCK, F32)]
    sends = sends + [jax.ShapeDtypeStruct(BLOCK, BF16)] * (3 * len(sends))
    out = pl.pallas_call(
        forward_kernel,
        grid=(STEPS,),
        in_specs=[whole(BLOCK)] * 4 + [whole(LANES), whole((128, D))] + weight_specs()[:count],
        out_specs=[whole(ALL), SLAB, SLAB, SLAB, whole(LANES)] + [whole(BLOCK)] * len(sends),
        out_shape=[
            jax.ShapeDtypeStruct(ALL, BF16),
            jax.ShapeDtypeStruct(ALL, F32),
            jax.ShapeDtypeStruct(ALL, F32),
            jax.ShapeDtypeStruct(ALL, BF16),
            jax.ShapeDtypeStruct(LANES, F32),
        ]
        + sends,
        scratch_shapes=[] if last else [pltpu.VMEM(ALL, F32)],
        compiler_params=pltpu.CompilerParams(vmem_limit_bytes=VMEM_LIMIT),
        cost_estimate=COST,
        name="experts_forward",
    )(*gathered, chosen, router, *[weights] * count)
    inputs, gate, up, hidden, share, *sends = out
    return ((stream, inv_rms, inputs, gate, up, share, hidden), sends)


def last_down_kernel(hidden, weight, own, row, col, both):
    send_blocks(dot(hidden[...], weight[...]), own, row, col, both)


def last_down(hidden, weights):
    return local_call(
        last_down_kernel,
        [(BLOCK, F32)] + [(BLOCK, BF16)] * 3,
        [hidden, weights],
        "last_down",
        {1: pl.BlockSpec((D, D), lambda j: (0, 2))},
    )


def backward_kernel(y0, y1, y2, y3, gate, up, share, router, wg, wu, wd, *rest):
    grads, gate_grad, up_grad, logits_grad, own, row, col, both, total_ref, share_grad = rest
    step = pl.program_id(0)

    @pl.when(step == 0)
    def _():
        join_blocks((y0, y1, y2, y3), grads)
        share_grad[...] = jnp.zeros_like(share_grad)

    hidden_grad = dot_across(grads[...], wd[...])
    gate_value, up_value = gate[...], up[...]
    sigmoid = 1.0 / (1.0 + jnp.exp(-gate_value))
    silu = gate_value * sigmoid
    weighed = hidden_grad * silu * up_value
    slope = hidden_grad * up_value * sigmoid * (1.0 + gate_value * (1.0 - sigmoid))
    through_up = hidden_grad * silu
    for k in range(PARTS):
        part = slice(k * 128, (k + 1) * 128)
        lanes, mine = share_of(share[...], step, k)
        share_grad[...] += jnp.where(
            lanes, jnp.sum(weighed[:, part], axis=1, keepdims=True), 0.0
        )
        gate_grad[:, part] = (mine * slope[:, part]).astype(BF16)
        up_grad[:, part] = (mine * through_up[:, part]).astype(BF16)
    low_gate, low_up = gate_grad[...], up_grad[...]
    result = dot_across(low_gate, wg[...]) + dot_across(low_up, wu[...])

    @pl.when(step == 0)
    def _():
        total_ref[...] = result

    @pl.when(step > 0)
    def _():
        total_ref[...] += result

    @pl.when(step == STEPS - 1)
    def _():
        part = share_grad[...]
        inner = jnp.sum(share[...] * part, axis=1, keepdims=True)
        exact = share[...] * (part - inner)
        high = exact.astype(BF16)
        low = (exact - high.astype(F32)).astype(BF16)
        logits_grad[:, :128] = high
        logits_grad[:, 128:] = low
        through = dot(high, router[...]) + dot(low, router[...])
        send_blocks(total_ref[...] + through, own, row, col, both)


def grads_kernel(inputs, hidden, gate_grad, up_grad, out_grad, order_x, order_h, *rest):
    *arrived, packed, turned_ref = rest
    step = pl.program_id(0)

    for at in range(6):

        @pl.when(step == at)
        def _(at=at):
            if at in (0, 2):
                turned_ref[...] = dot_across(order_x[...], inputs[...]).astype(BF16)
            if at >= 4:
                turned_ref[...] = dot_across(order_h[...], hidden[...]).astype(BF16)
            right = (gate_grad, up_grad, gate_grad, up_grad, out_grad, out_grad)[at]
            result = dot(turned_ref[...], right[...])
            for x in arrived:
                result = result + x[...].astype(F32)
            packed[...] = result.astype(packed.dtype)


def weight_grads(inputs, hidden, gate_grad, up_grad, out_grad, orders, half, arrived):
    def left(place):
        return pl.BlockSpec((TOK_DP, HALF), lambda j: (0, place(j)))

    tile = pl.BlockSpec((CORE_ROWS, D), lambda j: (0, j))
    rows = pl.BlockSpec((CORE_ROWS, HALF), lambda j: (half, 0))
    return pl.pallas_call(
        grads_kernel,
        grid=(6,),
        in_specs=[
            left(lambda j: jnp.minimum(j // 2, 1)),
            left(lambda j: jnp.maximum(j - 4, 0)),
        ]
        + [whole(ALL)] * 3
        + [rows] * 2
        + [tile] * len(arrived),
        out_specs=tile,
        out_shape=jax.ShapeDtypeStruct((CORE_ROWS, 6 * D), F32 if arrived else BF16),
        scratch_shapes=[pltpu.VMEM((CORE_ROWS, TOK_DP), BF16)],
        compiler_params=pltpu.CompilerParams(vmem_limit_bytes=VMEM_LIMIT),
        cost_estimate=pl.CostEstimate(
            flops=4 * TOK_DP * D * D, bytes_accessed=24 << 20, transcendentals=0
        ),
        name="expert_weight_grads",
    )(inputs, hidden, gate_grad, up_grad, out_grad, *orders, *arrived)


def expert_backward(upstream, cache, gain, router, weights, orders, gathered, settle):
    stream, inv_rms, inputs, gate, up, share, hidden = cache
    out = pl.pallas_call(
        backward_kernel,
        grid=(STEPS,),
        in_specs=[whole(BLOCK)] * 4
        + [SLAB, SLAB, whole(LANES), whole((128, D))]
        + weight_specs(),
        out_specs=[whole(ALL), SLAB, SLAB, whole((TOK_DP, 256))] + [whole(BLOCK)] * 4,
        out_shape=[jax.ShapeDtypeStruct(ALL, BF16)] * 3
        + [jax.ShapeDtypeStruct((TOK_DP, 256), BF16), jax.ShapeDtypeStruct(BLOCK, F32)]
        + [jax.ShapeDtypeStruct(BLOCK, BF16)] * 3,
        scratch_shapes=[pltpu.VMEM(ALL, F32), pltpu.VMEM(LANES, F32)],
        compiler_params=pltpu.CompilerParams(vmem_limit_bytes=VMEM_LIMIT),
        cost_estimate=COST,
        name="experts_backward",
    )(*gathered, gate, up, share, router, weights, weights, weights)
    out_grad, gate_grad, up_grad, logits_grad, own, row, col, both = out
    parts = settle(send_four((own, row, col, both)))
    operands = (inputs, hidden, gate_grad, up_grad, out_grad, orders)
    packed = weight_grads(*operands, 0, [])
    own, *parts = parts
    packed, *parts = tied(packed, *parts)
    parts = (own, *parts)
    arrived = over_dp(packed, lambda i: i ^ 1)
    normed_grad = total(parts)
    router_grad = dot_down(logits_grad, inputs)
    router_grad = router_grad[:EXPERTS] + router_grad[128 : 128 + EXPERTS]
    grad_stream = norm_back(upstream, normed_grad, stream, inv_rms, gain)
    grad_gain = jnp.sum(normed_grad * stream * inv_rms, axis=0)


    def finish(*values):
        return tied(weight_grads(*operands, 1, [arrived]), *values)

    return (grad_stream, finish, grad_gain, router_grad)


def exchange_orders(data_index):
    along_x, along_z, core = data_index // 8, data_index // 2 % 4, data_index % 2
    rows = np.arange(HALF, dtype=np.int32)
    block, inner = rows // 24, rows % 24
    side = jnp.where(block < 16, 1 - core, core)
    straight = block % 16 * 2 + side
    target = (along_x + block // 4) % 4 * 8 + (along_z + block) % 4 * 2 + side
    source = jnp.arange(HALF, dtype=jnp.int32)
    target_z = (along_x + block) % 4 * 8 + (along_z + block // 4) % 4 * 2 + side
    by_core, units, x_first, z_first = [
        (x[:, None] == source[None, :]).astype(BF16)
        for x in (
            straight * 24 + inner,
            inner // 12 * FF + straight * 12 + inner % 12,
            target * 24 + inner,
            target_z * 24 + inner,
        )
    ]
    return ([by_core, units], [x_first, z_first])


def shift_x(x, k):
    return over_dp(x, lambda i: (i // 8 + k) % 4 * 8 + i % 8)


def shift_z(x, k):
    return over_dp(x, lambda i: i // 8 * 8 + (i // 2 % 4 + k) % 4 * 2 + i % 2)


def sum_pairs(*sets):
    got = [over_dp(x[0], lambda i: i ^ 1) for x in sets]
    return [total((x[1], y)).astype(BF16) for x, y in zip(sets, got)]


def sum_round(values, shifts):
    rows = values[0].shape[0] // 4
    blocks = [[x[k * rows : (k + 1) * rows] for k in range(4)] for x in values]
    got = [
        [x[0]] + [shift(x[k], k) for k in range(1, 4)] for x, shift in zip(blocks, shifts)
    ]
    return [total(x).astype(BF16) for x in got]


def sum_over_cores(values):
    return lax.psum_scatter(
        values, "dp", scatter_dimension=0, tiled=True, axis_index_groups=SAME_CORE
    )


def sum_in_order(values, shift, place):
    got = jnp.stack([values] + [shift(values, k) for k in range(1, 4)])
    return sum(
        lax.dynamic_index_in_dim(got, (place - j) % 4, 0, keepdims=False) for j in range(4)
    )


def place(expert_own, expert_other, attention, column):
    wide = 2 * D
    far = [expert_other[:, :wide]] if expert_other is not None else []
    far += [other for _, other in attention]
    if expert_own is not None:
        far += [expert_own[:, wide:][:, HALF:], expert_other[:, wide:][:, HALF:]]
    got = over_col(jnp.concatenate(far, axis=1))
    ends, offset = [], 0
    for x in far:
        ends.append(got[:, offset : offset + x.shape[1]])
        offset += x.shape[1]
    results = []
    if expert_own is not None:
        gate_up = [
            jnp.stack([block[:, e * FF : (e + 1) * FF] for e in range(2 * MINE)])
            for block in (expert_own[:, :wide], ends[0])
        ]
        near = [x[:, wide : wide + HALF] for x in (expert_own, expert_other)]
        down = [
            jnp.stack([x[k * 12 : (k + 1) * 12] for x in pair for k in range(2)])
            for pair in (near, ends[-2:])
        ]
        results = [
            by_col(column, gate_up[0][k * MINE : (k + 1) * MINE], gate_up[1][k * MINE : (k + 1) * MINE], 0)
            for k in range(2)
        ] + [by_col(column, *down, 0)]
        results = [x.astype(F32) for x in results]
        ends = ends[1:-2]
    sums = [total((own, x)) for (own, _), x in zip(attention, ends)]
    return (results, [(x[:, :QKV], x[:, QKV:]) for x in sums])


def shards(
    tokens,
    cotangent,
    norm_gains,
    query_weight,
    key_weight,
    value_weight,
    output_weight,
    router_weight,
    gate_weight,
    up_weight,
    down_weight,
    expert_ids,
    seq_lengths,
    seq_owner,
):
    data_index = lax.axis_index("dp")
    row = lax.axis_index("row")
    column = lax.axis_index("col")
    core = data_index % 2
    weights = (
        gate_weight, up_weight, down_weight, query_weight, key_weight, value_weight, output_weight
    )

    squares = jnp.sum(jnp.square(tokens.astype(F32)), axis=1)
    small = jnp.concatenate(
        [
            norm_gains.reshape(2 * LAYERS, HALF).astype(F32),
            router_weight.transpose(0, 2, 1).reshape(LAYERS * EXPERTS, HALF).astype(F32),
            jnp.pad(squares, (0, HALF - 2 * QUARTER))[None],
        ],
        axis=0,
    )
    small_far = over_col(small)
    own, other, qkv_own, out_own, out_send = take_pieces(0, data_index, weights, True)
    small_far, other = tied(small_far, other)
    squares = small[-1, : 2 * QUARTER] + small_far[-1, : 2 * QUARTER]
    inv_rms = lax.rsqrt(squares / D + EPSILON)[:, None]
    normed = (tokens.astype(F32) * inv_rms * small[0]).astype(BF16)
    normed_pair = (normed, over_row(normed))
    piece = whole_piece(own, over_col(other), data_index)
    piece, peer_rows = tied(piece, normed_pair[1])
    gathered_parts = [gather_all(piece)]
    qkv, qkv_far, near = first_product(normed, peer_rows, qkv_own)
    qkv_far = over_col(qkv_far)
    data_index = later(data_index, near)
    seq_lengths, expert_ids = [later(x, near) for x in (seq_lengths, expert_ids)]
    out_sent = over_col(out_send)
    small = jnp.concatenate([small[:-1], small_far[:-1]], axis=1)
    gains = small[: 2 * LAYERS].reshape(LAYERS, 2, D)
    routers = small[2 * LAYERS :].reshape(LAYERS, EXPERTS, D).astype(BF16)
    routers = jnp.pad(routers, ((0, 0), (0, 128 - EXPERTS), (0, 0)))

    segment, position, valid_row, places = segments(seq_lengths, seq_owner, data_index)
    starts = (
        row * 256 + column * QUARTER,
        (1 - row) * 256 + column * QUARTER,
        row * 256 + (1 - column) * QUARTER,
        (1 - row) * 256 + (1 - column) * QUARTER,
    )

    def arranged(x, axis=0):
        return jnp.concatenate(
            [lax.dynamic_slice_in_dim(x, s, QUARTER, axis=axis) for s in starts], axis=axis
        )

    segment, position, places = arranged(segment), arranged(position), arranged(places)
    valid_row = arranged(valid_row.astype(jnp.int32)) > 0
    ids = arranged(expert_ids, 1)
    lanes = jnp.arange(128, dtype=jnp.int32)
    chosen = jnp.any(ids[:, :, :, None] == lanes, axis=2).astype(F32)
    rows = 2 * QUARTER
    frequency = jnp.power(
        ROPE_THETA, jnp.arange(HEAD // 2, dtype=F32) * (-2.0 / HEAD)
    )
    angle = position[:rows].astype(F32)[:, None] * frequency[None, :]
    seen_mask = (
        (segment[:rows, None] == segment[None, :])
        & (places[None, :] <= places[:rows, None])
        & valid_row[:rows, None]
    )
    cosine, sine = jnp.cos(angle), jnp.sin(angle)
    geometry = (
        jnp.concatenate([cosine, cosine], axis=1),
        jnp.concatenate([-sine, sine], axis=1),
        seen_mask.astype(F32),
        valid_row[:rows].astype(F32)[:, None],
    )

    by_core, by_steps = exchange_orders(data_index)
    far = over_col(half_of(tokens, 1 - column, 0))
    upstream = None

    def first_out(pair, pair_far):
        nonlocal far
        pair_far, far = tied(pair_far, far)
        return (pair, pair_far, (out_own, out_sent, over_dp(out_sent, lambda i: i ^ 1)))

    cache, parts = attention_forward(*first_heads(qkv, qkv_far, geometry), geometry, first_out)
    stream = jnp.concatenate([half_of(tokens, column, 0), far], axis=1).astype(F32)
    quarter_rms = half_of(inv_rms, column, 0)
    far_normed = (far.astype(F32) * quarter_rms * gains[0, 0, HALF:]).astype(BF16)
    attention_caches = [(stream, quarter_rms, None) + cache]
    stream = stream + total(parts)

    loaded = []

    def load_second(gathered):
        loaded.extend(take_pieces(1, data_index, weights, False))
        loaded.append(over_col(loaded[1]))
        return gathered

    expert_cache, sends = expert_forward(
        stream, gains[0, 1], routers[0], gathered_parts, chosen[0], load_second, False
    )
    second_piece = whole_piece(loaded[0], loaded[2], data_index)
    share = expert_cache[5]
    second_piece, share = tied(second_piece, share)
    gathered_parts.append(gather_all(second_piece))
    stream = stream + total(send_four(sends))
    caches = [expert_cache[:5] + (share,) + expert_cache[6:]]

    inv_rms, normed = normalize(stream, gains[1, 0])
    query, pair, inputs = make_heads(*gather_two(normed), gathered_parts[0], geometry)
    first_inputs = []

    def start_back(pair, pair_far):
        nonlocal upstream
        pair_far, source, block = tied(pair_far, far_normed, cotangent)
        upstream = to_quarter(block, column)
        first_inputs.append(source)
        first_inputs.append(over_row(source))
        return (pair, pair_far, (gathered_parts[0],))

    cache, parts = attention_forward(query, pair, geometry, start_back)
    attention_caches.append((stream, inv_rms, inputs) + cache)
    inputs = jnp.concatenate([near, jnp.concatenate(first_inputs, axis=0)], axis=1)
    attention_caches[0] = attention_caches[0][:2] + (inputs,) + attention_caches[0][3:]
    stream = stream + total(parts)

    expert_cache, _ = expert_forward(
        stream, gains[1, 1], routers[1], gathered_parts[1:], chosen[1], lambda x: x, True
    )
    caches.append(expert_cache)
    last_hidden = expert_cache[-1]
    gathered = gather_four(upstream)
    expert_parts = gathered_parts
    second_weights, first_weights = gathered_parts

    upstream, finish_second, expert_gain, router_grad = expert_backward(
        upstream.astype(F32),
        caches[1],
        gains[1, 1],
        routers[1],
        expert_parts[1],
        by_core,
        gathered,
        lambda x: x,
    )
    smalls = [None, expert_gain[None], router_grad]
    waiting = None

    expert_sum = None

    def keep(parts, operands, attention_gain):
        nonlocal waiting, expert_sum
        expert_sum, *parts = finish_second(*parts)
        expert_sum = sum_over_cores(expert_sum)
        waiting = operands
        smalls[0] = attention_gain[None]
        return parts

    upstream = attention_backward(
        upstream,
        attention_caches[1],
        gains[1, 0],
        second_weights,
        geometry,
        lambda x: x,
        lambda x: x,
        keep,
    )
    gathered = gather_four(upstream.astype(BF16))
    upstream, finish_first, expert_gain, router_grad = expert_backward(
        upstream,
        caches[0],
        gains[0, 1],
        routers[0],
        expert_parts[0],
        by_core,
        gathered,
        lambda x: x,
    )
    first_sum = None
    last = None

    def finish_sum(out_grads):
        nonlocal first_sum
        first_sum, *out_grads = finish_first(*out_grads)
        return out_grads

    def start_sum(far_pair):
        nonlocal first_sum, expert_sum
        first_sum, expert_sum, far_pair = tied(first_sum, expert_sum, far_pair)
        first_sum = sum_over_cores(first_sum)
        return far_pair

    def keep_last(parts, operands, attention_gain):
        nonlocal last, waiting
        packed = attention_grads(*operands, by_steps[0])
        *packed, own, peer = tied(*packed, *parts)
        values = tied(*packed, *waiting)
        last = [sum_pairs(x)[0] for x in (values[:2], attention_grads(*values[2:], by_steps[1]))]
        smalls[:0] = [attention_gain[None], expert_gain[None], router_grad]
        return (own, peer)

    upstream = attention_backward(
        upstream,
        attention_caches[0],
        gains[0, 0],
        first_weights,
        geometry,
        finish_sum,
        start_sum,
        keep_last,
    )
    small = jnp.concatenate(smalls, axis=0)
    last = sum_round(last, (shift_x, shift_z))
    *last, last_hidden, small, expert_sum = tied(*last, last_hidden, small, expert_sum)
    small = small[:, :HALF] + over_col(small[:, HALF:])
    small = small + over_row(small)
    small = small + over_dp(small, lambda i: i ^ 1)
    along_x, along_z = data_index // 8, data_index // 2 % 4
    small = sum_in_order(sum_in_order(small, shift_x, along_x), shift_z, along_z)
    small = small.reshape(LAYERS, 2 + EXPERTS, HALF)
    sends = last_down(last_hidden, gathered_parts[1])
    block_output = from_quarter((stream + total(send_four(sends))).astype(BF16), column)

    def columns(values):
        return [
            jnp.concatenate(
                [
                    values[:, k * 2 * D : (k + 1) * 2 * D],
                    values[:, (4 + k) * D : (5 + k) * D],
                ],
                axis=1,
            ).astype(BF16)
            for k in range(2)
        ]

    second, _ = place(*columns(expert_sum), [], column)
    last = sum_round(last, (shift_z, shift_x))
    half = QKV + HALF
    first, ((qkv_second, out_second), (qkv_first, out_first)) = place(
        *columns(first_sum), [(x[:, :half], x[:, half:]) for x in last[::-1]], column
    )
    grad_tokens = from_quarter(upstream.astype(BF16), column)

    grad_gains = small[:, :2]
    grad_router = small[:, 2:].transpose(0, 2, 1)

    qkv_grad = jnp.stack([qkv_first, qkv_second])
    out_grad = jnp.stack([out_first, out_second])
    grad_gate, grad_up, grad_down = [jnp.stack([x, y]) for x, y in zip(first, second)]
    width = Q_HEADS * HEAD
    return (
        block_output,
        grad_tokens,
        grad_gains,
        qkv_grad[:, :, :width],
        qkv_grad[:, :, width : width + HEAD],
        qkv_grad[:, :, width + HEAD :],
        out_grad,
        grad_router,
        grad_gate,
        grad_up,
        grad_down,
    )


def solution(mesh):
    in_specs = (
        P(("dp", "row"), "col"),
        P(("dp", "row"), "col"),
        P(None, None, "col"),
        P(None, "col", "row"),
        P(None, "col", "row"),
        P(None, "col", "row"),
        P(None, "row", "col"),
        P(None, "col", None),
        P(None, None, "col", "row"),
        P(None, None, "col", "row"),
        P(None, None, "row", "col"),
        P(None, "dp", None),
        P(),
        P(),
    )
    out_specs = (
        P(("dp", "row"), "col"),
        P(("dp", "row"), "col"),
        P(None, None, "col"),
        P(None, ("col", "dp"), "row"),
        P(None, ("col", "dp"), "row"),
        P(None, ("col", "dp"), "row"),
        P(None, ("row", "dp"), "col"),
        P(None, "col", None),
        P(None, None, ("col", "dp"), "row"),
        P(None, None, ("col", "dp"), "row"),
        P(None, None, ("row", "dp"), "col"),
    )
    return jax.shard_map(shards, mesh=mesh, in_specs=in_specs, out_specs=out_specs, check_vma=False)
```

```python
import jax
import jax.numpy as jnp
import numpy as np
from jax import lax
from jax.experimental import pallas as pl
from jax.experimental.pallas import tpu as pltpu
from jax.sharding import PartitionSpec as P

D = 1536
HALF = D // 2
HEAD = 128
Q_HEADS = 6
EXPERTS = 8
MINE = 4
FF = 384
LAYERS = 2
TOK_DP = 512
QUARTER = 128
EPSILON = 1e-06
ROPE_THETA = 1000000.0
MASKED_SCORE = -1e30
ACROSS = (((1,), (1,)), ((), ()))
DOWNWARD = (((0,), (0,)), ((), ()))
SWAP = [(0, 1), (1, 0)]
DIAGONAL = [(0, 3), (1, 2), (2, 1), (3, 0)]
N_DP = 32
SAME_CORE = [[2 * k + core for k in range(16)] for core in range(2)]
PIECE = 48
CORE_ROWS = 384
QKV = (Q_HEADS + 2) * HEAD
VMEM_LIMIT = 48 << 20
WIDE = 512
STEPS = D // WIDE
PARTS = WIDE // 128
BF16 = jnp.bfloat16
F32 = jnp.float32


def whole(shape):
    return pl.BlockSpec(shape, lambda j: (0,) * len(shape))


BLOCK = (QUARTER, D)
ALL = (TOK_DP, D)
LANES = (TOK_DP, 128)
SLAB = pl.BlockSpec((TOK_DP, WIDE), lambda j: (0, j))


def dot(a, b):
    return jnp.dot(a, b, preferred_element_type=F32)


def dot_across(a, b):
    return lax.dot_general(a, b, ACROSS, preferred_element_type=F32)


def dot_down(a, b):
    return lax.dot_general(a, b, DOWNWARD, preferred_element_type=F32)


def over_row(x):
    return lax.ppermute(x, "row", SWAP)


def over_col(x):
    return lax.ppermute(x, "col", SWAP)


def over_both(x):
    return lax.ppermute(x, ("row", "col"), DIAGONAL)


def over_dp(x, target):
    return lax.ppermute(x, "dp", [(i, target(i)) for i in range(N_DP)])


def by_col(column, own, other, axis):
    return jnp.where(
        column == 0,
        jnp.concatenate([own, other], axis=axis),
        jnp.concatenate([other, own], axis=axis),
    )


def half_of(x, index, axis):
    size = x.shape[axis] // 2
    return lax.dynamic_slice_in_dim(x, index * size, size, axis=axis)


def halves(x):
    return [x[:, :HALF], x[:, HALF:]]


def turned(x):
    return jnp.concatenate([x[:, HALF:], x[:, :HALF]], axis=1)


def tied(*values):
    return lax.optimization_barrier(values)


def none_of(value):
    return value[0, 0].astype(F32) * 0.0


def later(index, value):
    return index + none_of(value).astype(jnp.int32)


def pack(parts):
    return jnp.concatenate([x.astype(BF16) for x in parts], axis=1)


def to_quarter(block, column):
    own = half_of(block, column, 0)
    return jnp.concatenate([own, over_col(half_of(block, 1 - column, 0))], axis=1)


def from_quarter(block, column):
    own, other = halves(block)
    return by_col(column, own, over_col(other), 0)


def gather_four(x):
    other = turned(x)
    return (x, over_row(x), over_col(other), over_both(other))


def total(parts):
    return sum(x.astype(F32) for x in parts)


def gather_two(x):
    return (x, over_row(x))


def segments(seq_lengths, seq_owner, data_index):
    owned_len = jnp.where(seq_owner == data_index, seq_lengths, 0)
    seq_ends = jnp.cumsum(owned_len)
    places = jnp.arange(TOK_DP, dtype=jnp.int32)
    finished = (seq_ends[None, :] <= places[:, None]).astype(jnp.int32)
    segment = jnp.sum(finished, axis=1)
    starts = jnp.sum(finished * owned_len[None, :], axis=1)
    valid_row = places < jnp.sum(owned_len)
    position = jnp.where(valid_row, places - starts, 0)
    return (segment, position, valid_row, places)


def normalize(stream, gain):
    inv_rms = lax.rsqrt(jnp.mean(stream * stream, axis=1, keepdims=True) + EPSILON)
    return (inv_rms, (stream * inv_rms * gain).astype(BF16))


def norm_back(upstream, grad_normed, stream, inv_rms, gain):
    scaled = gain * grad_normed
    dots = jnp.sum(scaled * stream, axis=1, keepdims=True)
    grad_stream = upstream + inv_rms * scaled - stream * (inv_rms * inv_rms * inv_rms * dots / D)
    return grad_stream


def pieces_kernel(layer, place, gate, up, down, query, key, value, out, *rest):
    own, other, *extra, sems = rest
    column = lax.axis_index("col")
    index = place[0]
    start = pl.multiple_of((index % 16) * PIECE, 16)
    down_start = pl.multiple_of((index % 8) * PIECE, 16)
    upper = pl.multiple_of(index % 2 * CORE_ROWS, 128)
    out_start = pl.multiple_of(index // 2 * PIECE, 16)
    heads = ((query, Q_HEADS * HEAD), (key, HEAD), (value, HEAD))
    moves = []
    for side, target in ((column, own), (1 - column, other)):
        for k, weight in enumerate((gate, up)):
            for e in range(MINE):
                moves.append(
                    (
                        weight.at[layer, side * MINE + e, pl.ds(start, PIECE), :],
                        target.at[:, pl.ds((k * MINE + e) * FF, FF)],
                    )
                )
        moves.append(
            (
                down.at[layer, side * MINE + index // 8, pl.ds(down_start, PIECE), :],
                target.at[:, pl.ds(2 * D, HALF)],
            )
        )
        moves.append(
            (
                out.at[1 - layer, pl.ds(out_start, PIECE), pl.ds(upper, CORE_ROWS)],
                target.at[:, pl.ds(2 * D + HALF, CORE_ROWS)],
            )
        )
        offset = 2 * D + HALF + CORE_ROWS
        for weight, size in heads:
            moves.append(
                (weight.at[1 - layer, pl.ds(start, PIECE), :], target.at[:, pl.ds(offset, size)])
            )
            offset += size
    if extra:
        qkv_own, out_own, out_send = extra
        offset = 0
        for weight, size in heads:
            moves.append((weight.at[layer], qkv_own.at[:, pl.ds(offset, size)]))
            offset += size
        moves.append((out.at[layer], out_own))
        moves.append((out.at[layer, pl.ds(upper, CORE_ROWS), :], out_send))
    copies = [pltpu.make_async_copy(a, b, sems.at[i]) for i, (a, b) in enumerate(moves)]
    for copy in copies:
        copy.start()
    for copy in copies:
        copy.wait()


def take_pieces(layer, place, weights, first):
    shapes = [(PIECE, 2 * D + HALF + CORE_ROWS + QKV)] * 2
    if first:
        shapes += [(HALF, QKV), (HALF, HALF), (CORE_ROWS, HALF)]
    anywhere = pl.BlockSpec(memory_space=pltpu.HBM)
    inside = pl.BlockSpec(memory_space=pltpu.VMEM)
    return pl.pallas_call(
        lambda *refs: pieces_kernel(layer, *refs),
        out_shape=[jax.ShapeDtypeStruct(x, BF16) for x in shapes],
        in_specs=[pl.BlockSpec(memory_space=pltpu.SMEM)] + [anywhere] * 7,
        out_specs=[inside] * len(shapes),
        scratch_shapes=[pltpu.SemaphoreType.DMA((31,))],
        compiler_params=pltpu.CompilerParams(vmem_limit_bytes=VMEM_LIMIT),
        name="take_pieces",
    )(place.reshape(1), *weights)


def gather_all(piece):
    return lax.all_gather(piece, "dp", axis=0, tiled=True)


def piece_kernel(place, own, other, packed):
    gate_up = 2 * D
    outs = gate_up + HALF
    qkv = outs + CORE_ROWS
    near = place[0] < 16
    packed[:, :gate_up] = jnp.where(near, own[:, :gate_up], other[:, :gate_up])
    offset = gate_up
    for lower, upper in ((gate_up, outs), (outs, qkv)):
        for x in (own, other):
            packed[:, offset : offset + upper - lower] = x[:, lower:upper]
            offset += upper - lower
    packed[:, offset:] = jnp.where(near, own[:, qkv:], other[:, qkv:])


def whole_piece(own, other, data_index):
    return local_call(
        piece_kernel,
        [((PIECE, 3 * D + HALF + QKV), BF16)],
        [data_index.reshape(1), own, other],
        "whole_piece",
        {0: pl.BlockSpec(memory_space=pltpu.SMEM)},
    )[0]


def first_product_kernel(own, peer, weight, near, away, near_rows):
    column = lax.axis_index("col")
    for k, side in enumerate((column, 1 - column)):
        start = pl.multiple_of(side * QUARTER, QUARTER)
        rows = jnp.concatenate([x[pl.ds(start, QUARTER), :] for x in (own, peer)], axis=0)
        result = dot(rows, weight[...])
        if k == 0:
            near_rows[...] = rows
            near[...] = result
        else:
            away[...] = result.astype(BF16)


def first_product(own, peer, weight):
    return local_call(
        first_product_kernel,
        [((PAIR_ROWS, QKV), F32), ((PAIR_ROWS, QKV), BF16), ((PAIR_ROWS, HALF), BF16)],
        [own, peer, weight],
        "first_product",
    )


OUT_SPEC = pl.BlockSpec((D, HALF), lambda j: (0, 6))
QKV_SPECS = [pl.BlockSpec((D, 256), lambda j, k=k: (0, 21 + k)) for k in range(4)]


def output_weight(gathered, target):
    for k in range(2):
        for row in range(16):
            for side in range(2):
                start = (row * 2 + side) * PIECE
                target[
                    row * PIECE : (row + 1) * PIECE,
                    k * HALF + side * CORE_ROWS : k * HALF + (side + 1) * CORE_ROWS,
                ] = gathered[start : start + PIECE, k * CORE_ROWS : (k + 1) * CORE_ROWS]


def turn(x, cosine, sine):
    return x * cosine + pltpu.roll(x, HEAD // 2, 1) * sine


def write_heads(values, cosine, sine, query, pair):
    for h in range(Q_HEADS + 1):
        target, column = (query, h * HEAD) if h < Q_HEADS else (pair, 0)
        rotated = turn(values[:, h * HEAD : (h + 1) * HEAD], cosine[...], sine[...])
        target[:, column : column + HEAD] = rotated.astype(BF16)
    pair[:, HEAD:] = values[:, (Q_HEADS + 1) * HEAD :].astype(BF16)


def first_heads_kernel(cosine, sine, near, far, query, pair):
    write_heads(near[...] + far[...].astype(F32), cosine, sine, query, pair)


def heads_kernel(cosine, sine, own, peer, *rest):
    *weights, query, pair, inputs = rest
    inputs[:QUARTER, :] = own[...]
    inputs[QUARTER:, :] = peer[...]
    values = jnp.concatenate([dot(inputs[...], w[...]) for w in weights], axis=1)
    write_heads(values, cosine, sine, query, pair)


def local_call(kernel, shapes, operands, name, specs=None, scratch=()):
    outs = [jax.ShapeDtypeStruct(*x) for x in shapes]
    specs = specs or {}
    return pl.pallas_call(
        kernel,
        grid=(1,),
        in_specs=[specs.get(k) or whole(x.shape) for k, x in enumerate(operands)],
        out_specs=[whole(x.shape) for x in outs],
        out_shape=outs,
        scratch_shapes=scratch,
        compiler_params=pltpu.CompilerParams(vmem_limit_bytes=VMEM_LIMIT),
        cost_estimate=pl.CostEstimate(flops=4 << 30, bytes_accessed=8 << 20, transcendentals=1 << 20),
        name=name,
    )(*operands)


PAIR_ROWS = 2 * QUARTER
HEAD_SHAPES = [((PAIR_ROWS, Q_HEADS * HEAD), BF16), ((PAIR_ROWS, 2 * HEAD), BF16)]
OUT_SCRATCH = [pltpu.VMEM((HALF, D), BF16)]


def first_heads(near, far, geometry):
    return local_call(first_heads_kernel, HEAD_SHAPES, [*geometry[:2], near, far], "first_heads")


def make_heads(own, peer, weights, geometry):
    return local_call(
        heads_kernel,
        HEAD_SHAPES + [((PAIR_ROWS, D), BF16)],
        [*geometry[:2], own, peer] + [weights] * 4,
        "make_heads",
        {4 + k: x for k, x in enumerate(QKV_SPECS)},
    )


def keys_values(own, far):
    return [
        jnp.concatenate([x[:, k * HEAD : (k + 1) * HEAD] for x in (own, far)], axis=0)
        for k in range(2)
    ]


def attention_kernel(query, own, far, seen, valid, *rest):
    *side_outs, attended, log_total, near, peer, out_weight = rest
    keys, values = keys_values(own[...], far[...])
    mask = seen[...] > 0.0
    real = valid[...]
    lanes = lax.broadcasted_iota(jnp.int32, (PAIR_ROWS, 128), 1)
    logs = jnp.zeros((PAIR_ROWS, 128), F32)
    for h in range(Q_HEADS):
        columns = slice(h * HEAD, (h + 1) * HEAD)
        scores = dot_across(query[:, columns], keys) * HEAD ** (-0.5)
        scores = jnp.where(mask, scores, MASKED_SCORE)
        top = jnp.where(real > 0.0, jnp.max(scores, axis=1, keepdims=True), 0.0)
        exponent = jnp.where(mask, jnp.exp(scores - top), 0.0)
        denominator = jnp.sum(exponent, axis=1, keepdims=True) + (1.0 - real)
        attended[:, columns] = dot((exponent / denominator).astype(BF16), values).astype(BF16)
        logs = jnp.where(lanes == h, top + jnp.log(denominator), logs)
    log_total[...] = logs
    if len(side_outs) == 1:
        output_weight(side_outs[0], out_weight)
    else:
        out_own, out_first, out_second = side_outs
        straight = lax.axis_index("dp") % 2 == 0
        first, second = out_first[...], out_second[...]
        out_weight[:, :HALF] = out_own[...]
        out_weight[:CORE_ROWS, HALF:] = jnp.where(straight, first, second)
        out_weight[CORE_ROWS:, HALF:] = jnp.where(straight, second, first)
    branch = dot(attended[...], out_weight[...])
    near[...] = branch[:QUARTER]
    peer[...] = branch[QUARTER:].astype(BF16)


def attention_forward(query, pair, geometry, meanwhile):
    _, _, seen, valid = geometry
    far = over_col(pair)
    pair, far, out_parts = meanwhile(pair, far)
    attended, log_total, near, peer = local_call(
        attention_kernel,
        [
            ((PAIR_ROWS, Q_HEADS * HEAD), BF16),
            ((PAIR_ROWS, 128), F32),
            (BLOCK, F32),
            (BLOCK, BF16),
        ],
        [query, pair, far, seen, valid, *out_parts],
        "attention_forward",
        {5: OUT_SPEC} if len(out_parts) == 1 else None,
        OUT_SCRATCH,
    )
    return ((query, pair, far, log_total, attended), (near, over_row(peer)))


def attention_back_kernel(cosine, sine, seen, upstream, peer, gathered, *rest):
    query, own, far, log_total, out_grad, query_grad, pair_own, pair_far, out_weight = rest
    out_grad[:QUARTER, :] = upstream[...]
    out_grad[QUARTER:, :] = peer[...]
    output_weight(gathered, out_weight)
    keys, values = keys_values(own[...], far[...])
    mask = seen[...] > 0.0
    attended_grad = dot_across(out_grad[...], out_weight[...]).astype(BF16)
    key_grad = jnp.zeros((TOK_DP, HEAD), F32)
    value_grad = jnp.zeros((TOK_DP, HEAD), F32)
    for h in range(Q_HEADS):
        columns = slice(h * HEAD, (h + 1) * HEAD)
        head, grad = query[:, columns], attended_grad[:, columns]
        scores = dot_across(head, keys) * HEAD ** (-0.5)
        shift = log_total[:, h : h + 1]
        weights = jnp.where(mask, jnp.exp(scores - shift), 0.0)
        weight_grad = dot_across(grad, values)
        value_grad += dot_down(weights.astype(BF16), grad)
        inner = jnp.sum(weight_grad * weights, axis=1, keepdims=True)
        score_grad = (weights * (weight_grad - inner)).astype(BF16)
        key_grad += dot_down(score_grad, head)
        part = turn(dot(score_grad, keys) * HEAD ** (-0.5), cosine[...], -sine[...])
        query_grad[:, columns] = part.astype(BF16)
    key_grad = key_grad * HEAD ** (-0.5)
    pair_own[:, :HEAD] = key_grad[:PAIR_ROWS]
    pair_own[:, HEAD:] = value_grad[:PAIR_ROWS]
    pair_far[:, :HEAD] = key_grad[PAIR_ROWS:].astype(BF16)
    pair_far[:, HEAD:] = value_grad[PAIR_ROWS:].astype(BF16)


def input_grad_kernel(cosine, sine, query_grad, own, far, inputs, *rest):
    *weights, qkv_grad, near, peer, grad_gain = rest
    pair = own[...] + far[...].astype(F32)
    qkv_grad[:, : Q_HEADS * HEAD] = query_grad[...]
    key_grad = turn(pair[:, :HEAD], cosine[...], -sine[...])
    qkv_grad[:, Q_HEADS * HEAD : QKV - HEAD] = key_grad.astype(BF16)
    qkv_grad[:, QKV - HEAD :] = pair[:, HEAD:].astype(BF16)
    partial = sum(
        dot_across(qkv_grad[:, k * 256 : (k + 1) * 256], w[...]) for k, w in enumerate(weights)
    )
    near[...] = partial[:QUARTER]
    peer[...] = partial[QUARTER:].astype(BF16)
    grad_gain[...] = jnp.sum(inputs[...].astype(F32) * partial, axis=0, keepdims=True)


def attention_grads_kernel(inputs, attended, qkv_grad, out_grad, order, send, keep):
    def product(left, right, column):
        turned_left = dot_across(order[...], left).astype(BF16)
        result = dot(turned_left, right).astype(BF16)
        columns = slice(column, column + result.shape[1])
        send[:, columns] = result[:CORE_ROWS]
        keep[:, columns] = result[CORE_ROWS:]

    for k in range(2):
        half = slice(k * HALF, (k + 1) * HALF)
        product(inputs[:, half], qkv_grad[...], k * (QKV + HALF))
        product(attended[...], out_grad[:, half], k * (QKV + HALF) + QKV)


def attention_grads(*operands):
    return pl.pallas_call(
        attention_grads_kernel,
        out_shape=[jax.ShapeDtypeStruct((CORE_ROWS, 2 * (QKV + HALF)), BF16)] * 2,
        compiler_params=pltpu.CompilerParams(vmem_limit_bytes=VMEM_LIMIT),
        cost_estimate=pl.CostEstimate(
            flops=4 * QUARTER * HALF * 6 * HALF, bytes_accessed=10 << 20, transcendentals=0
        ),
        name="attention_weight_grads",
    )(*operands)


def attention_backward(upstream, cache, gain, weights, geometry, meanwhile, between, finish):
    cosine, sine, seen, _ = geometry
    stream, inv_rms, inputs, query, pair, far, log_total, attended = cache
    out_grads = meanwhile(gather_two(upstream.astype(BF16)))
    width = Q_HEADS * HEAD
    out_grad, query_grad, pair_own, pair_far = local_call(
        attention_back_kernel,
        [
            ((PAIR_ROWS, D), BF16),
            ((PAIR_ROWS, width), BF16),
            ((PAIR_ROWS, 2 * HEAD), F32),
            ((PAIR_ROWS, 2 * HEAD), BF16),
        ],
        [cosine, sine, seen, *out_grads, weights, query, pair, far, log_total],
        "attention_backward",
        {5: OUT_SPEC},
        OUT_SCRATCH,
    )
    qkv_grad, near, peer, grad_gain = local_call(
        input_grad_kernel,
        [((PAIR_ROWS, QKV), BF16), (BLOCK, F32), (BLOCK, BF16), ((1, D), F32)],
        [cosine, sine, query_grad, pair_own, over_col(between(pair_far)), inputs] + [weights] * 4,
        "attention_input_grad",
        {6 + k: x for k, x in enumerate(QKV_SPECS)},
    )
    parts = (near, over_row(peer))
    operands = (inputs, attended, qkv_grad, out_grad)
    parts = finish(parts, operands, grad_gain[0] / gain)
    return norm_back(upstream, total(parts), stream, inv_rms, gain)


def send_blocks(values, own, row, col, both):
    own[...] = values[:QUARTER, :]
    row[...] = values[QUARTER : 2 * QUARTER, :].astype(BF16)
    for k, target in ((2, col), (3, both)):
        block = values[k * QUARTER : (k + 1) * QUARTER, :].astype(BF16)
        target[:, :HALF] = block[:, HALF:]
        target[:, HALF:] = block[:, :HALF]


def join_blocks(blocks, target):
    for k, block in enumerate(blocks):
        target[k * QUARTER : (k + 1) * QUARTER, :] = block[...]


def share_of(share, step, k):
    lanes = lax.broadcasted_iota(jnp.int32, share.shape, 1)
    mine = lanes == lax.axis_index("col") * MINE + (step * PARTS + k) // 3
    return (mine, jnp.sum(jnp.where(mine, share, 0.0), axis=1, keepdims=True))


def forward_kernel(x0, x1, x2, x3, chosen, router, wg, wu, *rest):
    *down, inputs, gate, up, hidden, share = rest[: 6 if len(rest) > 5 else 5]
    sends = rest[6:]
    step = pl.program_id(0)

    @pl.when(step == 0)
    def _():
        join_blocks((x0, x1, x2, x3), inputs)
        logits = dot_across(inputs[...], router[...])
        picked = chosen[...] > 0.0
        top = jnp.max(jnp.where(picked, logits, MASKED_SCORE), axis=1, keepdims=True)
        exponent = jnp.where(picked, jnp.exp(jnp.where(picked, logits - top, 0.0)), 0.0)
        share[...] = exponent / jnp.sum(exponent, axis=1, keepdims=True)

    x = inputs[...]
    gate_value = dot(x, wg[...])
    up_value = dot(x, wu[...])
    gate[...] = gate_value
    up[...] = up_value
    low = (gate_value / (1.0 + jnp.exp(-gate_value))) * up_value
    for k in range(PARTS):
        part = slice(k * 128, (k + 1) * 128)
        hidden[:, part] = (share_of(share[...], step, k)[1] * low[:, part]).astype(BF16)
    if not down:
        return
    *sends, total_ref = sends
    result = dot(hidden[...], down[0][...])

    @pl.when(step == 0)
    def _():
        total_ref[...] = result

    @pl.when(step > 0)
    def _():
        total_ref[...] += result

    @pl.when(step == STEPS - 1)
    def _():
        send_blocks(total_ref[...], *sends)


def weight_specs():
    return [
        pl.BlockSpec((D, WIDE), lambda j: (0, j)),
        pl.BlockSpec((D, WIDE), lambda j: (0, STEPS + j)),
        pl.BlockSpec((WIDE, D), lambda j: (j, 2)),
    ]


COST = pl.CostEstimate(flops=6 * TOK_DP * D * D, bytes_accessed=24 << 20, transcendentals=TOK_DP * D)


def send_four(blocks):
    own, row, col, both = blocks
    return (own, over_row(row), over_col(col), over_both(both))


def expert_forward(stream, gain, router, weights, chosen, meanwhile, last):
    inv_rms, normed = normalize(stream, gain)
    gathered = meanwhile(gather_four(normed))
    weights = weights[0]
    count = 2 if last else 3
    sends = [] if last else [jax.ShapeDtypeStruct(BLOCK, F32)]
    sends = sends + [jax.ShapeDtypeStruct(BLOCK, BF16)] * (3 * len(sends))
    out = pl.pallas_call(
        forward_kernel,
        grid=(STEPS,),
        in_specs=[whole(BLOCK)] * 4 + [whole(LANES), whole((128, D))] + weight_specs()[:count],
        out_specs=[whole(ALL), SLAB, SLAB, SLAB, whole(LANES)] + [whole(BLOCK)] * len(sends),
        out_shape=[
            jax.ShapeDtypeStruct(ALL, BF16),
            jax.ShapeDtypeStruct(ALL, F32),
            jax.ShapeDtypeStruct(ALL, F32),
            jax.ShapeDtypeStruct(ALL, BF16),
            jax.ShapeDtypeStruct(LANES, F32),
        ]
        + sends,
        scratch_shapes=[] if last else [pltpu.VMEM(ALL, F32)],
        compiler_params=pltpu.CompilerParams(vmem_limit_bytes=VMEM_LIMIT),
        cost_estimate=COST,
        name="experts_forward",
    )(*gathered, chosen, router, *[weights] * count)
    inputs, gate, up, hidden, share, *sends = out
    return ((stream, inv_rms, inputs, gate, up, share, hidden), sends)


def last_down_kernel(hidden, weight, own, row, col, both):
    send_blocks(dot(hidden[...], weight[...]), own, row, col, both)


def last_down(hidden, weights):
    return local_call(
        last_down_kernel,
        [(BLOCK, F32)] + [(BLOCK, BF16)] * 3,
        [hidden, weights],
        "last_down",
        {1: pl.BlockSpec((D, D), lambda j: (0, 2))},
    )


def backward_kernel(y0, y1, y2, y3, gate, up, share, router, wg, wu, wd, *rest):
    grads, gate_grad, up_grad, logits_grad, own, row, col, both, total_ref, share_grad = rest
    step = pl.program_id(0)

    @pl.when(step == 0)
    def _():
        join_blocks((y0, y1, y2, y3), grads)
        share_grad[...] = jnp.zeros_like(share_grad)

    hidden_grad = dot_across(grads[...], wd[...])
    gate_value, up_value = gate[...], up[...]
    sigmoid = 1.0 / (1.0 + jnp.exp(-gate_value))
    silu = gate_value * sigmoid
    weighed = hidden_grad * silu * up_value
    slope = hidden_grad * up_value * sigmoid * (1.0 + gate_value * (1.0 - sigmoid))
    through_up = hidden_grad * silu
    for k in range(PARTS):
        part = slice(k * 128, (k + 1) * 128)
        lanes, mine = share_of(share[...], step, k)
        share_grad[...] += jnp.where(
            lanes, jnp.sum(weighed[:, part], axis=1, keepdims=True), 0.0
        )
        gate_grad[:, part] = (mine * slope[:, part]).astype(BF16)
        up_grad[:, part] = (mine * through_up[:, part]).astype(BF16)
    low_gate, low_up = gate_grad[...], up_grad[...]
    result = dot_across(low_gate, wg[...]) + dot_across(low_up, wu[...])

    @pl.when(step == 0)
    def _():
        total_ref[...] = result

    @pl.when(step > 0)
    def _():
        total_ref[...] += result

    @pl.when(step == STEPS - 1)
    def _():
        part = share_grad[...]
        inner = jnp.sum(share[...] * part, axis=1, keepdims=True)
        exact = share[...] * (part - inner)
        high = exact.astype(BF16)
        low = (exact - high.astype(F32)).astype(BF16)
        logits_grad[:, :128] = high
        logits_grad[:, 128:] = low
        through = dot(high, router[...]) + dot(low, router[...])
        send_blocks(total_ref[...] + through, own, row, col, both)


def grads_kernel(inputs, hidden, gate_grad, up_grad, out_grad, order_x, order_h, *rest):
    *arrived, packed, turned_ref = rest
    step = pl.program_id(0)

    for at in range(6):

        @pl.when(step == at)
        def _(at=at):
            if at in (0, 2):
                turned_ref[...] = dot_across(order_x[...], inputs[...]).astype(BF16)
            if at >= 4:
                turned_ref[...] = dot_across(order_h[...], hidden[...]).astype(BF16)
            right = (gate_grad, up_grad, gate_grad, up_grad, out_grad, out_grad)[at]
            result = dot(turned_ref[...], right[...])
            for x in arrived:
                result = result + x[...].astype(F32)
            packed[...] = result.astype(packed.dtype)


def weight_grads(inputs, hidden, gate_grad, up_grad, out_grad, orders, half, arrived):
    def left(place):
        return pl.BlockSpec((TOK_DP, HALF), lambda j: (0, place(j)))

    tile = pl.BlockSpec((CORE_ROWS, D), lambda j: (0, j))
    rows = pl.BlockSpec((CORE_ROWS, HALF), lambda j: (half, 0))
    return pl.pallas_call(
        grads_kernel,
        grid=(6,),
        in_specs=[
            left(lambda j: jnp.minimum(j // 2, 1)),
            left(lambda j: jnp.maximum(j - 4, 0)),
        ]
        + [whole(ALL)] * 3
        + [rows] * 2
        + [tile] * len(arrived),
        out_specs=tile,
        out_shape=jax.ShapeDtypeStruct((CORE_ROWS, 6 * D), F32 if arrived else BF16),
        scratch_shapes=[pltpu.VMEM((CORE_ROWS, TOK_DP), BF16)],
        compiler_params=pltpu.CompilerParams(vmem_limit_bytes=VMEM_LIMIT),
        cost_estimate=pl.CostEstimate(
            flops=4 * TOK_DP * D * D, bytes_accessed=24 << 20, transcendentals=0
        ),
        name="expert_weight_grads",
    )(inputs, hidden, gate_grad, up_grad, out_grad, *orders, *arrived)


def expert_backward(upstream, cache, gain, router, weights, orders, gathered, settle):
    stream, inv_rms, inputs, gate, up, share, hidden = cache
    out = pl.pallas_call(
        backward_kernel,
        grid=(STEPS,),
        in_specs=[whole(BLOCK)] * 4
        + [SLAB, SLAB, whole(LANES), whole((128, D))]
        + weight_specs(),
        out_specs=[whole(ALL), SLAB, SLAB, whole((TOK_DP, 256))] + [whole(BLOCK)] * 4,
        out_shape=[jax.ShapeDtypeStruct(ALL, BF16)] * 3
        + [jax.ShapeDtypeStruct((TOK_DP, 256), BF16), jax.ShapeDtypeStruct(BLOCK, F32)]
        + [jax.ShapeDtypeStruct(BLOCK, BF16)] * 3,
        scratch_shapes=[pltpu.VMEM(ALL, F32), pltpu.VMEM(LANES, F32)],
        compiler_params=pltpu.CompilerParams(vmem_limit_bytes=VMEM_LIMIT),
        cost_estimate=COST,
        name="experts_backward",
    )(*gathered, gate, up, share, router, weights, weights, weights)
    out_grad, gate_grad, up_grad, logits_grad, own, row, col, both = out
    parts = settle(send_four((own, row, col, both)))
    operands = (inputs, hidden, gate_grad, up_grad, out_grad, orders)
    packed = weight_grads(*operands, 0, [])
    own, *parts = parts
    packed, *parts = tied(packed, *parts)
    parts = (own, *parts)
    arrived = over_dp(packed, lambda i: i ^ 1)
    normed_grad = total(parts)
    router_grad = dot_down(logits_grad, inputs)
    router_grad = router_grad[:EXPERTS] + router_grad[128 : 128 + EXPERTS]
    grad_stream = norm_back(upstream, normed_grad, stream, inv_rms, gain)
    grad_gain = jnp.sum(normed_grad * stream * inv_rms, axis=0)


    def finish(*values):
        return tied(weight_grads(*operands, 1, [arrived]), *values)

    return (grad_stream, finish, grad_gain, router_grad)


def exchange_orders(data_index):
    along_x, along_z, core = data_index // 8, data_index // 2 % 4, data_index % 2
    rows = np.arange(HALF, dtype=np.int32)
    block, inner = rows // 24, rows % 24
    side = jnp.where(block < 16, 1 - core, core)
    straight = block % 16 * 2 + side
    target = (along_x + block // 4) % 4 * 8 + (along_z + block) % 4 * 2 + side
    source = jnp.arange(HALF, dtype=jnp.int32)
    target_z = (along_x + block) % 4 * 8 + (along_z + block // 4) % 4 * 2 + side
    by_core, units, x_first, z_first = [
        (x[:, None] == source[None, :]).astype(BF16)
        for x in (
            straight * 24 + inner,
            inner // 12 * FF + straight * 12 + inner % 12,
            target * 24 + inner,
            target_z * 24 + inner,
        )
    ]
    return ([by_core, units], [x_first, z_first])


def shift_x(x, k):
    return over_dp(x, lambda i: (i // 8 + k) % 4 * 8 + i % 8)


def shift_z(x, k):
    return over_dp(x, lambda i: i // 8 * 8 + (i // 2 % 4 + k) % 4 * 2 + i % 2)


def sum_pairs(*sets):
    got = [over_dp(x[0], lambda i: i ^ 1) for x in sets]
    return [total((x[1], y)).astype(BF16) for x, y in zip(sets, got)]


def sum_round(values, shifts):
    rows = values[0].shape[0] // 4
    blocks = [[x[k * rows : (k + 1) * rows] for k in range(4)] for x in values]
    got = [
        [x[0]] + [shift(x[k], k) for k in range(1, 4)] for x, shift in zip(blocks, shifts)
    ]
    return [total(x).astype(BF16) for x in got]


def sum_over_cores(values):
    return lax.psum_scatter(
        values, "dp", scatter_dimension=0, tiled=True, axis_index_groups=SAME_CORE
    )


def sum_in_order(values, shift, place):
    got = jnp.stack([values] + [shift(values, k) for k in range(1, 4)])
    return sum(
        lax.dynamic_index_in_dim(got, (place - j) % 4, 0, keepdims=False) for j in range(4)
    )


def place(expert_own, expert_other, attention, column):
    wide = 2 * D
    far = [expert_other[:, :wide]] if expert_other is not None else []
    far += [other for _, other in attention]
    if expert_own is not None:
        far += [expert_own[:, wide:][:, HALF:], expert_other[:, wide:][:, HALF:]]
    got = over_col(jnp.concatenate(far, axis=1))
    ends, offset = [], 0
    for x in far:
        ends.append(got[:, offset : offset + x.shape[1]])
        offset += x.shape[1]
    results = []
    if expert_own is not None:
        gate_up = [
            jnp.stack([block[:, e * FF : (e + 1) * FF] for e in range(2 * MINE)])
            for block in (expert_own[:, :wide], ends[0])
        ]
        near = [x[:, wide : wide + HALF] for x in (expert_own, expert_other)]
        down = [
            jnp.stack([x[k * 12 : (k + 1) * 12] for x in pair for k in range(2)])
            for pair in (near, ends[-2:])
        ]
        results = [
            by_col(column, gate_up[0][k * MINE : (k + 1) * MINE], gate_up[1][k * MINE : (k + 1) * MINE], 0)
            for k in range(2)
        ] + [by_col(column, *down, 0)]
        results = [x.astype(F32) for x in results]
        ends = ends[1:-2]
    sums = [total((own, x)) for (own, _), x in zip(attention, ends)]
    return (results, [(x[:, :QKV], x[:, QKV:]) for x in sums])


def shards(
    tokens,
    cotangent,
    norm_gains,
    query_weight,
    key_weight,
    value_weight,
    output_weight,
    router_weight,
    gate_weight,
    up_weight,
    down_weight,
    expert_ids,
    seq_lengths,
    seq_owner,
):
    data_index = lax.axis_index("dp")
    row = lax.axis_index("row")
    column = lax.axis_index("col")
    core = data_index % 2
    weights = (
        gate_weight, up_weight, down_weight, query_weight, key_weight, value_weight, output_weight
    )

    squares = jnp.sum(jnp.square(tokens.astype(F32)), axis=1)
    small = jnp.concatenate(
        [
            norm_gains.reshape(2 * LAYERS, HALF).astype(F32),
            router_weight.transpose(0, 2, 1).reshape(LAYERS * EXPERTS, HALF).astype(F32),
            jnp.pad(squares, (0, HALF - 2 * QUARTER))[None],
        ],
        axis=0,
    )
    small_far = over_col(small)
    own, other, qkv_own, out_own, out_send = take_pieces(0, data_index, weights, True)
    small_far, other = tied(small_far, other)
    squares = small[-1, : 2 * QUARTER] + small_far[-1, : 2 * QUARTER]
    inv_rms = lax.rsqrt(squares / D + EPSILON)[:, None]
    normed = (tokens.astype(F32) * inv_rms * small[0]).astype(BF16)
    normed_pair = (normed, over_row(normed))
    piece = whole_piece(own, over_col(other), data_index)
    piece, peer_rows = tied(piece, normed_pair[1])
    gathered_parts = [gather_all(piece)]
    qkv, qkv_far, near = first_product(normed, peer_rows, qkv_own)
    qkv_far = over_col(qkv_far)
    data_index = later(data_index, near)
    seq_lengths, expert_ids = [later(x, near) for x in (seq_lengths, expert_ids)]
    out_sent = over_col(out_send)
    small = jnp.concatenate([small[:-1], small_far[:-1]], axis=1)
    gains = small[: 2 * LAYERS].reshape(LAYERS, 2, D)
    routers = small[2 * LAYERS :].reshape(LAYERS, EXPERTS, D).astype(BF16)
    routers = jnp.pad(routers, ((0, 0), (0, 128 - EXPERTS), (0, 0)))

    segment, position, valid_row, places = segments(seq_lengths, seq_owner, data_index)
    starts = (
        row * 256 + column * QUARTER,
        (1 - row) * 256 + column * QUARTER,
        row * 256 + (1 - column) * QUARTER,
        (1 - row) * 256 + (1 - column) * QUARTER,
    )

    def arranged(x, axis=0):
        return jnp.concatenate(
            [lax.dynamic_slice_in_dim(x, s, QUARTER, axis=axis) for s in starts], axis=axis
        )

    segment, position, places = arranged(segment), arranged(position), arranged(places)
    valid_row = arranged(valid_row.astype(jnp.int32)) > 0
    ids = arranged(expert_ids, 1)
    lanes = jnp.arange(128, dtype=jnp.int32)
    chosen = jnp.any(ids[:, :, :, None] == lanes, axis=2).astype(F32)
    rows = 2 * QUARTER
    frequency = jnp.power(
        ROPE_THETA, jnp.arange(HEAD // 2, dtype=F32) * (-2.0 / HEAD)
    )
    angle = position[:rows].astype(F32)[:, None] * frequency[None, :]
    seen_mask = (
        (segment[:rows, None] == segment[None, :])
        & (places[None, :] <= places[:rows, None])
        & valid_row[:rows, None]
    )
    cosine, sine = jnp.cos(angle), jnp.sin(angle)
    geometry = (
        jnp.concatenate([cosine, cosine], axis=1),
        jnp.concatenate([-sine, sine], axis=1),
        seen_mask.astype(F32),
        valid_row[:rows].astype(F32)[:, None],
    )

    by_core, by_steps = exchange_orders(data_index)
    far = over_col(half_of(tokens, 1 - column, 0))
    upstream = None

    def first_out(pair, pair_far):
        nonlocal far
        pair_far, far = tied(pair_far, far)
        return (pair, pair_far, (out_own, out_sent, over_dp(out_sent, lambda i: i ^ 1)))

    cache, parts = attention_forward(*first_heads(qkv, qkv_far, geometry), geometry, first_out)
    stream = jnp.concatenate([half_of(tokens, column, 0), far], axis=1).astype(F32)
    quarter_rms = half_of(inv_rms, column, 0)
    far_normed = (far.astype(F32) * quarter_rms * gains[0, 0, HALF:]).astype(BF16)
    attention_caches = [(stream, quarter_rms, None) + cache]
    stream = stream + total(parts)

    loaded = []

    def load_second(gathered):
        loaded.extend(take_pieces(1, data_index, weights, False))
        loaded.append(over_col(loaded[1]))
        return gathered

    expert_cache, sends = expert_forward(
        stream, gains[0, 1], routers[0], gathered_parts, chosen[0], load_second, False
    )
    second_piece = whole_piece(loaded[0], loaded[2], data_index)
    share = expert_cache[5]
    second_piece, share = tied(second_piece, share)
    gathered_parts.append(gather_all(second_piece))
    stream = stream + total(send_four(sends))
    caches = [expert_cache[:5] + (share,) + expert_cache[6:]]

    inv_rms, normed = normalize(stream, gains[1, 0])
    query, pair, inputs = make_heads(*gather_two(normed), gathered_parts[0], geometry)
    first_inputs = []

    def start_back(pair, pair_far):
        nonlocal upstream
        pair_far, source, block = tied(pair_far, far_normed, cotangent)
        upstream = to_quarter(block, column)
        first_inputs.append(source)
        first_inputs.append(over_row(source))
        return (pair, pair_far, (gathered_parts[0],))

    cache, parts = attention_forward(query, pair, geometry, start_back)
    attention_caches.append((stream, inv_rms, inputs) + cache)
    inputs = jnp.concatenate([near, jnp.concatenate(first_inputs, axis=0)], axis=1)
    attention_caches[0] = attention_caches[0][:2] + (inputs,) + attention_caches[0][3:]
    stream = stream + total(parts)

    expert_cache, _ = expert_forward(
        stream, gains[1, 1], routers[1], gathered_parts[1:], chosen[1], lambda x: x, True
    )
    caches.append(expert_cache)
    last_hidden = expert_cache[-1]
    gathered = gather_four(upstream)
    expert_parts = gathered_parts
    second_weights, first_weights = gathered_parts

    upstream, finish_second, expert_gain, router_grad = expert_backward(
        upstream.astype(F32),
        caches[1],
        gains[1, 1],
        routers[1],
        expert_parts[1],
        by_core,
        gathered,
        lambda x: x,
    )
    smalls = [None, expert_gain[None], router_grad]
    waiting = None

    expert_sum = None

    def keep(parts, operands, attention_gain):
        nonlocal waiting, expert_sum
        expert_sum, *parts = finish_second(*parts)
        expert_sum = sum_over_cores(expert_sum)
        waiting = operands
        smalls[0] = attention_gain[None]
        return parts

    upstream = attention_backward(
        upstream,
        attention_caches[1],
        gains[1, 0],
        second_weights,
        geometry,
        lambda x: x,
        lambda x: x,
        keep,
    )
    gathered = gather_four(upstream.astype(BF16))
    upstream, finish_first, expert_gain, router_grad = expert_backward(
        upstream,
        caches[0],
        gains[0, 1],
        routers[0],
        expert_parts[0],
        by_core,
        gathered,
        lambda x: x,
    )
    first_sum = None
    last = None

    def finish_sum(out_grads):
        nonlocal first_sum
        first_sum, *out_grads = finish_first(*out_grads)
        return out_grads

    def start_sum(far_pair):
        nonlocal first_sum, expert_sum
        first_sum, expert_sum, far_pair = tied(first_sum, expert_sum, far_pair)
        first_sum = sum_over_cores(first_sum)
        return far_pair

    def keep_last(parts, operands, attention_gain):
        nonlocal last, small
        small = jnp.concatenate([attention_gain[None], expert_gain[None], router_grad] + smalls)
        small = small[:, :HALF] + over_col(small[:, HALF:])
        packed = attention_grads(*operands, by_steps[0])
        small = small + none_of(packed[0])
        after_first = by_steps[1] + none_of(packed[0]).astype(BF16)
        second_packed = attention_grads(*waiting, after_first)
        small = small + over_row(small) + none_of(second_packed[0])
        last = [sum_pairs(x)[0] for x in (packed, second_packed)]
        small = small + over_dp(small, lambda i: i ^ 1)
        return parts

    small = None
    upstream = attention_backward(
        upstream,
        attention_caches[0],
        gains[0, 0],
        first_weights,
        geometry,
        finish_sum,
        start_sum,
        keep_last,
    )
    expert_sum = expert_sum + none_of(last[1])
    last_hidden = last_hidden + none_of(last[1]).astype(BF16)
    last = sum_round(last, (shift_x, shift_z))
    small = small + none_of(last[0]) + none_of(last[1])
    along_x, along_z = data_index // 8, data_index // 2 % 4
    small = sum_in_order(sum_in_order(small, shift_x, along_x), shift_z, along_z)
    small = small.reshape(LAYERS, 2 + EXPERTS, HALF)
    def columns(values):
        return [
            jnp.concatenate(
                [
                    values[:, k * 2 * D : (k + 1) * 2 * D],
                    values[:, (4 + k) * D : (5 + k) * D],
                ],
                axis=1,
            ).astype(BF16)
            for k in range(2)
        ]

    second, _ = place(*columns(expert_sum), [], column)
    sends = send_four(last_down(last_hidden, gathered_parts[1]))
    *last, second[0], far_send = tied(*last, second[0], sends[3])
    last = sum_round(last, (shift_z, shift_x))
    stream = stream + total((*sends[:3], far_send))
    block_output = from_quarter(stream.astype(BF16), column)
    half = QKV + HALF
    first, ((qkv_second, out_second), (qkv_first, out_first)) = place(
        *columns(first_sum), [(x[:, :half], x[:, half:]) for x in last[::-1]], column
    )
    grad_tokens = from_quarter(upstream.astype(BF16), column)

    grad_gains = small[:, :2]
    grad_router = small[:, 2:].transpose(0, 2, 1)

    qkv_grad = jnp.stack([qkv_first, qkv_second])
    out_grad = jnp.stack([out_first, out_second])
    grad_gate, grad_up, grad_down = [jnp.stack([x, y]) for x, y in zip(first, second)]
    width = Q_HEADS * HEAD
    return (
        block_output,
        grad_tokens,
        grad_gains,
        qkv_grad[:, :, :width],
        qkv_grad[:, :, width : width + HEAD],
        qkv_grad[:, :, width + HEAD :],
        out_grad,
        grad_router,
        grad_gate,
        grad_up,
        grad_down,
    )


def solution(mesh):
    in_specs = (
        P(("dp", "row"), "col"),
        P(("dp", "row"), "col"),
        P(None, None, "col"),
        P(None, "col", "row"),
        P(None, "col", "row"),
        P(None, "col", "row"),
        P(None, "row", "col"),
        P(None, "col", None),
        P(None, None, "col", "row"),
        P(None, None, "col", "row"),
        P(None, None, "row", "col"),
        P(None, "dp", None),
        P(),
        P(),
    )
    out_specs = (
        P(("dp", "row"), "col"),
        P(("dp", "row"), "col"),
        P(None, None, "col"),
        P(None, ("col", "dp"), "row"),
        P(None, ("col", "dp"), "row"),
        P(None, ("col", "dp"), "row"),
        P(None, ("row", "dp"), "col"),
        P(None, "col", None),
        P(None, None, ("col", "dp"), "row"),
        P(None, None, ("col", "dp"), "row"),
        P(None, None, ("row", "dp"), "col"),
    )
    return jax.shard_map(shards, mesh=mesh, in_specs=in_specs, out_specs=out_specs, check_vma=False)
```

```python
import jax
import jax.numpy as jnp
import numpy as np
from jax import lax
from jax.experimental import pallas as pl
from jax.experimental.pallas import tpu as pltpu
from jax.sharding import PartitionSpec as P

D = 1536
HALF = D // 2
HEAD = 128
Q_HEADS = 6
EXPERTS = 8
MINE = 4
FF = 384
LAYERS = 2
TOK_DP = 512
QUARTER = 128
EPSILON = 1e-06
ROPE_THETA = 1000000.0
MASKED_SCORE = -1e30
ACROSS = (((1,), (1,)), ((), ()))
DOWNWARD = (((0,), (0,)), ((), ()))
SWAP = [(0, 1), (1, 0)]
DIAGONAL = [(0, 3), (1, 2), (2, 1), (3, 0)]
N_DP = 32
SAME_CORE = [[2 * k + core for k in range(16)] for core in range(2)]
PIECE = 48
CORE_ROWS = 384
QKV = (Q_HEADS + 2) * HEAD
VMEM_LIMIT = 48 << 20
WIDE = 512
STEPS = D // WIDE
PARTS = WIDE // 128
BF16 = jnp.bfloat16
F32 = jnp.float32


def whole(shape):
    return pl.BlockSpec(shape, lambda j: (0,) * len(shape))


BLOCK = (QUARTER, D)
ALL = (TOK_DP, D)
LANES = (TOK_DP, 128)
SLAB = pl.BlockSpec((TOK_DP, WIDE), lambda j: (0, j))


def dot(a, b):
    return jnp.dot(a, b, preferred_element_type=F32)


def dot_across(a, b):
    return lax.dot_general(a, b, ACROSS, preferred_element_type=F32)


def dot_down(a, b):
    return lax.dot_general(a, b, DOWNWARD, preferred_element_type=F32)


def over_row(x):
    return lax.ppermute(x, "row", SWAP)


def over_col(x):
    return lax.ppermute(x, "col", SWAP)


def over_both(x):
    return lax.ppermute(x, ("row", "col"), DIAGONAL)


def over_dp(x, target):
    return lax.ppermute(x, "dp", [(i, target(i)) for i in range(N_DP)])


def by_col(column, own, other, axis):
    return jnp.where(
        column == 0,
        jnp.concatenate([own, other], axis=axis),
        jnp.concatenate([other, own], axis=axis),
    )


def half_of(x, index, axis):
    size = x.shape[axis] // 2
    return lax.dynamic_slice_in_dim(x, index * size, size, axis=axis)


def halves(x):
    return [x[:, :HALF], x[:, HALF:]]


def turned(x):
    return jnp.concatenate([x[:, HALF:], x[:, :HALF]], axis=1)


def tied(*values):
    return lax.optimization_barrier(values)


def none_of(value):
    return value[0, 0].astype(F32) * 0.0


def later(index, value):
    return index + none_of(value).astype(jnp.int32)


def pack(parts):
    return jnp.concatenate([x.astype(BF16) for x in parts], axis=1)


def to_quarter(block, column):
    own = half_of(block, column, 0)
    return jnp.concatenate([own, over_col(half_of(block, 1 - column, 0))], axis=1)


def from_quarter(block, column):
    own, other = halves(block)
    return by_col(column, own, over_col(other), 0)


def gather_four(x):
    other = turned(x)
    return (x, over_row(x), over_col(other), over_both(other))


def total(parts):
    return sum(x.astype(F32) for x in parts)


def gather_two(x):
    return (x, over_row(x))


def segments(seq_lengths, seq_owner, data_index):
    owned_len = jnp.where(seq_owner == data_index, seq_lengths, 0)
    seq_ends = jnp.cumsum(owned_len)
    places = jnp.arange(TOK_DP, dtype=jnp.int32)
    finished = (seq_ends[None, :] <= places[:, None]).astype(jnp.int32)
    segment = jnp.sum(finished, axis=1)
    starts = jnp.sum(finished * owned_len[None, :], axis=1)
    valid_row = places < jnp.sum(owned_len)
    position = jnp.where(valid_row, places - starts, 0)
    return (segment, position, valid_row, places)


def normalize(stream, gain):
    inv_rms = lax.rsqrt(jnp.mean(stream * stream, axis=1, keepdims=True) + EPSILON)
    return (inv_rms, (stream * inv_rms * gain).astype(BF16))


def norm_back(upstream, grad_normed, stream, inv_rms, gain):
    scaled = gain * grad_normed
    dots = jnp.sum(scaled * stream, axis=1, keepdims=True)
    grad_stream = upstream + inv_rms * scaled - stream * (inv_rms * inv_rms * inv_rms * dots / D)
    return grad_stream


def pieces_kernel(layer, place, gate, up, down, query, key, value, out, *rest):
    own, other, *extra, sems = rest
    column = lax.axis_index("col")
    index = place[0]
    start = pl.multiple_of((index % 16) * PIECE, 16)
    down_start = pl.multiple_of((index % 8) * PIECE, 16)
    upper = pl.multiple_of(index % 2 * CORE_ROWS, 128)
    out_start = pl.multiple_of(index // 2 * PIECE, 16)
    heads = ((query, Q_HEADS * HEAD), (key, HEAD), (value, HEAD))
    moves = []
    for side, target in ((column, own), (1 - column, other)):
        for k, weight in enumerate((gate, up)):
            for e in range(MINE):
                moves.append(
                    (
                        weight.at[layer, side * MINE + e, pl.ds(start, PIECE), :],
                        target.at[:, pl.ds((k * MINE + e) * FF, FF)],
                    )
                )
        moves.append(
            (
                down.at[layer, side * MINE + index // 8, pl.ds(down_start, PIECE), :],
                target.at[:, pl.ds(2 * D, HALF)],
            )
        )
        moves.append(
            (
                out.at[1 - layer, pl.ds(out_start, PIECE), pl.ds(upper, CORE_ROWS)],
                target.at[:, pl.ds(2 * D + HALF, CORE_ROWS)],
            )
        )
        offset = 2 * D + HALF + CORE_ROWS
        for weight, size in heads:
            moves.append(
                (weight.at[1 - layer, pl.ds(start, PIECE), :], target.at[:, pl.ds(offset, size)])
            )
            offset += size
    if extra:
        qkv_own, out_own, out_send = extra
        offset = 0
        for weight, size in heads:
            moves.append((weight.at[layer], qkv_own.at[:, pl.ds(offset, size)]))
            offset += size
        moves.append((out.at[layer], out_own))
        moves.append((out.at[layer, pl.ds(upper, CORE_ROWS), :], out_send))
    copies = [pltpu.make_async_copy(a, b, sems.at[i]) for i, (a, b) in enumerate(moves)]
    for copy in copies:
        copy.start()
    for copy in copies:
        copy.wait()


def take_pieces(layer, place, weights, first):
    shapes = [(PIECE, 2 * D + HALF + CORE_ROWS + QKV)] * 2
    if first:
        shapes += [(HALF, QKV), (HALF, HALF), (CORE_ROWS, HALF)]
    anywhere = pl.BlockSpec(memory_space=pltpu.HBM)
    inside = pl.BlockSpec(memory_space=pltpu.VMEM)
    return pl.pallas_call(
        lambda *refs: pieces_kernel(layer, *refs),
        out_shape=[jax.ShapeDtypeStruct(x, BF16) for x in shapes],
        in_specs=[pl.BlockSpec(memory_space=pltpu.SMEM)] + [anywhere] * 7,
        out_specs=[inside] * len(shapes),
        scratch_shapes=[pltpu.SemaphoreType.DMA((31,))],
        compiler_params=pltpu.CompilerParams(vmem_limit_bytes=VMEM_LIMIT),
        name="take_pieces",
    )(place.reshape(1), *weights)


def gather_all(piece):
    return lax.all_gather(piece, "dp", axis=0, tiled=True)


def piece_kernel(place, own, other, packed):
    gate_up = 2 * D
    outs = gate_up + HALF
    qkv = outs + CORE_ROWS
    near = place[0] < 16
    packed[:, :gate_up] = jnp.where(near, own[:, :gate_up], other[:, :gate_up])
    offset = gate_up
    for lower, upper in ((gate_up, outs), (outs, qkv)):
        for x in (own, other):
            packed[:, offset : offset + upper - lower] = x[:, lower:upper]
            offset += upper - lower
    packed[:, offset:] = jnp.where(near, own[:, qkv:], other[:, qkv:])


def whole_piece(own, other, data_index):
    return local_call(
        piece_kernel,
        [((PIECE, 3 * D + HALF + QKV), BF16)],
        [data_index.reshape(1), own, other],
        "whole_piece",
        {0: pl.BlockSpec(memory_space=pltpu.SMEM)},
    )[0]


def first_product_kernel(own, peer, weight, near, away, near_rows):
    column = lax.axis_index("col")
    for k, side in enumerate((column, 1 - column)):
        start = pl.multiple_of(side * QUARTER, QUARTER)
        rows = jnp.concatenate([x[pl.ds(start, QUARTER), :] for x in (own, peer)], axis=0)
        result = dot(rows, weight[...])
        if k == 0:
            near_rows[...] = rows
            near[...] = result
        else:
            away[...] = result.astype(BF16)


def first_product(own, peer, weight):
    return local_call(
        first_product_kernel,
        [((PAIR_ROWS, QKV), F32), ((PAIR_ROWS, QKV), BF16), ((PAIR_ROWS, HALF), BF16)],
        [own, peer, weight],
        "first_product",
    )


OUT_SPEC = pl.BlockSpec((D, HALF), lambda j: (0, 6))
QKV_SPECS = [pl.BlockSpec((D, 256), lambda j, k=k: (0, 21 + k)) for k in range(4)]


def output_weight(gathered, target):
    for k in range(2):
        for row in range(16):
            for side in range(2):
                start = (row * 2 + side) * PIECE
                target[
                    row * PIECE : (row + 1) * PIECE,
                    k * HALF + side * CORE_ROWS : k * HALF + (side + 1) * CORE_ROWS,
                ] = gathered[start : start + PIECE, k * CORE_ROWS : (k + 1) * CORE_ROWS]


def turn(x, cosine, sine):
    return x * cosine + pltpu.roll(x, HEAD // 2, 1) * sine


def write_heads(values, cosine, sine, query, pair):
    for h in range(Q_HEADS + 1):
        target, column = (query, h * HEAD) if h < Q_HEADS else (pair, 0)
        rotated = turn(values[:, h * HEAD : (h + 1) * HEAD], cosine[...], sine[...])
        target[:, column : column + HEAD] = rotated.astype(BF16)
    pair[:, HEAD:] = values[:, (Q_HEADS + 1) * HEAD :].astype(BF16)


def first_heads_kernel(cosine, sine, near, far, query, pair):
    write_heads(near[...] + far[...].astype(F32), cosine, sine, query, pair)


def heads_kernel(cosine, sine, own, peer, *rest):
    *weights, query, pair, inputs = rest
    inputs[:QUARTER, :] = own[...]
    inputs[QUARTER:, :] = peer[...]
    values = jnp.concatenate([dot(inputs[...], w[...]) for w in weights], axis=1)
    write_heads(values, cosine, sine, query, pair)


def local_call(kernel, shapes, operands, name, specs=None, scratch=()):
    outs = [jax.ShapeDtypeStruct(*x) for x in shapes]
    specs = specs or {}
    return pl.pallas_call(
        kernel,
        grid=(1,),
        in_specs=[specs.get(k) or whole(x.shape) for k, x in enumerate(operands)],
        out_specs=[whole(x.shape) for x in outs],
        out_shape=outs,
        scratch_shapes=scratch,
        compiler_params=pltpu.CompilerParams(vmem_limit_bytes=VMEM_LIMIT),
        cost_estimate=pl.CostEstimate(flops=4 << 30, bytes_accessed=8 << 20, transcendentals=1 << 20),
        name=name,
    )(*operands)


PAIR_ROWS = 2 * QUARTER
HEAD_SHAPES = [((PAIR_ROWS, Q_HEADS * HEAD), BF16), ((PAIR_ROWS, 2 * HEAD), BF16)]
OUT_SCRATCH = [pltpu.VMEM((HALF, D), BF16)]


def first_heads(near, far, geometry):
    return local_call(first_heads_kernel, HEAD_SHAPES, [*geometry[:2], near, far], "first_heads")


def make_heads(own, peer, weights, geometry):
    return local_call(
        heads_kernel,
        HEAD_SHAPES + [((PAIR_ROWS, D), BF16)],
        [*geometry[:2], own, peer] + [weights] * 4,
        "make_heads",
        {4 + k: x for k, x in enumerate(QKV_SPECS)},
    )


def keys_values(own, far):
    return [
        jnp.concatenate([x[:, k * HEAD : (k + 1) * HEAD] for x in (own, far)], axis=0)
        for k in range(2)
    ]


def attention_kernel(query, own, far, seen, valid, *rest):
    *side_outs, attended, log_total, near, peer, out_weight = rest
    keys, values = keys_values(own[...], far[...])
    mask = seen[...] > 0.0
    real = valid[...]
    lanes = lax.broadcasted_iota(jnp.int32, (PAIR_ROWS, 128), 1)
    logs = jnp.zeros((PAIR_ROWS, 128), F32)
    for h in range(Q_HEADS):
        columns = slice(h * HEAD, (h + 1) * HEAD)
        scores = dot_across(query[:, columns], keys) * HEAD ** (-0.5)
        scores = jnp.where(mask, scores, MASKED_SCORE)
        top = jnp.where(real > 0.0, jnp.max(scores, axis=1, keepdims=True), 0.0)
        exponent = jnp.where(mask, jnp.exp(scores - top), 0.0)
        denominator = jnp.sum(exponent, axis=1, keepdims=True) + (1.0 - real)
        attended[:, columns] = dot((exponent / denominator).astype(BF16), values).astype(BF16)
        logs = jnp.where(lanes == h, top + jnp.log(denominator), logs)
    log_total[...] = logs
    if len(side_outs) == 1:
        output_weight(side_outs[0], out_weight)
    else:
        out_own, out_first, out_second = side_outs
        straight = lax.axis_index("dp") % 2 == 0
        first, second = out_first[...], out_second[...]
        out_weight[:, :HALF] = out_own[...]
        out_weight[:CORE_ROWS, HALF:] = jnp.where(straight, first, second)
        out_weight[CORE_ROWS:, HALF:] = jnp.where(straight, second, first)
    branch = dot(attended[...], out_weight[...])
    near[...] = branch[:QUARTER]
    peer[...] = branch[QUARTER:].astype(BF16)


def attention_forward(query, pair, geometry, meanwhile):
    _, _, seen, valid = geometry
    far = over_col(pair)
    pair, far, out_parts = meanwhile(pair, far)
    attended, log_total, near, peer = local_call(
        attention_kernel,
        [
            ((PAIR_ROWS, Q_HEADS * HEAD), BF16),
            ((PAIR_ROWS, 128), F32),
            (BLOCK, F32),
            (BLOCK, BF16),
        ],
        [query, pair, far, seen, valid, *out_parts],
        "attention_forward",
        {5: OUT_SPEC} if len(out_parts) == 1 else None,
        OUT_SCRATCH,
    )
    return ((query, pair, far, log_total, attended), (near, over_row(peer)))


def attention_back_kernel(cosine, sine, seen, upstream, peer, gathered, *rest):
    query, own, far, log_total, out_grad, query_grad, pair_own, pair_far, out_weight = rest
    out_grad[:QUARTER, :] = upstream[...]
    out_grad[QUARTER:, :] = peer[...]
    output_weight(gathered, out_weight)
    keys, values = keys_values(own[...], far[...])
    mask = seen[...] > 0.0
    attended_grad = dot_across(out_grad[...], out_weight[...]).astype(BF16)
    key_grad = jnp.zeros((TOK_DP, HEAD), F32)
    value_grad = jnp.zeros((TOK_DP, HEAD), F32)
    for h in range(Q_HEADS):
        columns = slice(h * HEAD, (h + 1) * HEAD)
        head, grad = query[:, columns], attended_grad[:, columns]
        scores = dot_across(head, keys) * HEAD ** (-0.5)
        shift = log_total[:, h : h + 1]
        weights = jnp.where(mask, jnp.exp(scores - shift), 0.0)
        weight_grad = dot_across(grad, values)
        value_grad += dot_down(weights.astype(BF16), grad)
        inner = jnp.sum(weight_grad * weights, axis=1, keepdims=True)
        score_grad = (weights * (weight_grad - inner)).astype(BF16)
        key_grad += dot_down(score_grad, head)
        part = turn(dot(score_grad, keys) * HEAD ** (-0.5), cosine[...], -sine[...])
        query_grad[:, columns] = part.astype(BF16)
    key_grad = key_grad * HEAD ** (-0.5)
    pair_own[:, :HEAD] = key_grad[:PAIR_ROWS]
    pair_own[:, HEAD:] = value_grad[:PAIR_ROWS]
    pair_far[:, :HEAD] = key_grad[PAIR_ROWS:].astype(BF16)
    pair_far[:, HEAD:] = value_grad[PAIR_ROWS:].astype(BF16)


def input_grad_kernel(cosine, sine, query_grad, own, far, inputs, *rest):
    *weights, qkv_grad, near, peer, grad_gain = rest
    pair = own[...] + far[...].astype(F32)
    qkv_grad[:, : Q_HEADS * HEAD] = query_grad[...]
    key_grad = turn(pair[:, :HEAD], cosine[...], -sine[...])
    qkv_grad[:, Q_HEADS * HEAD : QKV - HEAD] = key_grad.astype(BF16)
    qkv_grad[:, QKV - HEAD :] = pair[:, HEAD:].astype(BF16)
    partial = sum(
        dot_across(qkv_grad[:, k * 256 : (k + 1) * 256], w[...]) for k, w in enumerate(weights)
    )
    near[...] = partial[:QUARTER]
    peer[...] = partial[QUARTER:].astype(BF16)
    grad_gain[...] = jnp.sum(inputs[...].astype(F32) * partial, axis=0, keepdims=True)


def attention_grads_kernel(inputs, attended, qkv_grad, out_grad, order, send, keep):
    def product(left, right, column):
        turned_left = dot_across(order[...], left).astype(BF16)
        result = dot(turned_left, right).astype(BF16)
        columns = slice(column, column + result.shape[1])
        send[:, columns] = result[:CORE_ROWS]
        keep[:, columns] = result[CORE_ROWS:]

    for k in range(2):
        half = slice(k * HALF, (k + 1) * HALF)
        product(inputs[:, half], qkv_grad[...], k * (QKV + HALF))
        product(attended[...], out_grad[:, half], k * (QKV + HALF) + QKV)


def attention_grads(*operands):
    return pl.pallas_call(
        attention_grads_kernel,
        out_shape=[jax.ShapeDtypeStruct((CORE_ROWS, 2 * (QKV + HALF)), BF16)] * 2,
        compiler_params=pltpu.CompilerParams(vmem_limit_bytes=VMEM_LIMIT),
        cost_estimate=pl.CostEstimate(
            flops=4 * QUARTER * HALF * 6 * HALF, bytes_accessed=10 << 20, transcendentals=0
        ),
        name="attention_weight_grads",
    )(*operands)


def attention_backward(upstream, cache, gain, weights, geometry, meanwhile, between, finish):
    cosine, sine, seen, _ = geometry
    stream, inv_rms, inputs, query, pair, far, log_total, attended = cache
    out_grads = meanwhile(gather_two(upstream.astype(BF16)))
    width = Q_HEADS * HEAD
    out_grad, query_grad, pair_own, pair_far = local_call(
        attention_back_kernel,
        [
            ((PAIR_ROWS, D), BF16),
            ((PAIR_ROWS, width), BF16),
            ((PAIR_ROWS, 2 * HEAD), F32),
            ((PAIR_ROWS, 2 * HEAD), BF16),
        ],
        [cosine, sine, seen, *out_grads, weights, query, pair, far, log_total],
        "attention_backward",
        {5: OUT_SPEC},
        OUT_SCRATCH,
    )
    qkv_grad, near, peer, grad_gain = local_call(
        input_grad_kernel,
        [((PAIR_ROWS, QKV), BF16), (BLOCK, F32), (BLOCK, BF16), ((1, D), F32)],
        [cosine, sine, query_grad, pair_own, over_col(between(pair_far)), inputs] + [weights] * 4,
        "attention_input_grad",
        {6 + k: x for k, x in enumerate(QKV_SPECS)},
    )
    parts = (near, over_row(peer))
    operands = (inputs, attended, qkv_grad, out_grad)
    parts = finish(parts, operands, grad_gain[0] / gain)
    return norm_back(upstream, total(parts), stream, inv_rms, gain)


def send_blocks(values, own, row, col, both):
    own[...] = values[:QUARTER, :]
    row[...] = values[QUARTER : 2 * QUARTER, :].astype(BF16)
    for k, target in ((2, col), (3, both)):
        block = values[k * QUARTER : (k + 1) * QUARTER, :].astype(BF16)
        target[:, :HALF] = block[:, HALF:]
        target[:, HALF:] = block[:, :HALF]


def fetch(pairs, sems):
    copies = [pltpu.make_async_copy(x, y, sems.at[k]) for k, (x, y) in enumerate(pairs)]
    for copy in copies:
        copy.start()
    for copy in copies:
        copy.wait()


def row_blocks(blocks, target):
    return [
        (block, target.at[pl.ds(k * QUARTER, QUARTER), :]) for k, block in enumerate(blocks)
    ]


def share_of(share, step, k):
    lanes = lax.broadcasted_iota(jnp.int32, share.shape, 1)
    mine = lanes == lax.axis_index("col") * MINE + (step * PARTS + k) // 3
    return (mine, jnp.sum(jnp.where(mine, share, 0.0), axis=1, keepdims=True))


def forward_kernel(x0, x1, x2, x3, mask_ref, router_ref, wg, wu, *rest):
    *rest, chosen, router, sems = rest
    *down, inputs, gate, up, hidden, share = rest[: 6 if len(rest) > 5 else 5]
    sends = rest[6:]
    step = pl.program_id(0)

    @pl.when(step == 0)
    def _():
        blocks = row_blocks((x0, x1, x2, x3), inputs)
        fetch(blocks + [(mask_ref, chosen), (router_ref, router)], sems)
        logits = dot_across(inputs[...], router[...])
        picked = chosen[...] > 0.0
        top = jnp.max(jnp.where(picked, logits, MASKED_SCORE), axis=1, keepdims=True)
        exponent = jnp.where(picked, jnp.exp(jnp.where(picked, logits - top, 0.0)), 0.0)
        share[...] = exponent / jnp.sum(exponent, axis=1, keepdims=True)

    x = inputs[...]
    gate_value = dot(x, wg[...])
    up_value = dot(x, wu[...])
    gate[...] = gate_value
    up[...] = up_value
    low = (gate_value / (1.0 + jnp.exp(-gate_value))) * up_value
    for k in range(PARTS):
        part = slice(k * 128, (k + 1) * 128)
        hidden[:, part] = (share_of(share[...], step, k)[1] * low[:, part]).astype(BF16)
    if not down:
        return
    *sends, total_ref = sends
    result = dot(hidden[...], down[0][...])

    @pl.when(step == 0)
    def _():
        total_ref[...] = result

    @pl.when(step > 0)
    def _():
        total_ref[...] += result

    @pl.when(step == STEPS - 1)
    def _():
        send_blocks(total_ref[...], *sends)


FAR = pl.BlockSpec(memory_space=pltpu.HBM)


def weight_specs():
    return [
        pl.BlockSpec((D, WIDE), lambda j: (0, j)),
        pl.BlockSpec((D, WIDE), lambda j: (0, STEPS + j)),
        pl.BlockSpec((WIDE, D), lambda j: (j, 2)),
    ]


COST = pl.CostEstimate(flops=6 * TOK_DP * D * D, bytes_accessed=24 << 20, transcendentals=TOK_DP * D)


def send_four(blocks):
    own, row, col, both = blocks
    return (own, over_row(row), over_col(col), over_both(both))


def expert_forward(stream, gain, router, weights, chosen, meanwhile, last):
    inv_rms, normed = normalize(stream, gain)
    gathered = meanwhile(gather_four(normed))
    weights = weights[0]
    count = 2 if last else 3
    sends = [] if last else [jax.ShapeDtypeStruct(BLOCK, F32)]
    sends = sends + [jax.ShapeDtypeStruct(BLOCK, BF16)] * (3 * len(sends))
    out = pl.pallas_call(
        forward_kernel,
        grid=(STEPS,),
        in_specs=[FAR] * 6 + weight_specs()[:count],
        out_specs=[whole(ALL), SLAB, SLAB, SLAB, whole(LANES)] + [whole(BLOCK)] * len(sends),
        out_shape=[
            jax.ShapeDtypeStruct(ALL, BF16),
            jax.ShapeDtypeStruct(ALL, F32),
            jax.ShapeDtypeStruct(ALL, F32),
            jax.ShapeDtypeStruct(ALL, BF16),
            jax.ShapeDtypeStruct(LANES, F32),
        ]
        + sends,
        scratch_shapes=([] if last else [pltpu.VMEM(ALL, F32)])
        + [pltpu.VMEM(LANES, F32), pltpu.VMEM((128, D), BF16), pltpu.SemaphoreType.DMA((6,))],
        compiler_params=pltpu.CompilerParams(vmem_limit_bytes=VMEM_LIMIT),
        cost_estimate=COST,
        name="experts_forward",
    )(*gathered, chosen, router, *[weights] * count)
    inputs, gate, up, hidden, share, *sends = out
    return ((stream, inv_rms, inputs, gate, up, share, hidden), sends)


def last_down_kernel(hidden, weight, own, row, col, both):
    send_blocks(dot(hidden[...], weight[...]), own, row, col, both)


def last_down(hidden, weights):
    return local_call(
        last_down_kernel,
        [(BLOCK, F32)] + [(BLOCK, BF16)] * 3,
        [hidden, weights],
        "last_down",
        {1: pl.BlockSpec((D, D), lambda j: (0, 2))},
    )


def backward_kernel(y0, y1, y2, y3, gate, up, share, router, wg, wu, wd, *rest):
    grads, gate_grad, up_grad, logits_grad, own, row, col, both, total_ref, share_grad, sems = rest
    step = pl.program_id(0)

    @pl.when(step == 0)
    def _():
        fetch(row_blocks((y0, y1, y2, y3), grads), sems)
        share_grad[...] = jnp.zeros_like(share_grad)

    hidden_grad = dot_across(grads[...], wd[...])
    gate_value, up_value = gate[...], up[...]
    sigmoid = 1.0 / (1.0 + jnp.exp(-gate_value))
    silu = gate_value * sigmoid
    weighed = hidden_grad * silu * up_value
    slope = hidden_grad * up_value * sigmoid * (1.0 + gate_value * (1.0 - sigmoid))
    through_up = hidden_grad * silu
    for k in range(PARTS):
        part = slice(k * 128, (k + 1) * 128)
        lanes, mine = share_of(share[...], step, k)
        share_grad[...] += jnp.where(
            lanes, jnp.sum(weighed[:, part], axis=1, keepdims=True), 0.0
        )
        gate_grad[:, part] = (mine * slope[:, part]).astype(BF16)
        up_grad[:, part] = (mine * through_up[:, part]).astype(BF16)
    low_gate, low_up = gate_grad[...], up_grad[...]
    result = dot_across(low_gate, wg[...]) + dot_across(low_up, wu[...])

    @pl.when(step == 0)
    def _():
        total_ref[...] = result

    @pl.when(step > 0)
    def _():
        total_ref[...] += result

    @pl.when(step == STEPS - 1)
    def _():
        part = share_grad[...]
        inner = jnp.sum(share[...] * part, axis=1, keepdims=True)
        exact = share[...] * (part - inner)
        high = exact.astype(BF16)
        low = (exact - high.astype(F32)).astype(BF16)
        logits_grad[:, :128] = high
        logits_grad[:, 128:] = low
        through = dot(high, router[...]) + dot(low, router[...])
        send_blocks(total_ref[...] + through, own, row, col, both)


def grads_kernel(inputs, hidden, gate_grad, up_grad, out_grad, order_x, order_h, *rest):
    *arrived, packed, turned_ref = rest
    step = pl.program_id(0)

    for at in range(6):

        @pl.when(step == at)
        def _(at=at):
            if at in (0, 2):
                turned_ref[...] = dot_across(order_x[...], inputs[...]).astype(BF16)
            if at >= 4:
                turned_ref[...] = dot_across(order_h[...], hidden[...]).astype(BF16)
            right = (gate_grad, up_grad, gate_grad, up_grad, out_grad, out_grad)[at]
            result = dot(turned_ref[...], right[...])
            for x in arrived:
                result = result + x[...].astype(F32)
            packed[...] = result.astype(packed.dtype)


def weight_grads(inputs, hidden, gate_grad, up_grad, out_grad, orders, half, arrived):
    def left(place):
        return pl.BlockSpec((TOK_DP, HALF), lambda j: (0, place(j)))

    tile = pl.BlockSpec((CORE_ROWS, D), lambda j: (0, j))
    rows = pl.BlockSpec((CORE_ROWS, HALF), lambda j: (half, 0))
    return pl.pallas_call(
        grads_kernel,
        grid=(6,),
        in_specs=[
            left(lambda j: jnp.minimum(j // 2, 1)),
            left(lambda j: jnp.maximum(j - 4, 0)),
        ]
        + [whole(ALL)] * 3
        + [rows] * 2
        + [tile] * len(arrived),
        out_specs=tile,
        out_shape=jax.ShapeDtypeStruct((CORE_ROWS, 6 * D), F32 if arrived else BF16),
        scratch_shapes=[pltpu.VMEM((CORE_ROWS, TOK_DP), BF16)],
        compiler_params=pltpu.CompilerParams(vmem_limit_bytes=VMEM_LIMIT),
        cost_estimate=pl.CostEstimate(
            flops=4 * TOK_DP * D * D, bytes_accessed=24 << 20, transcendentals=0
        ),
        name="expert_weight_grads",
    )(inputs, hidden, gate_grad, up_grad, out_grad, *orders, *arrived)


def expert_backward(upstream, cache, gain, router, weights, orders, gathered, settle):
    stream, inv_rms, inputs, gate, up, share, hidden = cache
    out = pl.pallas_call(
        backward_kernel,
        grid=(STEPS,),
        in_specs=[FAR] * 4
        + [SLAB, SLAB, whole(LANES), whole((128, D))]
        + weight_specs(),
        out_specs=[whole(ALL), SLAB, SLAB, whole((TOK_DP, 256))] + [whole(BLOCK)] * 4,
        out_shape=[jax.ShapeDtypeStruct(ALL, BF16)] * 3
        + [jax.ShapeDtypeStruct((TOK_DP, 256), BF16), jax.ShapeDtypeStruct(BLOCK, F32)]
        + [jax.ShapeDtypeStruct(BLOCK, BF16)] * 3,
        scratch_shapes=[
            pltpu.VMEM(ALL, F32),
            pltpu.VMEM(LANES, F32),
            pltpu.SemaphoreType.DMA((4,)),
        ],
        compiler_params=pltpu.CompilerParams(vmem_limit_bytes=VMEM_LIMIT),
        cost_estimate=COST,
        name="experts_backward",
    )(*gathered, gate, up, share, router, weights, weights, weights)
    out_grad, gate_grad, up_grad, logits_grad, own, row, col, both = out
    parts = settle(send_four((own, row, col, both)))
    operands = (inputs, hidden, gate_grad, up_grad, out_grad, orders)
    packed = weight_grads(*operands, 0, [])
    own, *parts = parts
    packed, *parts = tied(packed, *parts)
    parts = (own, *parts)
    arrived = over_dp(packed, lambda i: i ^ 1)
    normed_grad = total(parts)
    router_grad = dot_down(logits_grad, inputs)
    router_grad = router_grad[:EXPERTS] + router_grad[128 : 128 + EXPERTS]
    grad_stream = norm_back(upstream, normed_grad, stream, inv_rms, gain)
    grad_gain = jnp.sum(normed_grad * stream * inv_rms, axis=0)


    def finish(*values):
        return tied(weight_grads(*operands, 1, [arrived]), *values)

    return (grad_stream, finish, grad_gain, router_grad)


def exchange_orders(data_index):
    along_x, along_z, core = data_index // 8, data_index // 2 % 4, data_index % 2
    rows = np.arange(HALF, dtype=np.int32)
    block, inner = rows // 24, rows % 24
    side = jnp.where(block < 16, 1 - core, core)
    straight = block % 16 * 2 + side
    target = (along_x + block // 4) % 4 * 8 + (along_z + block) % 4 * 2 + side
    source = jnp.arange(HALF, dtype=jnp.int32)
    target_z = (along_x + block) % 4 * 8 + (along_z + block // 4) % 4 * 2 + side
    by_core, units, x_first, z_first = [
        (x[:, None] == source[None, :]).astype(BF16)
        for x in (
            straight * 24 + inner,
            inner // 12 * FF + straight * 12 + inner % 12,
            target * 24 + inner,
            target_z * 24 + inner,
        )
    ]
    return ([by_core, units], [x_first, z_first])


def shift_x(x, k):
    return over_dp(x, lambda i: (i // 8 + k) % 4 * 8 + i % 8)


def shift_z(x, k):
    return over_dp(x, lambda i: i // 8 * 8 + (i // 2 % 4 + k) % 4 * 2 + i % 2)


def sum_pairs(*sets):
    got = [over_dp(x[0], lambda i: i ^ 1) for x in sets]
    return [total((x[1], y)).astype(BF16) for x, y in zip(sets, got)]


def sum_round(values, shifts):
    rows = values[0].shape[0] // 4
    blocks = [[x[k * rows : (k + 1) * rows] for k in range(4)] for x in values]
    got = [
        [x[0]] + [shift(x[k], k) for k in range(1, 4)] for x, shift in zip(blocks, shifts)
    ]
    return [total(x).astype(BF16) for x in got]


def sum_over_cores(values):
    return lax.psum_scatter(
        values, "dp", scatter_dimension=0, tiled=True, axis_index_groups=SAME_CORE
    )


def sum_in_order(values, shift, place):
    got = jnp.stack([values] + [shift(values, k) for k in range(1, 4)])
    return sum(
        lax.dynamic_index_in_dim(got, (place - j) % 4, 0, keepdims=False) for j in range(4)
    )


def place(expert_own, expert_other, attention, column):
    wide = 2 * D
    far = [expert_other[:, :wide]] if expert_other is not None else []
    far += [other for _, other in attention]
    if expert_own is not None:
        far += [expert_own[:, wide:][:, HALF:], expert_other[:, wide:][:, HALF:]]
    got = over_col(jnp.concatenate(far, axis=1))
    ends, offset = [], 0
    for x in far:
        ends.append(got[:, offset : offset + x.shape[1]])
        offset += x.shape[1]
    results = []
    if expert_own is not None:
        gate_up = [
            jnp.stack([block[:, e * FF : (e + 1) * FF] for e in range(2 * MINE)])
            for block in (expert_own[:, :wide], ends[0])
        ]
        near = [x[:, wide : wide + HALF] for x in (expert_own, expert_other)]
        down = [
            jnp.stack([x[k * 12 : (k + 1) * 12] for x in pair for k in range(2)])
            for pair in (near, ends[-2:])
        ]
        results = [
            by_col(column, gate_up[0][k * MINE : (k + 1) * MINE], gate_up[1][k * MINE : (k + 1) * MINE], 0)
            for k in range(2)
        ] + [by_col(column, *down, 0)]
        results = [x.astype(F32) for x in results]
        ends = ends[1:-2]
    sums = [total((own, x)) for (own, _), x in zip(attention, ends)]
    return (results, [(x[:, :QKV], x[:, QKV:]) for x in sums])


def shards(
    tokens,
    cotangent,
    norm_gains,
    query_weight,
    key_weight,
    value_weight,
    output_weight,
    router_weight,
    gate_weight,
    up_weight,
    down_weight,
    expert_ids,
    seq_lengths,
    seq_owner,
):
    data_index = lax.axis_index("dp")
    row = lax.axis_index("row")
    column = lax.axis_index("col")
    core = data_index % 2
    weights = (
        gate_weight, up_weight, down_weight, query_weight, key_weight, value_weight, output_weight
    )

    squares = jnp.sum(jnp.square(tokens.astype(F32)), axis=1)
    small = jnp.concatenate(
        [
            norm_gains.reshape(2 * LAYERS, HALF).astype(F32),
            router_weight.transpose(0, 2, 1).reshape(LAYERS * EXPERTS, HALF).astype(F32),
            jnp.pad(squares, (0, HALF - 2 * QUARTER))[None],
        ],
        axis=0,
    )
    small_far = over_col(small)
    own, other, qkv_own, out_own, out_send = take_pieces(0, data_index, weights, True)
    small_far, other = tied(small_far, other)
    squares = small[-1, : 2 * QUARTER] + small_far[-1, : 2 * QUARTER]
    inv_rms = lax.rsqrt(squares / D + EPSILON)[:, None]
    normed = (tokens.astype(F32) * inv_rms * small[0]).astype(BF16)
    normed_pair = (normed, over_row(normed))
    piece = whole_piece(own, over_col(other), data_index)
    piece, peer_rows = tied(piece, normed_pair[1])
    gathered_parts = [gather_all(piece)]
    qkv, qkv_far, near = first_product(normed, peer_rows, qkv_own)
    qkv_far = over_col(qkv_far)
    data_index = later(data_index, near)
    seq_lengths, expert_ids = [later(x, near) for x in (seq_lengths, expert_ids)]
    out_sent = over_col(out_send)
    small = jnp.concatenate([small[:-1], small_far[:-1]], axis=1)
    gains = small[: 2 * LAYERS].reshape(LAYERS, 2, D)
    routers = small[2 * LAYERS :].reshape(LAYERS, EXPERTS, D).astype(BF16)
    routers = jnp.pad(routers, ((0, 0), (0, 128 - EXPERTS), (0, 0)))

    segment, position, valid_row, places = segments(seq_lengths, seq_owner, data_index)
    starts = (
        row * 256 + column * QUARTER,
        (1 - row) * 256 + column * QUARTER,
        row * 256 + (1 - column) * QUARTER,
        (1 - row) * 256 + (1 - column) * QUARTER,
    )

    def arranged(x, axis=0):
        return jnp.concatenate(
            [lax.dynamic_slice_in_dim(x, s, QUARTER, axis=axis) for s in starts], axis=axis
        )

    segment, position, places = arranged(segment), arranged(position), arranged(places)
    valid_row = arranged(valid_row.astype(jnp.int32)) > 0
    ids = arranged(expert_ids, 1)
    lanes = jnp.arange(128, dtype=jnp.int32)
    chosen = jnp.any(ids[:, :, :, None] == lanes, axis=2).astype(F32)
    rows = 2 * QUARTER
    frequency = jnp.power(
        ROPE_THETA, jnp.arange(HEAD // 2, dtype=F32) * (-2.0 / HEAD)
    )
    angle = position[:rows].astype(F32)[:, None] * frequency[None, :]
    seen_mask = (
        (segment[:rows, None] == segment[None, :])
        & (places[None, :] <= places[:rows, None])
        & valid_row[:rows, None]
    )
    cosine, sine = jnp.cos(angle), jnp.sin(angle)
    geometry = (
        jnp.concatenate([cosine, cosine], axis=1),
        jnp.concatenate([-sine, sine], axis=1),
        seen_mask.astype(F32),
        valid_row[:rows].astype(F32)[:, None],
    )

    by_core, by_steps = exchange_orders(data_index)
    far = over_col(half_of(tokens, 1 - column, 0))
    upstream = None

    def first_out(pair, pair_far):
        nonlocal far
        pair_far, far = tied(pair_far, far)
        return (pair, pair_far, (out_own, out_sent, over_dp(out_sent, lambda i: i ^ 1)))

    cache, parts = attention_forward(*first_heads(qkv, qkv_far, geometry), geometry, first_out)
    stream = jnp.concatenate([half_of(tokens, column, 0), far], axis=1).astype(F32)
    quarter_rms = half_of(inv_rms, column, 0)
    far_normed = (far.astype(F32) * quarter_rms * gains[0, 0, HALF:]).astype(BF16)
    attention_caches = [(stream, quarter_rms, None) + cache]
    stream = stream + total(parts)

    loaded = []

    def load_second(gathered):
        loaded.extend(take_pieces(1, data_index, weights, False))
        loaded.append(over_col(loaded[1]))
        return gathered

    expert_cache, sends = expert_forward(
        stream, gains[0, 1], routers[0], gathered_parts, chosen[0], load_second, False
    )
    second_piece = whole_piece(loaded[0], loaded[2], data_index)
    share = expert_cache[5]
    second_piece, share = tied(second_piece, share)
    gathered_parts.append(gather_all(second_piece))
    stream = stream + total(send_four(sends))
    caches = [expert_cache[:5] + (share,) + expert_cache[6:]]

    inv_rms, normed = normalize(stream, gains[1, 0])
    query, pair, inputs = make_heads(*gather_two(normed), gathered_parts[0], geometry)
    first_inputs = []

    def start_back(pair, pair_far):
        nonlocal upstream
        pair_far, source, block = tied(pair_far, far_normed, cotangent)
        upstream = to_quarter(block, column)
        first_inputs.append(source)
        first_inputs.append(over_row(source))
        return (pair, pair_far, (gathered_parts[0],))

    cache, parts = attention_forward(query, pair, geometry, start_back)
    attention_caches.append((stream, inv_rms, inputs) + cache)
    inputs = jnp.concatenate([near, jnp.concatenate(first_inputs, axis=0)], axis=1)
    attention_caches[0] = attention_caches[0][:2] + (inputs,) + attention_caches[0][3:]
    stream = stream + total(parts)

    expert_cache, _ = expert_forward(
        stream, gains[1, 1], routers[1], gathered_parts[1:], chosen[1], lambda x: x, True
    )
    caches.append(expert_cache)
    last_hidden = expert_cache[-1]
    gathered = gather_four(upstream)
    expert_parts = gathered_parts
    second_weights, first_weights = gathered_parts

    upstream, finish_second, expert_gain, router_grad = expert_backward(
        upstream.astype(F32),
        caches[1],
        gains[1, 1],
        routers[1],
        expert_parts[1],
        by_core,
        gathered,
        lambda x: x,
    )
    smalls = [None, expert_gain[None], router_grad]
    waiting = None

    expert_sum = None

    def keep(parts, operands, attention_gain):
        nonlocal waiting, expert_sum
        expert_sum, *parts = finish_second(*parts)
        expert_sum = sum_over_cores(expert_sum)
        waiting = operands
        smalls[0] = attention_gain[None]
        return parts

    upstream = attention_backward(
        upstream,
        attention_caches[1],
        gains[1, 0],
        second_weights,
        geometry,
        lambda x: x,
        lambda x: x,
        keep,
    )
    gathered = gather_four(upstream.astype(BF16))
    upstream, finish_first, expert_gain, router_grad = expert_backward(
        upstream,
        caches[0],
        gains[0, 1],
        routers[0],
        expert_parts[0],
        by_core,
        gathered,
        lambda x: x,
    )
    first_sum = None
    last = None

    def finish_sum(out_grads):
        nonlocal first_sum
        first_sum, *out_grads = finish_first(*out_grads)
        return out_grads

    def start_sum(far_pair):
        nonlocal first_sum, expert_sum
        first_sum, expert_sum, far_pair = tied(first_sum, expert_sum, far_pair)
        first_sum = sum_over_cores(first_sum)
        return far_pair

    def keep_last(parts, operands, attention_gain):
        nonlocal last, small
        small = jnp.concatenate([attention_gain[None], expert_gain[None], router_grad] + smalls)
        small = small[:, :HALF] + over_col(small[:, HALF:])
        packed = attention_grads(*operands, by_steps[0])
        small = small + none_of(packed[0])
        after_first = by_steps[1] + none_of(packed[0]).astype(BF16)
        second_packed = attention_grads(*waiting, after_first)
        small = small + over_row(small) + none_of(second_packed[0])
        last = [sum_pairs(x)[0] for x in (packed, second_packed)]
        small = small + over_dp(small, lambda i: i ^ 1)
        return parts

    small = None
    upstream = attention_backward(
        upstream,
        attention_caches[0],
        gains[0, 0],
        first_weights,
        geometry,
        finish_sum,
        start_sum,
        keep_last,
    )
    expert_sum = expert_sum + none_of(last[1])
    last_hidden = last_hidden + none_of(last[1]).astype(BF16)
    last = sum_round(last, (shift_x, shift_z))
    small = small + none_of(last[0]) + none_of(last[1])
    along_x, along_z = data_index // 8, data_index // 2 % 4
    small = sum_in_order(sum_in_order(small, shift_x, along_x), shift_z, along_z)
    small = small.reshape(LAYERS, 2 + EXPERTS, HALF)
    def columns(values):
        return [
            jnp.concatenate(
                [
                    values[:, k * 2 * D : (k + 1) * 2 * D],
                    values[:, (4 + k) * D : (5 + k) * D],
                ],
                axis=1,
            ).astype(BF16)
            for k in range(2)
        ]

    second, _ = place(*columns(expert_sum), [], column)
    sends = send_four(last_down(last_hidden, gathered_parts[1]))
    *last, second[0], far_send = tied(*last, second[0], sends[3])
    last = sum_round(last, (shift_z, shift_x))
    stream = stream + total((*sends[:3], far_send))
    block_output = from_quarter(stream.astype(BF16), column)
    half = QKV + HALF
    first, ((qkv_second, out_second), (qkv_first, out_first)) = place(
        *columns(first_sum), [(x[:, :half], x[:, half:]) for x in last[::-1]], column
    )
    grad_tokens = from_quarter(upstream.astype(BF16), column)

    grad_gains = small[:, :2]
    grad_router = small[:, 2:].transpose(0, 2, 1)

    qkv_grad = jnp.stack([qkv_first, qkv_second])
    out_grad = jnp.stack([out_first, out_second])
    grad_gate, grad_up, grad_down = [jnp.stack([x, y]) for x, y in zip(first, second)]
    width = Q_HEADS * HEAD
    return (
        block_output,
        grad_tokens,
        grad_gains,
        qkv_grad[:, :, :width],
        qkv_grad[:, :, width : width + HEAD],
        qkv_grad[:, :, width + HEAD :],
        out_grad,
        grad_router,
        grad_gate,
        grad_up,
        grad_down,
    )


def solution(mesh):
    in_specs = (
        P(("dp", "row"), "col"),
        P(("dp", "row"), "col"),
        P(None, None, "col"),
        P(None, "col", "row"),
        P(None, "col", "row"),
        P(None, "col", "row"),
        P(None, "row", "col"),
        P(None, "col", None),
        P(None, None, "col", "row"),
        P(None, None, "col", "row"),
        P(None, None, "row", "col"),
        P(None, "dp", None),
        P(),
        P(),
    )
    out_specs = (
        P(("dp", "row"), "col"),
        P(("dp", "row"), "col"),
        P(None, None, "col"),
        P(None, ("col", "dp"), "row"),
        P(None, ("col", "dp"), "row"),
        P(None, ("col", "dp"), "row"),
        P(None, ("row", "dp"), "col"),
        P(None, "col", None),
        P(None, None, ("col", "dp"), "row"),
        P(None, None, ("col", "dp"), "row"),
        P(None, None, ("row", "dp"), "col"),
    )
    return jax.shard_map(shards, mesh=mesh, in_specs=in_specs, out_specs=out_specs, check_vma=False)
```
